32 devices in a mesh: row: 8 (over y, x, core), col: 4 (over z).
Axes of the slice: x: 2, y: 2, z: 4, core: 2. Of those that a mesh axis runs over, the one named last changes fastest.
Arguments:
- adj_tiles: bfloat16 [8, 4, 448, 128, 128], P('row', 'col'), may hold values from -0.046875 to 0.046875
- tile_counts: int32 [8, 4, 16], P('row', 'col'), may hold values from 5 to 32, as said below
- tile_cols: int32 [8, 4, 448], P('row', 'col'), may hold values from 0 to 31, as said below
- features: bfloat16 [16384, 256], P(('col', 'row')), may hold values from -6 to 6
- weight: bfloat16 [256, 256], replicated, may hold values from -0.375 to 0.375
- upstream: bfloat16 [16384, 256], P(('row', 'col')), may hold values from -6 to 6
Outputs:
- hidden: bfloat16 [16384, 256], P(('row', 'col'))
- weight_grad: float32 [256, 256], replicated
- feature_grad: bfloat16 [16384, 256], P(('col', 'row'))
The draws below stay inside these ranges and needn't reach their ends.
Inputs may be any that keep to these rules, and one draw needn't show every extreme that they name: `tile_counts`: entry (r, c, t) counts the nonzero tiles of row tile t in block (r, c); the counts of one block sum to 448 or less, and to exactly 448 in at least one block. `tile_cols`: live slots are filled in order of row tile; the entries of slots past a block's total count are not used.
All inputs are finite; a program needn't handle non-finite values.
Results may differ from the reference program's by a relative error of at most 0.023.
Values may be sent and summed in bfloat16 or wider, within the bound.
No kernel may reach another device: no remote copies, remote signals or barrier semaphores. Data moves between devices by JAX's collectives and lax.ppermute only.
A program may use at most 128 MiB of HBM per device.

```python
import jax
import jax.numpy as jnp
from jax import lax

F = 256
TILE = 128
RT = 16
FILL_ROW = 28
CT = 32
SLOTS = 448
NODES = 16384
N_ROW = 8
N_COL = 4


def pattern(key):
    base_key = jax.random.fold_in(key, 7013)
    key_full, key_high, key_drop, key_shift, key_start, key_stride = jax.random.split(base_key, 6)
    devices_all = N_ROW * N_COL
    spread = min(4, CT - FILL_ROW, FILL_ROW)
    lowest = max(1, FILL_ROW // 3)
    full_dev = jax.random.randint(key_full, (), 0, devices_all)
    highs = jax.random.randint(key_high, (devices_all, 1), lowest, FILL_ROW + 1)
    drops = jax.random.randint(key_drop, (devices_all, RT), 0, 1 << 20) % (highs // 2 + 1)
    drawn = highs - drops
    half_rows = RT // 2
    shifts = jax.random.randint(key_shift, (half_rows,), -spread, spread + 1)
    shifts = shifts.at[0].set(spread)
    fulls = FILL_ROW + jnp.concatenate([shifts, -shifts])
    is_full = (jnp.arange(devices_all, dtype=jnp.int32) == full_dev)[:, None]
    counts = jnp.where(is_full, fulls[None, :], drawn).astype(jnp.int32)
    ending = jnp.cumsum(counts, axis=1).astype(jnp.int32)
    starts = ending - counts
    position = jnp.arange(SLOTS, dtype=jnp.int32)
    row_of = jnp.sum((position[None, :, None] >= ending[:, None, :]).astype(jnp.int32), axis=2)
    clipped = jnp.minimum(row_of, RT - 1)
    within = position[None, :] - jnp.take_along_axis(starts, clipped, axis=1)
    offsets = jax.random.randint(key_start, (devices_all, RT), 0, CT)
    strides = 2 * jax.random.randint(key_stride, (devices_all, RT), 0, max(1, CT // 2)) + 1
    slot_off = jnp.take_along_axis(offsets, clipped, axis=1)
    slot_stride = jnp.take_along_axis(strides, clipped, axis=1)
    live = row_of < RT
    col_ids = jnp.where(live, (slot_off + within * slot_stride) % CT, position[None, :] % CT)
    return (counts.reshape(N_ROW, N_COL, RT), col_ids.astype(jnp.int32).reshape(N_ROW, N_COL, SLOTS))


def draw_tile_counts(key, part):
    counts, col_ids = pattern(key)
    return counts


def draw_tile_cols(key, part):
    counts, col_ids = pattern(key)
    return col_ids


def block_scale(stream_key, shape, cuts, smallest, high):
    loudness, own = 1.0, jax.random.fold_in(stream_key, 6)
    for dim, blocks in cuts:
        steps = jnp.exp(jax.random.uniform(jax.random.fold_in(own, dim), (blocks,), jnp.float32, smallest / len(cuts), high / len(cuts)))
        loudness = loudness * jnp.repeat(steps, shape[dim] // blocks).reshape([-1 if axis == dim else 1 for axis in range(len(shape))])
    return loudness


def centred(own_key, shape, scale, bound, shards=(), kind=jnp.bfloat16):
    factor_of = block_scale(own_key, shape, shards, -0.22, 0.18) if shards else 1.0
    array = jax.random.normal(own_key, shape, jnp.float32) * scale * factor_of
    return jnp.minimum(jnp.maximum(array, -bound), bound).astype(kind)


def setup_inputs(seed: int = 0) -> dict:
    seeds = jax.random.split(jax.random.key(seed), 7)
    return {
        "adj_tiles": centred(seeds[0], (N_ROW, N_COL, SLOTS, TILE, TILE), (FILL_ROW * N_COL * TILE) ** -0.5, 0.046875, ((0, 8), (1, 4))),
        "tile_counts": draw_tile_counts(jax.random.fold_in(seeds[6], 71), 0),
        "tile_cols": draw_tile_cols(jax.random.fold_in(seeds[6], 71), 0),
        "features": centred(seeds[3], (NODES, F), 1.0, 6.0, ((0, 32),)),
        "weight": centred(seeds[4], (F, F), F ** -0.5, 0.375),
        "upstream": centred(seeds[5], (NODES, F), 1.0, 6.0, ((0, 32),)),
    }


def membership(counts, slots):
    ending = jnp.cumsum(counts).astype(jnp.int32)
    starts = ending - counts
    position = jnp.arange(slots, dtype=jnp.int32)[:, None]
    return ((position >= starts[None, :]) & (position < ending[None, :])).astype(jnp.float32)

def forward_block(adj_block, col_ids, counts, col_block):
    rows_t = counts.shape[0]
    group_size = adj_block.shape[0] // rows_t
    col_tiles = col_block.shape[0] // TILE
    member = membership(counts, adj_block.shape[0])
    block_tiles = col_block.reshape(col_tiles, TILE, F)

    def advance(total, pieces):
        tile_g, col_g, mem_g = pieces
        picked = block_tiles[col_g].astype(jnp.float32)
        product = jnp.einsum('sij,sjf->sif', tile_g.astype(jnp.float32), picked, precision=lax.Precision.HIGHEST)
        return (total + jnp.einsum('st,sif->tif', mem_g, product, precision=lax.Precision.HIGHEST), None)
    stacked = (adj_block.reshape(rows_t, group_size, TILE, TILE), col_ids.reshape(rows_t, group_size), member.reshape(rows_t, group_size, rows_t))
    total, unused = lax.scan(advance, jnp.zeros((rows_t, TILE, F), jnp.float32), stacked)
    return total.reshape(rows_t * TILE, F)

def backward_block(adj_block, col_ids, counts, row_grad, col_tiles):
    rows_t = counts.shape[0]
    group_size = adj_block.shape[0] // rows_t
    member = membership(counts, adj_block.shape[0])
    grad_tiles = row_grad.reshape(rows_t, TILE, F).astype(jnp.float32)
    col_range = jnp.arange(col_tiles, dtype=jnp.int32)

    def advance(total, pieces):
        tile_g, col_g, mem_g = pieces
        chosen = jnp.einsum('st,tif->sif', mem_g, grad_tiles, precision=lax.Precision.HIGHEST)
        product = jnp.einsum('sij,sif->sjf', tile_g.astype(jnp.float32), chosen, precision=lax.Precision.HIGHEST)
        onehot = (col_g[:, None] == col_range[None, :]).astype(jnp.float32)
        return (total + jnp.einsum('sc,sjf->cjf', onehot, product, precision=lax.Precision.HIGHEST), None)
    stacked = (adj_block.reshape(rows_t, group_size, TILE, TILE), col_ids.reshape(rows_t, group_size), member.reshape(rows_t, group_size, rows_t))
    total, unused = lax.scan(advance, jnp.zeros((col_tiles, TILE, F), jnp.float32), stacked)
    return total.reshape(col_tiles * TILE, F)

def reference(adj_tiles, tile_counts, tile_cols, features, weight, upstream):
    feat_blocks = features.reshape(N_COL, CT * TILE, F)

    def row_pass(row_id):

        def col_step(total, col_id):
            part = forward_block(adj_tiles[row_id, col_id], tile_cols[row_id, col_id], tile_counts[row_id, col_id], feat_blocks[col_id])
            return (total + part, None)
        total, unused = lax.scan(col_step, jnp.zeros((RT * TILE, F), jnp.float32), jnp.arange(N_COL, dtype=jnp.int32))
        return total
    partial_value = lax.map(row_pass, jnp.arange(N_ROW, dtype=jnp.int32))
    aggregated = partial_value.reshape(NODES, F).astype(jnp.bfloat16)
    pre = jnp.dot(aggregated, weight, preferred_element_type=jnp.float32)
    hidden = jax.nn.silu(pre).astype(jnp.bfloat16)
    sigmoid_pre = jax.nn.sigmoid(pre)
    pre_grad = (upstream.astype(jnp.float32) * sigmoid_pre * (1.0 + pre * (1.0 - sigmoid_pre))).astype(jnp.bfloat16)
    weight_grad = jnp.dot(aggregated.T, pre_grad, preferred_element_type=jnp.float32) / jnp.sqrt(jnp.float32(NODES))
    agg_grad = jnp.dot(pre_grad, weight.T, preferred_element_type=jnp.float32).astype(jnp.bfloat16)
    grad_blocks = agg_grad.reshape(N_ROW, RT * TILE, F)

    def col_pass(col_id):

        def row_step(total, row_id):
            part = backward_block(adj_tiles[row_id, col_id], tile_cols[row_id, col_id], tile_counts[row_id, col_id], grad_blocks[row_id], CT)
            return (total + part, None)
        total, unused = lax.scan(row_step, jnp.zeros((CT * TILE, F), jnp.float32), jnp.arange(N_ROW, dtype=jnp.int32))
        return total
    columns = lax.map(col_pass, jnp.arange(N_COL, dtype=jnp.int32))
    feature_grad = columns.reshape(NODES, F).astype(jnp.bfloat16)
    return (hidden, weight_grad, feature_grad)
```

```python
import functools
import math

import jax
import jax.numpy as jnp
from jax import lax
from jax.experimental import pallas as pl
from jax.experimental.pallas import tpu as pltpu
from jax.sharding import PartitionSpec as P

VMEM_LIMIT = 40 * 1024 * 1024


def dense_kernel(counts, cols, adj_ref, out_ref, held, total, sems, *, window, slots):
    row_tiles = pl.num_programs(0)
    t = pl.program_id(0)
    tile = adj_ref.shape[1]
    width = out_ref.shape[1]

    def begin(index):
        return lax.fori_loop(0, index, lambda i, s: s + counts[i], jnp.int32(0))

    def fetch(index, slot):
        base = jnp.minimum(begin(index), slots - window)
        return pltpu.make_async_copy(adj_ref.at[pl.ds(base, window)], held.at[slot], sems.at[slot])

    slot = lax.rem(t, 2)

    @pl.when(t == 0)
    def _():
        fetch(t, slot).start()

    @pl.when(t + 1 < row_tiles)
    def _():
        fetch(t + 1, 1 - slot).start()

    start = begin(t)
    shift = start - jnp.minimum(start, slots - window)
    count = counts[t]
    out_ref[...] = jnp.zeros_like(out_ref)
    fetch(t, slot).wait()

    def place(j):
        c = cols[start + j]
        out_ref[:, pl.ds(pl.multiple_of(c * tile, tile), tile)] = held[slot, shift + j]
        return lax.shift_left(jnp.int32(1), c)

    def four(i, state):
        seen, twice = state
        for u in range(4):
            bit = place(4 * i + u)
            twice = twice | (seen & bit)
            seen = seen | bit
        return seen, twice

    def one(j, state):
        seen, twice = state
        bit = place(j)
        return seen | bit, twice | (seen & bit)

    groups = lax.div(count, 4)
    state = lax.fori_loop(0, groups, four, (jnp.int32(0), jnp.int32(0)))
    seen, twice = lax.fori_loop(4 * groups, count, one, state)
    repeated = (twice != 0) if width // tile <= 32 else (count > 0)

    @pl.when(repeated)
    def _():
        total[...] = jnp.zeros_like(total)

        def add(j, carry):
            where = pl.ds(pl.multiple_of(cols[start + j] * tile, tile), tile)
            total[:, where] += held[slot, shift + j].astype(jnp.float32)
            return carry

        lax.fori_loop(0, count, add, 0)
        out_ref[...] = total[...].astype(out_ref.dtype)


def dense_block(adj, counts, cols, col_tiles):
    slots, tile, _ = adj.shape
    row_tiles = counts.shape[0]
    window = min(col_tiles, slots)
    width = col_tiles * tile
    return pl.pallas_call(
        functools.partial(dense_kernel, window=window, slots=slots),
        out_shape=jax.ShapeDtypeStruct((row_tiles * tile, width), adj.dtype),
        grid_spec=pltpu.PrefetchScalarGridSpec(
            num_scalar_prefetch=2,
            grid=(row_tiles,),
            in_specs=[pl.BlockSpec(memory_space=pl.ANY)],
            out_specs=pl.BlockSpec((tile, width), lambda t, *_: (t, 0)),
            scratch_shapes=[
                pltpu.VMEM((2, window, tile, tile), adj.dtype),
                pltpu.VMEM((tile, width), jnp.float32),
                pltpu.SemaphoreType.DMA((2,)),
            ],
        ),
        compiler_params=pltpu.CompilerParams(vmem_limit_bytes=VMEM_LIMIT),
        cost_estimate=pl.CostEstimate(
            flops=0, bytes_accessed=adj.size * 2 + row_tiles * tile * width * 2, transcendentals=0
        ),
        name="dense_block",
    )(counts, cols, adj)


def forward_kernel(where, a_ref, *refs, first, total):
    shards, out_ref = refs[:-1], refs[-1]
    depth = shards[0].shape[0]
    value = None
    for k, shard in enumerate(shards):
        cols = pl.ds(pl.multiple_of(where[total + k] * depth, depth), depth)
        part = jnp.dot(a_ref[:, cols], shard[...], preferred_element_type=jnp.float32)
        value = part if value is None else value + part
    out_ref[0] = value.astype(out_ref.dtype)


def forward(where, dense, shards, first, last, total, rows, kind):
    width = shards[0].shape[1]
    step = min(rows, 256)
    per = rows // step
    count = last - first
    return pl.pallas_call(
        functools.partial(forward_kernel, first=first, total=total),
        out_shape=jax.ShapeDtypeStruct((count, rows, width), kind),
        grid_spec=pltpu.PrefetchScalarGridSpec(
            num_scalar_prefetch=1,
            grid=(count, per),
            in_specs=[
                pl.BlockSpec((step, dense.shape[1]), lambda i, m, where: (where[first + i] * per + m, 0))
            ]
            + [pl.BlockSpec(s.shape, lambda i, m, where: (0, 0)) for s in shards],
            out_specs=pl.BlockSpec((1, step, width), lambda i, m, where: (i, m, 0)),
        ),
        compiler_params=pltpu.CompilerParams(vmem_limit_bytes=VMEM_LIMIT),
        cost_estimate=pl.CostEstimate(
            flops=2 * count * rows * dense.shape[1] * width,
            bytes_accessed=count * rows * dense.shape[1] * 2,
            transcendentals=0,
        ),
        name="forward_rows",
    )(where, dense, *shards)


def middle_kernel(came_ref, own_ref, weight_ref, up_ref, hidden_ref, grad_ref, wgrad_ref, *, scale):
    agg = (came_ref[...].astype(jnp.float32) + own_ref[...].astype(jnp.float32)).astype(jnp.bfloat16)
    weight = weight_ref[...]
    pre = jnp.dot(agg, weight, preferred_element_type=jnp.float32)
    sig = jax.nn.sigmoid(pre)
    hidden_ref[...] = (pre * sig).astype(jnp.bfloat16)
    pre_grad = (up_ref[...].astype(jnp.float32) * sig * (1.0 + pre * (1.0 - sig))).astype(jnp.bfloat16)
    grad_ref[...] = lax.dot_general(
        weight, pre_grad, (((1,), (1,)), ((), ())), preferred_element_type=jnp.float32
    ).astype(jnp.bfloat16)
    wgrad_ref[...] = scale * lax.dot_general(
        agg, pre_grad, (((0,), (0,)), ((), ())), preferred_element_type=jnp.float32
    )


def middle(came, own, weight, upstream, scale):
    rows, width = upstream.shape
    return pl.pallas_call(
        functools.partial(middle_kernel, scale=scale),
        out_shape=(
            jax.ShapeDtypeStruct((rows, width), jnp.bfloat16),
            jax.ShapeDtypeStruct((width, rows), jnp.bfloat16),
            jax.ShapeDtypeStruct((width, width), jnp.float32),
        ),
        compiler_params=pltpu.CompilerParams(vmem_limit_bytes=VMEM_LIMIT),
        cost_estimate=pl.CostEstimate(
            flops=6 * rows * width * width, bytes_accessed=10 * rows * width, transcendentals=rows * width
        ),
        name="middle",
    )(came, own, weight, upstream)


def backward_kernel(where, *refs, count, has_sum):
    blocks, pieces = refs[:count], refs[count : 2 * count]
    out_ref = refs[-1]
    value = refs[2 * count][0] if has_sum else None
    for a_ref, piece in zip(blocks, pieces):
        part = jnp.dot(piece[...], a_ref[...], preferred_element_type=jnp.float32)
        value = part if value is None else value + part
    out_ref[0] = value.astype(out_ref.dtype)


def backward(where, dense, pieces, row_at, col_at, columns, depth, before, before_at, kind):
    count = len(pieces)
    width, rows = pieces[0].shape

    def block(i):
        return pl.BlockSpec((rows, depth), lambda j, where: (where[row_at + i], where[col_at + j]))

    in_specs = [block(i) for i in range(count)]
    in_specs += [pl.BlockSpec((width, rows), lambda j, where: (0, 0)) for _ in range(count)]
    operands = [dense] * count + list(pieces)
    if before is not None:
        in_specs.append(pl.BlockSpec((1, width, depth), lambda j, where: (before_at + j, 0, 0)))
        operands.append(before)
    return pl.pallas_call(
        functools.partial(backward_kernel, count=count, has_sum=before is not None),
        out_shape=jax.ShapeDtypeStruct((columns, width, depth), kind),
        grid_spec=pltpu.PrefetchScalarGridSpec(
            num_scalar_prefetch=1,
            grid=(columns,),
            in_specs=in_specs,
            out_specs=pl.BlockSpec((1, width, depth), lambda j, where: (j, 0, 0)),
        ),
        compiler_params=pltpu.CompilerParams(vmem_limit_bytes=VMEM_LIMIT),
        cost_estimate=pl.CostEstimate(
            flops=2 * count * rows * width * columns * depth,
            bytes_accessed=count * rows * columns * depth * 2,
            transcendentals=0,
        ),
        name="backward_cols",
    )(where, *operands)


def finish_kernel(*refs):
    parts, out_ref = refs[:-1], refs[-1]
    value = parts[0][...].astype(jnp.float32)
    for part in parts[1:]:
        value = value + part[...].astype(jnp.float32)
    out_ref[...] = value.T.astype(out_ref.dtype)


def finish(parts):
    width, rows = parts[0].shape
    return pl.pallas_call(
        finish_kernel,
        out_shape=jax.ShapeDtypeStruct((rows, width), jnp.bfloat16),
        compiler_params=pltpu.CompilerParams(vmem_limit_bytes=VMEM_LIMIT),
        cost_estimate=pl.CostEstimate(
            flops=len(parts) * rows * width, bytes_accessed=4 * len(parts) * rows * width, transcendentals=0
        ),
        name="finish",
    )(*parts)


def swap(value, axis, size, bit):
    return lax.ppermute(value, axis, [(i, i ^ bit) for i in range(size)])


def turn(value, order):
    count = len(order)
    return lax.ppermute(value, "col", [(order[p], order[(p + 1) % count]) for p in range(count)])


def gather_rows(features, size, core):
    across_x = swap(features, "row", size, 2)
    across_y = swap(features, "row", size, 4)
    beside = swap(features, "row", size, 1)
    onward = jnp.where(core == 0, across_x, across_y)
    corner = lax.ppermute(onward, "row", [(i, i ^ (4 if i % 2 == 0 else 2)) for i in range(size)])
    beside_x = swap(across_x, "row", size, 1)
    beside_y = swap(across_y, "row", size, 1)
    beside_corner = swap(corner, "row", size, 1)
    return [features, beside, across_x, beside_x, across_y, beside_y, corner, beside_corner]


def sum_all(value, n_row, n_col):
    if n_row & (n_row - 1) or n_col & (n_col - 1) or value.shape[0] % (8 * n_row):
        return lax.psum(value, ("row", "col"))
    row, col_bits, bit = lax.axis_index("row"), 1, 1
    while bit < n_row:
        half = value.shape[0] // 2
        high = ((row // bit) % 2).astype(jnp.int32)
        kept = lax.dynamic_slice_in_dim(value, high * half, half, 0)
        sent = lax.dynamic_slice_in_dim(value, (1 - high) * half, half, 0)
        value = kept + swap(sent, "row", n_row, bit)
        bit *= 2
    while col_bits < n_col:
        value = value + swap(value, "col", n_col, col_bits)
        col_bits *= 2
    while bit > 1:
        bit //= 2
        high = ((row // bit) % 2) == 1
        other = swap(value, "row", n_row, bit)
        value = jnp.concatenate([jnp.where(high, other, value), jnp.where(high, value, other)], axis=0)
    return value


def shards(adj_tiles, tile_counts, tile_cols, features, weight, upstream):
    n_row, n_col = lax.axis_size("row"), lax.axis_size("col")
    row, col = lax.axis_index("row"), lax.axis_index("col")
    adj, counts, cols = adj_tiles[0, 0], tile_counts[0, 0], tile_cols[0, 0]
    tile = adj.shape[1]
    rows, depth = upstream.shape[0], features.shape[0]
    col_tiles = depth * n_row // tile
    scale = 1.0 / math.sqrt(rows * n_row * n_col)
    paired = n_row == 8

    order = [i for i in range(0, n_col, 2)] + [i for i in range(n_col)[::-1] if i % 2]
    ring = jnp.array(order, jnp.int32)
    place = jnp.argmax(ring == col).astype(jnp.int32)
    steps = jnp.arange(n_col, dtype=jnp.int32)
    by_owner = ring[(place + n_col - 1 - steps) % n_col]
    by_arrival = ring[(place + n_col - steps) % n_col]
    core = row % 2
    if paired:
        held = row ^ jnp.arange(n_row, dtype=jnp.int32)
        even, odd = jnp.array([0, 6, 2, 4], jnp.int32), jnp.array([0, 6, 4, 2], jnp.int32)
        mine = jnp.where(core == 0, even, odd)
        others = jnp.where(core == 0, odd, even)
        targets = jnp.concatenate([(row ^ 1) ^ others, row ^ mine])
    else:
        held = jnp.arange(n_row, dtype=jnp.int32)
        targets = held
    where = jnp.concatenate([by_owner, by_arrival, held, targets]).astype(jnp.int32)
    at_arrival, at_held, at_targets = n_col, 2 * n_col, 2 * n_col + n_row

    if paired:
        parts = gather_rows(features, n_row, core)
    else:
        block = lax.all_gather(features, "row", axis=0, tiled=True)
        parts = [block[i * depth : (i + 1) * depth] for i in range(n_row)]
    dense = dense_block(adj, counts, cols, col_tiles)

    moving = forward(where, dense, parts, 0, 1, at_held, rows, jnp.bfloat16)[0]
    rest = forward(where, dense, parts, 1, n_col, at_held, rows, jnp.float32)
    for step in range(n_col - 1):
        moving = turn(moving, order)
        if step < n_col - 2:
            moving = (moving.astype(jnp.float32) + rest[step]).astype(jnp.bfloat16)
    hidden, piece, weight_part = middle(moving, rest[n_col - 2], weight, upstream, scale)

    pieces = [piece]
    for step in range(n_col - 1):
        pieces.append(turn(pieces[-1], order))
    weight_grad = sum_all(weight_part, n_row, n_col)

    early = backward(
        where, dense, pieces[:-1], at_arrival, at_targets, n_row, depth, None, 0, jnp.float32
    )
    last = functools.partial(backward, where, dense, pieces[-1:], at_arrival + n_col - 1)
    if not paired:
        grads = last(at_targets, n_row, depth, early, 0, jnp.bfloat16)
        return hidden, weight_grad, finish([lax.psum_scatter(grads, "row", scatter_dimension=0, tiled=True)[0]])

    half = n_row // 2
    sent = last(at_targets, half, depth, early, 0, jnp.bfloat16)
    kept = last(at_targets + half, half, depth, early, half, jnp.float32)
    came = swap(sent, "row", n_row, 1)
    summed = kept + came.astype(jnp.float32)
    near = [(i, i ^ (2 if i % 2 == 0 else 4)) for i in range(n_row)]
    far = [(i, i ^ (4 if i % 2 == 0 else 2)) for i in range(n_row)]
    corner = lax.ppermute(summed[1].astype(jnp.bfloat16), "row", near)
    first = lax.ppermute(summed[2].astype(jnp.bfloat16), "row", near)
    second = lax.ppermute((summed[3] + corner.astype(jnp.float32)).astype(jnp.bfloat16), "row", far)
    return hidden, weight_grad, finish([summed[0], first, second])


def solution(mesh):
    placed = (
        P("row", "col", None, None, None),
        P("row", "col", None),
        P("row", "col", None),
        P(("col", "row"), None),
        P(),
        P(("row", "col"), None),
    )
    return jax.shard_map(
        shards,
        mesh=mesh,
        in_specs=placed,
        out_specs=(P(("row", "col"), None), P(), P(("col", "row"), None)),
        check_vma=False,
    )
```

```python
import functools
import math

import jax
import jax.numpy as jnp
from jax import lax
from jax.experimental import pallas as pl
from jax.experimental.pallas import tpu as pltpu
from jax.sharding import PartitionSpec as P

MIB = 1024 * 1024
SCALARS = pl.BlockSpec(memory_space=pltpu.SMEM)
WHOLE = pl.BlockSpec(memory_space=pltpu.VMEM)


def params(mib):
    return pltpu.CompilerParams(vmem_limit_bytes=mib * MIB)


def cost(flops, moved, exps=0):
    return pl.CostEstimate(flops=flops, bytes_accessed=moved, transcendentals=exps)


def near(value):
    return pltpu.with_memory_space_constraint(value, pltpu.VMEM)


def dense_kernel(where, counts, cols, adj_ref, out_ref, held, total, sems, *, at, window):
    tile = adj_ref.shape[1]
    slots = adj_ref.shape[0]
    per = out_ref.shape[0] // tile
    width = out_ref.shape[1]
    first = where[at] * per

    starts = [lax.fori_loop(0, first, lambda i, s: s + counts[i], jnp.int32(0))]
    for u in range(per - 1):
        starts.append(starts[-1] + counts[first + u])
    bases = [jnp.minimum(start, slots - window) for start in starts]
    fetches = [
        pltpu.make_async_copy(adj_ref.at[pl.ds(bases[u], window)], held.at[u], sems.at[u]) for u in range(per)
    ]
    for fetch in fetches:
        fetch.start()

    out_ref[...] = jnp.zeros_like(out_ref)
    for u in range(per):
        start, shift, count = starts[u], starts[u] - bases[u], counts[first + u]
        rows = pl.ds(u * tile, tile)
        fetches[u].wait()

        def place(j):
            c = cols[start + j]
            out_ref[rows, pl.ds(pl.multiple_of(c * tile, tile), tile)] = held[u, shift + j]
            return lax.shift_left(jnp.int32(1), c)

        def four(i, state):
            seen, twice = state
            for v in range(4):
                bit = place(4 * i + v)
                twice = twice | (seen & bit)
                seen = seen | bit
            return seen, twice

        def one(j, state):
            seen, twice = state
            bit = place(j)
            return seen | bit, twice | (seen & bit)

        groups = lax.div(count, 4)
        state = lax.fori_loop(0, groups, four, (jnp.int32(0), jnp.int32(0)))
        seen, twice = lax.fori_loop(4 * groups, count, one, state)
        repeated = (twice != 0) if width // tile <= 32 else (count > 0)

        @pl.when(repeated)
        def _():
            total[...] = jnp.zeros_like(total)

            def add(j, carry):
                here = pl.ds(pl.multiple_of(cols[start + j] * tile, tile), tile)
                total[:, here] += held[u, shift + j].astype(jnp.float32)
                return carry

            lax.fori_loop(0, count, add, 0)
            out_ref[rows, :] = total[...].astype(out_ref.dtype)


def dense_rows(where, at, counts, cols, adj, rows, col_tiles):
    slots, tile, _ = adj.shape
    window = min(col_tiles, slots)
    width = col_tiles * tile
    per = rows // tile
    return pl.pallas_call(
        functools.partial(dense_kernel, at=at, window=window),
        out_shape=pltpu.VMEM((rows, width), adj.dtype),
        in_specs=[SCALARS, SCALARS, SCALARS, pl.BlockSpec(memory_space=pltpu.HBM)],
        out_specs=WHOLE,
        scratch_shapes=[
            pltpu.VMEM((per, window, tile, tile), adj.dtype),
            pltpu.VMEM((tile, width), jnp.float32),
            pltpu.SemaphoreType.DMA((per,)),
        ],
        compiler_params=params(14),
        cost_estimate=cost(0, 5 * rows * width),
        name="dense_rows",
    )(where, counts, cols, pltpu.with_memory_space_constraint(adj, pltpu.HBM))


def forward_kernel(where, *refs, blocks, at):
    dense, shards, outs = refs[:blocks], refs[blocks:-blocks], refs[-blocks:]
    depth = shards[0].shape[0]
    for a_ref, out_ref in zip(dense, outs):
        value = None
        for k, shard in enumerate(shards):
            cols = pl.ds(pl.multiple_of(where[at + k] * depth, depth), depth)
            part = jnp.dot(a_ref[:, cols], shard[...], preferred_element_type=jnp.float32)
            value = part if value is None else value + part
        out_ref[...] = value.astype(out_ref.dtype)


def forward(where, at, dense, shards, kinds):
    rows, width = dense[0].shape[0], shards[0].shape[1]
    count = len(dense)
    return pl.pallas_call(
        functools.partial(forward_kernel, blocks=count, at=at),
        out_shape=[pltpu.VMEM((rows, width), kind) for kind in kinds],
        in_specs=[SCALARS] + [WHOLE] * (count + len(shards)),
        out_specs=[WHOLE] * count,
        compiler_params=params(10),
        cost_estimate=cost(2 * count * dense[0].size * width, count * dense[0].size * 2),
        name="forward_rows",
    )(where, *map(near, dense), *map(near, shards))


def middle_kernel(*refs, scale, came):
    parts = refs[: came + 1]
    weight_ref, up_ref, hidden_ref, grad_ref, wgrad_ref = refs[came + 1 :]
    agg = parts[0][...].astype(jnp.float32)
    for part in parts[1:]:
        agg = agg + part[...].astype(jnp.float32)
    agg = agg.astype(jnp.bfloat16)
    weight = weight_ref[...]
    pre = jnp.dot(agg, weight, preferred_element_type=jnp.float32)
    sig = jax.nn.sigmoid(pre)
    hidden_ref[...] = (pre * sig).astype(jnp.bfloat16)
    pre_grad = (up_ref[...].astype(jnp.float32) * sig * (1.0 + pre * (1.0 - sig))).astype(jnp.bfloat16)
    grad_ref[...] = lax.dot_general(
        weight, pre_grad, (((1,), (1,)), ((), ())), preferred_element_type=jnp.float32
    ).astype(jnp.bfloat16)
    wgrad_ref[...] = scale * lax.dot_general(
        agg, pre_grad, (((0,), (0,)), ((), ())), preferred_element_type=jnp.float32
    )


def middle(parts, weight, upstream, scale):
    rows, width = upstream.shape
    return pl.pallas_call(
        functools.partial(middle_kernel, scale=scale, came=len(parts) - 1),
        out_shape=(
            jax.ShapeDtypeStruct((rows, width), jnp.bfloat16),
            jax.ShapeDtypeStruct((width, rows), jnp.bfloat16),
            jax.ShapeDtypeStruct((width, width), jnp.float32),
        ),
        compiler_params=params(16),
        cost_estimate=cost(6 * rows * width * width, 10 * rows * width, rows * width),
        name="middle",
    )(*parts, weight, upstream)


def backward_kernel(where, *refs, count, at, before_at):
    dense, pieces = refs[:count], refs[count : 2 * count]
    out_ref = refs[-1]
    columns, _, depth = out_ref.shape

    def one(j, carry):
        cols = pl.ds(pl.multiple_of(where[at + j] * depth, depth), depth)
        value = None if before_at is None else refs[2 * count][before_at + j]
        for a_ref, piece in zip(dense, pieces):
            part = jnp.dot(piece[...], a_ref[:, cols], preferred_element_type=jnp.float32)
            value = part if value is None else value + part
        out_ref[j] = value.astype(out_ref.dtype)
        return carry

    lax.fori_loop(0, columns, one, 0)


def backward(where, at, dense, pieces, columns, depth, before, before_at, kind, after=()):
    count = len(pieces)
    width, rows = pieces[0].shape
    operands = [near(x) for x in [*dense, *pieces] + ([] if before is None else [before])]
    return pl.pallas_call(
        functools.partial(
            backward_kernel, count=count, at=at, before_at=None if before is None else before_at
        ),
        out_shape=pltpu.VMEM((columns, width, depth), kind),
        in_specs=[SCALARS] + [WHOLE] * len(operands) + [pl.BlockSpec(memory_space=pl.ANY)] * len(after),
        out_specs=WHOLE,
        compiler_params=params(10),
        cost_estimate=cost(
            2 * count * rows * width * columns * depth, count * rows * columns * depth * 2
        ),
        name="backward_cols",
    )(where, *operands, *after)


def finish_kernel(*refs):
    parts, out_ref = refs[:-1], refs[-1]
    value = parts[0][...].astype(jnp.float32)
    for part in parts[1:]:
        value = value + part[...].astype(jnp.float32)
    out_ref[...] = value.T.astype(out_ref.dtype)


def finish(parts):
    width, rows = parts[0].shape
    return pl.pallas_call(
        finish_kernel,
        out_shape=jax.ShapeDtypeStruct((rows, width), jnp.bfloat16),
        compiler_params=params(10),
        cost_estimate=cost(len(parts) * rows * width, 4 * len(parts) * rows * width),
        name="finish",
    )(*parts)


def pick_kernel(which, even_ref, odd_ref, *refs):
    out_ref = refs[-1]

    @pl.when(which[0] == 0)
    def _():
        out_ref[...] = even_ref[...]

    @pl.when(which[0] != 0)
    def _():
        out_ref[...] = odd_ref[...]


def pick(which, even, odd, before):
    return pl.pallas_call(
        pick_kernel,
        out_shape=pltpu.VMEM(even.shape, even.dtype),
        in_specs=[SCALARS, WHOLE, WHOLE] + [pl.BlockSpec(memory_space=pl.ANY)] * len(before),
        out_specs=WHOLE,
        compiler_params=params(10),
        cost_estimate=cost(0, 4 * even.size),
        name="pick",
    )(which.reshape(1), near(even), near(odd), *before)


def join_kernel(mine, *refs, count):
    out_ref = refs[-1]
    rows = refs[0].shape[0]
    for bit in range(count):
        out_ref[pl.ds(pl.multiple_of((mine[0] ^ bit) * rows, rows), rows), :] = refs[bit][...]


def join(mine, parts, before):
    count, (rows, width) = len(parts), parts[0].shape
    return pl.pallas_call(
        functools.partial(join_kernel, count=count),
        out_shape=jax.ShapeDtypeStruct((count * rows, width), parts[0].dtype),
        in_specs=[SCALARS] + [WHOLE] * count + [pl.BlockSpec(memory_space=pl.ANY)] * len(before),
        out_specs=WHOLE,
        compiler_params=params(10),
        cost_estimate=cost(0, 8 * count * rows * width),
        name="join",
    )(mine.reshape(1), *parts, *before)


def swap(value, axis, size, bit):
    return lax.ppermute(value, axis, [(i, i ^ bit) for i in range(size)])


def corner_first(size):
    return [(i, i ^ (2 if i % 2 == 0 else 4)) for i in range(size)]


def corner_second(size):
    return [(i, i ^ (4 if i % 2 == 0 else 2)) for i in range(size)]


def gather_rows(features, size, core, beside):
    across_x = swap(features, "row", size, 2)
    across_y = swap(features, "row", size, 4)
    sibling = swap(features, "row", size, 1)
    onward = pick(core, across_x, across_y, beside)
    corner = lax.ppermute(onward, "row", corner_second(size))
    sibling_x = swap(across_x, "row", size, 1)
    sibling_y = swap(across_y, "row", size, 1)
    sibling_corner = swap(corner, "row", size, 1)
    return [features, sibling, across_x, sibling_x, across_y, sibling_y, corner, sibling_corner]


def add(value, came):
    return (value.astype(jnp.float32) + came.astype(jnp.float32)).astype(jnp.bfloat16)


def choose(index, options):
    options = dict(options) if isinstance(options, dict) else dict(enumerate(options))
    last = max(options)
    value = options[last]
    for i, option in options.items():
        if option is not value and i != last:
            value = jnp.where(index == i, option, value)
    return value


def shards(adj_tiles, tile_counts, tile_cols, features, weight, upstream):
    n_row, n_col = lax.axis_size("row"), lax.axis_size("col")
    row, col = lax.axis_index("row"), lax.axis_index("col")
    adj, counts, cols = adj_tiles[0, 0], tile_counts[0, 0], tile_cols[0, 0]
    tile = adj.shape[1]
    rows, depth = upstream.shape[0], features.shape[0]
    col_tiles = depth * n_row // tile
    scale = 1.0 / math.sqrt(rows * n_row * n_col)
    paired = n_row == 8
    core = row % 2

    order = [sorted(range(n_col), key=lambda s: (-abs(s - z), s)) for z in range(n_col)]
    owners = choose(col, [jnp.array(line, jnp.int32) for line in order])
    if paired:
        held = row ^ jnp.arange(n_row, dtype=jnp.int32)
        even, odd = jnp.array([0, 6, 2, 4], jnp.int32), jnp.array([0, 6, 4, 2], jnp.int32)
        mine = jnp.where(core == 0, even, odd)
        others = jnp.where(core == 0, odd, even)
        targets = jnp.concatenate([(row ^ 1) ^ others, row ^ mine])
    else:
        held = jnp.arange(n_row, dtype=jnp.int32)
        targets = held
    where = jnp.concatenate([owners, held, targets]).astype(jnp.int32)
    at_held, at_targets = n_col, n_col + n_row

    dense = [dense_rows(where, i, counts, cols, adj, rows, col_tiles) for i in range(n_col)]
    if paired:
        parts = gather_rows(features, n_row, core, dense[: n_col // 2])
    else:
        block = lax.all_gather(features, "row", axis=0, tiled=True)
        parts = [block[i * depth : (i + 1) * depth] for i in range(n_row)]

    sums = list(forward(where, at_held, dense[:1], parts, [jnp.bfloat16]))
    sums += forward(where, at_held, dense[1:], parts, [jnp.bfloat16] * (n_col - 2) + [jnp.float32])
    up = down = None
    for k in range(1, n_col):
        rising = {z: sums[order[z].index(z + n_col - k)] for z in range(n_col - 1) if z <= k - 1}
        falling = {z: sums[order[z].index(z - n_col + k)] for z in range(1, n_col) if z >= n_col - k}
        upward, downward = choose(col, rising), choose(col, falling)
        if k > 1:
            upward, downward = add(upward, up), add(downward, down)
        up = lax.ppermute(upward, "col", [(z, z + 1) for z in rising])
        down = lax.ppermute(downward, "col", [(z, z - 1) for z in falling])
    hidden, piece, part = middle([sums[-1], up, down], weight, upstream, scale)

    beside = paired and n_col == 4 and part.shape[0] % 64 == 0
    chip = row // 2
    below, above = [piece], [piece]
    for k in range(1, n_col):
        up, down = below[-1], above[-1]
        if beside and k > 1:
            up, down, part = lax.optimization_barrier((up, down, part))
        below.append(lax.ppermute(up, "col", [(z, z + 1) for z in range(k - 1, n_col - 1)]))
        above.append(lax.ppermute(down, "col", [(z, z - 1) for z in range(1, n_col - k + 1)]))
        if beside and k == 1:
            half = part.shape[0] // 2
            sent = lax.dynamic_slice_in_dim(part, (1 - core) * half, half, 0)
            kept = lax.dynamic_slice_in_dim(part, core * half, half, 0)
            part = kept + swap(sent, "row", n_row, 1)
        if beside and k == 2:
            quarter = part.shape[0] // 4
            whole, part = part, lax.dynamic_slice_in_dim(part, chip * quarter, quarter, 0)
            for bit in (1, 2, 3):
                sent = lax.dynamic_slice_in_dim(whole, (chip ^ bit) * quarter, quarter, 0)
                part = part + swap(sent, "row", n_row, 2 * bit)
        if beside and k == 3:
            part = sum([swap(part, "col", n_col, bit) for bit in (1, 2, 3)], part)

    def came_from(i):
        came = {z: below[z - line[i]] if line[i] <= z else above[line[i] - z] for z, line in enumerate(order)}
        return choose(col, came)

    pieces = [came_from(i) for i in range(1, n_col)]
    early = backward(where, at_targets, dense[1:], pieces, n_row, depth, None, 0, jnp.float32)
    below, above, early = lax.optimization_barrier((below, above, early))
    late = [came_from(0)]
    last = functools.partial(backward, where)
    if not paired:
        grads = last(at_targets, dense[:1], late, n_row, depth, early, 0, jnp.bfloat16)
        weight_grad = lax.psum(part, ("row", "col"))
        return hidden, weight_grad, finish([lax.psum_scatter(grads, "row", scatter_dimension=0, tiled=True)[0]])

    half = n_row // 2
    sent = last(at_targets, dense[:1], late, half, depth, early, 0, jnp.bfloat16, [part] if beside else [])
    kept = last(at_targets + half, dense[:1], late, half, depth, early, half, jnp.float32)
    came = swap(sent, "row", n_row, 1)
    if beside:
        quarters = [part] + [swap(part, "row", n_row, 2 * bit) for bit in (1, 2, 3)]
        part = join(chip, quarters, [kept])
    summed = [add(kept[i], came[i]) for i in (1, 2)]
    corner = lax.ppermute(summed[0], "row", corner_first(n_row))
    first = lax.ppermute(summed[1], "row", corner_first(n_row))
    if beside:
        other = swap(part, "row", n_row, 1)
        weight_grad = join(core, [part, other], [])
    else:
        weight_grad = lax.psum(part, ("row", "col"))
    onward = (kept[3] + came[3].astype(jnp.float32) + corner.astype(jnp.float32)).astype(jnp.bfloat16)
    second = lax.ppermute(onward, "row", corner_second(n_row))
    return hidden, weight_grad, finish([kept[0], came[0], first, second])


def solution(mesh):
    placed = (
        P("row", "col", None, None, None),
        P("row", "col", None),
        P("row", "col", None),
        P(("col", "row"), None),
        P(),
        P(("row", "col"), None),
    )
    return jax.shard_map(
        shards,
        mesh=mesh,
        in_specs=placed,
        out_specs=(P(("row", "col"), None), P(), P(("col", "row"), None)),
        check_vma=False,
    )
```

```python
import functools
import math

import jax
import jax.numpy as jnp
from jax import lax
from jax.experimental import pallas as pl
from jax.experimental.pallas import tpu as pltpu
from jax.sharding import PartitionSpec as P


MIB = 1024 * 1024
SCALARS = pl.BlockSpec(memory_space=pltpu.SMEM)
WHOLE = pl.BlockSpec(memory_space=pltpu.VMEM)
UNREAD = pl.BlockSpec(memory_space=pl.ANY)


def params(mib):
    return pltpu.CompilerParams(vmem_limit_bytes=mib * MIB)


def cost(flops, moved, exps=0):
    return pl.CostEstimate(flops=flops, bytes_accessed=moved, transcendentals=exps)


def near(value):
    return pltpu.with_memory_space_constraint(value, pltpu.VMEM)


def dense_kernel(where, counts, cols, adj_ref, *refs, steps, window):
    outs, (held, total, sems) = refs[: len(steps)], refs[len(steps) :]
    slots, tile, _ = adj_ref.shape
    per = outs[0].shape[0] // tile
    width = outs[0].shape[1]

    plans = []
    for i, step in enumerate(steps):
        first = (where[1] ^ step) * per
        start = lax.fori_loop(0, first, lambda t, s: s + counts[t], jnp.int32(0))
        for u in range(per):
            count = counts[first + u]
            base = jnp.minimum(start, slots - window)
            fetch = pltpu.make_async_copy(
                adj_ref.at[pl.ds(base, window)], held.at[i * per + u], sems.at[i * per + u]
            )
            fetch.start()
            plans.append((start, start - base, count, fetch))
            start = start + count

    for i, out_ref in enumerate(outs):
        out_ref[...] = jnp.zeros_like(out_ref)
    for n, (start, shift, count, fetch) in enumerate(plans):
        out_ref = outs[n // per]
        rows = pl.ds((n % per) * tile, tile)
        fetch.wait()

        def place(j):
            c = cols[start + j]
            out_ref[rows, pl.ds(pl.multiple_of(c * tile, tile), tile)] = held[n, shift + j]
            return lax.shift_left(jnp.int32(1), c)

        def four(i, state):
            seen, twice = state
            for v in range(4):
                bit = place(4 * i + v)
                twice = twice | (seen & bit)
                seen = seen | bit
            return seen, twice

        def one(j, state):
            seen, twice = state
            bit = place(j)
            return seen | bit, twice | (seen & bit)

        groups = lax.div(count, 4)
        state = lax.fori_loop(0, groups, four, (jnp.int32(0), jnp.int32(0)))
        seen, twice = lax.fori_loop(4 * groups, count, one, state)
        repeated = (twice != 0) if width // tile <= 32 else (count > 0)

        @pl.when(repeated)
        def _():
            total[...] = jnp.zeros_like(total)

            def add(j, carry):
                here = pl.ds(pl.multiple_of(cols[start + j] * tile, tile), tile)
                total[:, here] += held[n, shift + j].astype(jnp.float32)
                return carry

            lax.fori_loop(0, count, add, 0)
            out_ref[rows, :] = total[...].astype(out_ref.dtype)


def dense_rows(where, steps, counts, cols, adj, rows, col_tiles):
    slots, tile, _ = adj.shape
    window = min(col_tiles, slots)
    width = col_tiles * tile
    tiles = rows // tile * len(steps)
    return pl.pallas_call(
        functools.partial(dense_kernel, steps=steps, window=window),
        out_shape=[pltpu.VMEM((rows, width), adj.dtype) for _ in steps],
        in_specs=[SCALARS, SCALARS, SCALARS, pl.BlockSpec(memory_space=pltpu.HBM)],
        out_specs=[WHOLE] * len(steps),
        scratch_shapes=[
            pltpu.VMEM((tiles, window, tile, tile), adj.dtype),
            pltpu.VMEM((tile, width), jnp.float32),
            pltpu.SemaphoreType.DMA((tiles,)),
        ],
        compiler_params=params(16),
        cost_estimate=cost(0, 5 * len(steps) * rows * width),
        name="dense_rows",
    )(where, counts, cols, pltpu.with_memory_space_constraint(adj, pltpu.HBM))


def forward_kernel(where, *refs, blocks, count, odd, before):
    dense, shards, sums = refs[:blocks], refs[blocks : blocks + count], refs[blocks + count :]
    depth = shards[0].shape[0]
    for i, a_ref in enumerate(dense):
        value = sums[i][...] if before else None
        for k, shard in enumerate(shards):
            cols = pl.ds(pl.multiple_of((where[0] ^ (2 * k + odd)) * depth, depth), depth)
            part = jnp.dot(a_ref[:, cols], shard[...], preferred_element_type=jnp.float32)
            value = part if value is None else value + part
        out_ref = sums[blocks + i if before else i]
        out_ref[...] = value.astype(out_ref.dtype)


def forward(where, dense, shards, odd, before, kind):
    rows, width = dense[0].shape[0], shards[0].shape[1]
    blocks, count = len(dense), len(shards)
    operands = [near(x) for x in [*dense, *shards, *before]]
    return pl.pallas_call(
        functools.partial(forward_kernel, blocks=blocks, count=count, odd=odd, before=bool(before)),
        out_shape=[pltpu.VMEM((rows, width), kind)] * blocks,
        in_specs=[SCALARS] + [WHOLE] * len(operands),
        out_specs=[WHOLE] * blocks,
        compiler_params=params(10),
        cost_estimate=cost(blocks * dense[0].size * width, blocks * dense[0].size),
        name="forward_rows",
    )(where, *operands)


def middle_kernel(*refs, scale, came):
    parts = refs[: came + 1]
    weight_ref, up_ref, hidden_ref, grad_ref, wgrad_ref = refs[came + 1 :]
    agg = parts[0][...].astype(jnp.float32)
    for part in parts[1:]:
        agg = agg + part[...].astype(jnp.float32)
    agg = agg.astype(jnp.bfloat16)
    weight = weight_ref[...]
    pre = jnp.dot(agg, weight, preferred_element_type=jnp.float32)
    sig = jax.nn.sigmoid(pre)
    hidden_ref[...] = (pre * sig).astype(jnp.bfloat16)
    pre_grad = (up_ref[...].astype(jnp.float32) * sig * (1.0 + pre * (1.0 - sig))).astype(jnp.bfloat16)
    grad_ref[...] = lax.dot_general(
        weight, pre_grad, (((1,), (1,)), ((), ())), preferred_element_type=jnp.float32
    ).astype(jnp.bfloat16)
    wgrad_ref[...] = scale * lax.dot_general(
        agg, pre_grad, (((0,), (0,)), ((), ())), preferred_element_type=jnp.float32
    )


def middle(parts, weight, upstream, scale):
    rows, width = upstream.shape
    return pl.pallas_call(
        functools.partial(middle_kernel, scale=scale, came=len(parts) - 1),
        out_shape=(
            jax.ShapeDtypeStruct((rows, width), jnp.bfloat16),
            jax.ShapeDtypeStruct((width, rows), jnp.bfloat16),
            jax.ShapeDtypeStruct((width, width), jnp.float32),
        ),
        compiler_params=params(16),
        cost_estimate=cost(6 * rows * width * width, 10 * rows * width, rows * width),
        name="middle",
    )(*parts, weight, upstream)


def backward_kernel(where, *refs, count, first, before, n_row):
    dense, pieces = refs[:count], refs[count : 2 * count]
    out_ref = refs[-1]
    columns, _, depth = out_ref.shape
    half = n_row // 2

    def one(j, carry):
        at = first + j
        step = 2 * lax.rem(at, half) + (at < half).astype(jnp.int32)
        cols = pl.ds(pl.multiple_of((where[0] ^ step) * depth, depth), depth)
        value = refs[2 * count][at] if before else None
        for a_ref, piece in zip(dense, pieces):
            part = jnp.dot(piece[...], a_ref[:, cols], preferred_element_type=jnp.float32)
            value = part if value is None else value + part
        out_ref[j] = value.astype(out_ref.dtype)
        return carry

    lax.fori_loop(0, columns, one, 0)


def backward(where, dense, pieces, first, columns, n_row, depth, before, kind, after=()):
    count = len(pieces)
    width, rows = pieces[0].shape
    operands = [near(x) for x in [*dense, *pieces] + ([] if before is None else [before])]
    return pl.pallas_call(
        functools.partial(
            backward_kernel, count=count, first=first, before=before is not None, n_row=n_row
        ),
        out_shape=pltpu.VMEM((columns, width, depth), kind),
        in_specs=[SCALARS] + [WHOLE] * len(operands) + [UNREAD] * len(after),
        out_specs=WHOLE,
        compiler_params=params(10),
        cost_estimate=cost(0, 0),
        name="backward_cols",
    )(where, *operands, *after)


def finish_kernel(*refs):
    parts, out_ref = refs[:-1], refs[-1]
    value = parts[0][0].astype(jnp.float32) + parts[1][0].astype(jnp.float32)
    for part in parts[2:]:
        value = value + part[...].astype(jnp.float32)
    out_ref[...] = value.T.astype(out_ref.dtype)


def finish(kept, came, parts):
    _, width, rows = kept.shape
    own = pl.BlockSpec((1, width, rows), lambda i: (0, 0, 0))
    part = pl.BlockSpec((width, rows), lambda i: (0, 0))
    return pl.pallas_call(
        finish_kernel,
        out_shape=jax.ShapeDtypeStruct((rows, width), jnp.bfloat16),
        grid=(1,),
        in_specs=[own, own] + [part] * len(parts),
        out_specs=pl.BlockSpec((rows, width), lambda i: (0, 0)),
        compiler_params=params(12),
        cost_estimate=cost(len(parts) * rows * width, 4 * len(parts) * rows * width),
        name="finish",
    )(kept, came, *parts)


def gate(values, after):
    count = len(values)
    return pl.pallas_call(
        lambda *refs: None,
        out_shape=[pltpu.VMEM(x.shape, x.dtype) for x in values],
        in_specs=[WHOLE] * count + [UNREAD] * len(after),
        out_specs=[WHOLE] * count,
        input_output_aliases={i: i for i in range(count)},
        compiler_params=params(4),
        cost_estimate=cost(0, 0),
        name="gate",
    )(*map(near, values), *after)


def split_kernel(where, *refs, by_core):
    outs = refs[1:] if by_core else refs[2:]
    rows = outs[0].shape[0]
    place = where[0] & 1 if by_core else lax.div(where[0], 2)
    for step, out_ref in enumerate(outs):
        at = pl.ds(pl.multiple_of((place ^ step) * rows, rows), rows)
        out_ref[...] = refs[0][at, :] if by_core else refs[0][at, :] + refs[1][at, :]


def split(where, values, count, by_core):
    rows, width = values[0].shape
    return pl.pallas_call(
        functools.partial(split_kernel, by_core=by_core),
        out_shape=[jax.ShapeDtypeStruct((rows // count, width), values[0].dtype)] * count,
        in_specs=[SCALARS] + [WHOLE] * len(values),
        compiler_params=params(10),
        cost_estimate=cost(0, 0),
        name="split",
    )(where, *values)


def join_kernel(where, *refs, by_core):
    parts, out_ref = refs[:-1], refs[-1]
    rows = parts[0].shape[0]
    place = where[0] & 1 if by_core else lax.div(where[0], 2)
    for step, part in enumerate(parts):
        out_ref[pl.ds(pl.multiple_of((place ^ step) * rows, rows), rows), :] = part[...]


def join(where, parts, by_core):
    count, (rows, width) = len(parts), parts[0].shape
    return pl.pallas_call(
        functools.partial(join_kernel, by_core=by_core),
        out_shape=jax.ShapeDtypeStruct((count * rows, width), parts[0].dtype),
        in_specs=[SCALARS] + [WHOLE] * count,
        compiler_params=params(10),
        cost_estimate=cost(0, 0),
        name="join",
    )(where, *parts)


def swap(value, axis, size, step):
    return lax.ppermute(value, axis, [(i, i ^ step) for i in range(size)])


def shards(adj_tiles, tile_counts, tile_cols, features, weight, upstream):
    n_row, n_col = lax.axis_size("row"), lax.axis_size("col")
    assert n_row & (n_row - 1) == 0 and n_col & (n_col - 1) == 0 and n_row > 1
    adj, counts, cols = adj_tiles[0, 0], tile_counts[0, 0], tile_cols[0, 0]
    rows, depth = upstream.shape[0], features.shape[0]
    col_tiles = depth * n_row // adj.shape[1]
    chips = n_row // 2
    where = jnp.stack([lax.axis_index("row"), lax.axis_index("col")]).astype(jnp.int32)
    steps = [*range(n_col - 1, 0, -1), 0]

    dense = {}
    for i in range(0, n_col, 2):
        group = steps[i : i + 2]
        dense.update(zip(group, dense_rows(where, group, counts, cols, adj, rows, col_tiles)))
    blocks = [dense[s] for s in steps]

    away = gate([swap(features, "row", n_row, 2 * s) for s in range(chips - 1, 0, -1)], blocks)
    even = [features, *away[::-1]]
    odd = [swap(shard, "row", n_row, 1) for shard in even]
    halves = forward(where, blocks, even, 0, [], jnp.float32)

    came = []
    for s, block, half in zip(steps[:-1], blocks, halves):
        share = forward(where, [block], odd, 1, [half], jnp.bfloat16)[0]
        came.append(swap(share, "col", n_col, s))
    own = forward(where, blocks[-1:], odd, 1, halves[-1:], jnp.float32)
    scale = 1.0 / math.sqrt(rows * n_row * n_col)
    hidden, piece, part = middle([*own, *came], weight, upstream, scale)

    pieces = {s: swap(piece, "col", n_col, s) for s in steps[:-1]}
    pieces[0] = piece
    kept, sent = split(where, [part], 2, True)
    part, *others = split(where, [kept, swap(sent, "row", n_row, 1)], chips, False)

    soon, late = [0, 1], steps[:-2]
    early = backward(
        where, [dense[s] for s in soon], [pieces[s] for s in soon], 0, n_row, n_row, depth, None, jnp.float32
    )
    last = functools.partial(backward, where, [dense[s] for s in late], [pieces[s] for s in late])
    sent = last(0, chips, n_row, depth, early, jnp.bfloat16, [part])
    kept = last(chips, chips, n_row, depth, early, jnp.float32)
    came = swap(sent, "row", n_row, 1)
    summed = [(kept[s] + came[s].astype(jnp.float32)).astype(jnp.bfloat16) for s in range(1, chips)]
    parts = [swap(summed[s - 1], "row", n_row, 2 * s) for s in range(chips - 1, 0, -1)]

    others = gate([swap(other, "row", n_row, 2 * s) for s, other in enumerate(others, 1)], [kept])
    part = sum(others, part)
    part = sum([swap(part, "col", n_col, s) for s in range(1, n_col)], part)
    half = join(where, [part] + [swap(part, "row", n_row, 2 * s) for s in range(1, chips)], False)
    weight_grad = join(where, [half, swap(half, "row", n_row, 1)], True)
    return hidden, weight_grad, finish(kept, came, parts)


def solution(mesh):
    placed = (
        P("row", "col", None, None, None),
        P("row", "col", None),
        P("row", "col", None),
        P(("col", "row"), None),
        P(),
        P(("row", "col"), None),
    )
    return jax.shard_map(
        shards,
        mesh=mesh,
        in_specs=placed,
        out_specs=(P(("row", "col"), None), P(), P(("col", "row"), None)),
        check_vma=False,
    )
```

```python
import functools
import math

import jax
import jax.numpy as jnp
from jax import lax
from jax.experimental import pallas as pl
from jax.experimental.pallas import tpu as pltpu
from jax.sharding import PartitionSpec as P


MIB = 1024 * 1024
SCALARS = pl.BlockSpec(memory_space=pltpu.SMEM)
WHOLE = pl.BlockSpec(memory_space=pltpu.VMEM)
UNREAD = pl.BlockSpec(memory_space=pl.ANY)


def params(mib):
    return pltpu.CompilerParams(vmem_limit_bytes=mib * MIB)


def cost(flops, moved, exps=0):
    return pl.CostEstimate(flops=flops, bytes_accessed=moved, transcendentals=exps)


def near(value):
    return pltpu.with_memory_space_constraint(value, pltpu.VMEM)


def dense_kernel(where, counts, cols, adj_ref, *refs, steps, window):
    outs, (held, total, sems) = refs[: len(steps)], refs[len(steps) :]
    slots, tile, _ = adj_ref.shape
    per = outs[0].shape[0] // tile
    width = outs[0].shape[1]

    plans = []
    for i, step in enumerate(steps):
        first = (where[1] ^ step) * per
        start = lax.fori_loop(0, first, lambda t, s: s + counts[t], jnp.int32(0))
        for u in range(per):
            count = counts[first + u]
            base = jnp.minimum(start, slots - window)
            fetch = pltpu.make_async_copy(
                adj_ref.at[pl.ds(base, window)], held.at[i * per + u], sems.at[i * per + u]
            )
            fetch.start()
            plans.append((start, start - base, count, fetch))
            start = start + count

    for i, out_ref in enumerate(outs):
        out_ref[...] = jnp.zeros_like(out_ref)
    for n, (start, shift, count, fetch) in enumerate(plans):
        out_ref = outs[n // per]
        rows = pl.ds((n % per) * tile, tile)
        fetch.wait()

        def place(j):
            c = cols[start + j]
            out_ref[rows, pl.ds(pl.multiple_of(c * tile, tile), tile)] = held[n, shift + j]
            return lax.shift_left(jnp.int32(1), c)

        def four(i, state):
            seen, twice = state
            for v in range(4):
                bit = place(4 * i + v)
                twice = twice | (seen & bit)
                seen = seen | bit
            return seen, twice

        def one(j, state):
            seen, twice = state
            bit = place(j)
            return seen | bit, twice | (seen & bit)

        groups = lax.div(count, 4)
        state = lax.fori_loop(0, groups, four, (jnp.int32(0), jnp.int32(0)))
        seen, twice = lax.fori_loop(4 * groups, count, one, state)
        repeated = (twice != 0) if width // tile <= 32 else (count > 0)

        @pl.when(repeated)
        def _():
            total[...] = jnp.zeros_like(total)

            def add(j, carry):
                here = pl.ds(pl.multiple_of(cols[start + j] * tile, tile), tile)
                total[:, here] += held[n, shift + j].astype(jnp.float32)
                return carry

            lax.fori_loop(0, count, add, 0)
            out_ref[rows, :] = total[...].astype(out_ref.dtype)


def dense_rows(where, steps, counts, cols, adj, rows, col_tiles):
    slots, tile, _ = adj.shape
    window = min(col_tiles, slots)
    width = col_tiles * tile
    tiles = rows // tile * len(steps)
    return pl.pallas_call(
        functools.partial(dense_kernel, steps=steps, window=window),
        out_shape=[pltpu.VMEM((rows, width), adj.dtype) for _ in steps],
        in_specs=[SCALARS, SCALARS, SCALARS, pl.BlockSpec(memory_space=pltpu.HBM)],
        out_specs=[WHOLE] * len(steps),
        scratch_shapes=[
            pltpu.VMEM((tiles, window, tile, tile), adj.dtype),
            pltpu.VMEM((tile, width), jnp.float32),
            pltpu.SemaphoreType.DMA((tiles,)),
        ],
        compiler_params=params(16),
        cost_estimate=cost(0, 5 * len(steps) * rows * width),
        name="dense_rows",
    )(where, counts, cols, pltpu.with_memory_space_constraint(adj, pltpu.HBM))


def forward_kernel(where, *refs, blocks, count, odd, before):
    dense, shards, sums = refs[:blocks], refs[blocks : blocks + count], refs[blocks + count :]
    depth = shards[0].shape[0]
    for i, a_ref in enumerate(dense):
        value = sums[i][...] if before else None
        for k, shard in enumerate(shards):
            cols = pl.ds(pl.multiple_of((where[0] ^ (2 * k + odd)) * depth, depth), depth)
            part = jnp.dot(a_ref[:, cols], shard[...], preferred_element_type=jnp.float32)
            value = part if value is None else value + part
        out_ref = sums[blocks + i if before else i]
        out_ref[...] = value.astype(out_ref.dtype)


def forward(where, dense, shards, odd, before, kind):
    rows, width = dense[0].shape[0], shards[0].shape[1]
    blocks, count = len(dense), len(shards)
    operands = [near(x) for x in [*dense, *shards, *before]]
    return pl.pallas_call(
        functools.partial(forward_kernel, blocks=blocks, count=count, odd=odd, before=bool(before)),
        out_shape=[pltpu.VMEM((rows, width), kind)] * blocks,
        in_specs=[SCALARS] + [WHOLE] * len(operands),
        out_specs=[WHOLE] * blocks,
        compiler_params=params(10),
        cost_estimate=cost(blocks * dense[0].size * width, blocks * dense[0].size),
        name="forward_rows",
    )(where, *operands)


def middle_kernel(*refs, scale, came):
    parts = refs[: came + 1]
    weight_ref, up_ref, hidden_ref, grad_ref, wgrad_ref = refs[came + 1 :]
    agg = parts[0][...].astype(jnp.float32)
    for part in parts[1:]:
        agg = agg + part[...].astype(jnp.float32)
    agg = agg.astype(jnp.bfloat16)
    weight = weight_ref[...]
    pre = jnp.dot(agg, weight, preferred_element_type=jnp.float32)
    sig = jax.nn.sigmoid(pre)
    hidden_ref[...] = (pre * sig).astype(jnp.bfloat16)
    pre_grad = (up_ref[...].astype(jnp.float32) * sig * (1.0 + pre * (1.0 - sig))).astype(jnp.bfloat16)
    grad_ref[...] = lax.dot_general(
        weight, pre_grad, (((1,), (1,)), ((), ())), preferred_element_type=jnp.float32
    ).astype(jnp.bfloat16)
    wgrad_ref[...] = scale * lax.dot_general(
        agg, pre_grad, (((0,), (0,)), ((), ())), preferred_element_type=jnp.float32
    )


def middle(parts, weight, upstream, scale):
    rows, width = upstream.shape
    return pl.pallas_call(
        functools.partial(middle_kernel, scale=scale, came=len(parts) - 1),
        out_shape=(
            jax.ShapeDtypeStruct((rows, width), jnp.bfloat16),
            jax.ShapeDtypeStruct((width, rows), jnp.bfloat16),
            jax.ShapeDtypeStruct((width, width), jnp.float32),
        ),
        compiler_params=params(16),
        cost_estimate=cost(6 * rows * width * width, 10 * rows * width, rows * width),
        name="middle",
    )(*parts, weight, upstream)


def backward_kernel(where, *refs, count, first, before, n_row):
    dense, pieces = refs[:count], refs[count : 2 * count]
    out_ref = refs[-1]
    columns, _, depth = out_ref.shape
    half = n_row // 2

    def one(j, carry):
        at = first + j
        step = 2 * lax.rem(at, half) + (at < half).astype(jnp.int32)
        cols = pl.ds(pl.multiple_of((where[0] ^ step) * depth, depth), depth)
        value = refs[2 * count][at] if before else None
        for a_ref, piece in zip(dense, pieces):
            part = jnp.dot(piece[...], a_ref[:, cols], preferred_element_type=jnp.float32)
            value = part if value is None else value + part
        out_ref[j] = value.astype(out_ref.dtype)
        return carry

    lax.fori_loop(0, columns, one, 0)


def backward(where, dense, pieces, first, columns, n_row, depth, before, kind, after=()):
    count = len(pieces)
    width, rows = pieces[0].shape
    operands = [near(x) for x in [*dense, *pieces] + ([] if before is None else [before])]
    return pl.pallas_call(
        functools.partial(
            backward_kernel, count=count, first=first, before=before is not None, n_row=n_row
        ),
        out_shape=pltpu.VMEM((columns, width, depth), kind),
        in_specs=[SCALARS] + [WHOLE] * len(operands) + [UNREAD] * len(after),
        out_specs=WHOLE,
        compiler_params=params(10),
        cost_estimate=cost(0, 0),
        name="backward_cols",
    )(where, *operands, *after)


def finish_kernel(*refs):
    parts, out_ref = refs[:-1], refs[-1]
    value = parts[0][0].astype(jnp.float32) + parts[1][0].astype(jnp.float32)
    for part in parts[2:]:
        value = value + part[...].astype(jnp.float32)
    out_ref[...] = value.T.astype(out_ref.dtype)


def finish(kept, came, parts):
    _, width, rows = kept.shape
    own = pl.BlockSpec((1, width, rows), lambda i: (0, 0, 0))
    part = pl.BlockSpec((width, rows), lambda i: (0, 0))
    return pl.pallas_call(
        finish_kernel,
        out_shape=jax.ShapeDtypeStruct((rows, width), jnp.bfloat16),
        grid=(1,),
        in_specs=[own, own] + [part] * len(parts),
        out_specs=pl.BlockSpec((rows, width), lambda i: (0, 0)),
        compiler_params=params(12),
        cost_estimate=cost(len(parts) * rows * width, 4 * len(parts) * rows * width),
        name="finish",
    )(kept, came, *parts)


def gate(values, after):
    count = len(values)
    return pl.pallas_call(
        lambda *refs: None,
        out_shape=[pltpu.VMEM(x.shape, x.dtype) for x in values],
        in_specs=[WHOLE] * count + [UNREAD] * len(after),
        out_specs=[WHOLE] * count,
        input_output_aliases={i: i for i in range(count)},
        compiler_params=params(4),
        cost_estimate=cost(0, 0),
        name="gate",
    )(*map(near, values), *after)


def split_kernel(where, value_ref, kept_ref, sent_ref, *, rows):
    core = where[0] & 1
    for i in range(kept_ref.shape[0] // rows):
        at = pl.ds(i * rows, rows)
        kept_ref[at, :] = value_ref[pl.ds(pl.multiple_of((2 * i + core) * rows, rows), rows), :]
        sent_ref[at, :] = value_ref[pl.ds(pl.multiple_of((2 * i + 1 - core) * rows, rows), rows), :]


def split(where, value, count):
    rows, width = value.shape
    half = jax.ShapeDtypeStruct((rows // 2, width), value.dtype)
    return pl.pallas_call(
        functools.partial(split_kernel, rows=rows // count),
        out_shape=[half, half],
        in_specs=[SCALARS, WHOLE],
        compiler_params=params(10),
        cost_estimate=cost(0, 0),
        name="split",
    )(where, value)


def own_kernel(where, values_ref, out_ref):
    rows = out_ref.shape[0]
    at = pl.ds(pl.multiple_of(lax.div(where[0], 2) * rows, rows), rows)
    value = values_ref[0, at, :]
    for i in range(1, values_ref.shape[0]):
        value = value + values_ref[i, at, :]
    out_ref[...] = value


def own(where, values, rows):
    return pl.pallas_call(
        own_kernel,
        out_shape=jax.ShapeDtypeStruct((rows, values.shape[2]), values.dtype),
        in_specs=[SCALARS, WHOLE],
        compiler_params=params(10),
        cost_estimate=cost(0, 0),
        name="own",
    )(where, values)


def keep_kernel(value_ref, out_ref):
    out_ref[...] = value_ref[...]


def keep(value):
    return pl.pallas_call(
        keep_kernel,
        out_shape=jax.ShapeDtypeStruct(value.shape, value.dtype),
        compiler_params=params(10),
        cost_estimate=cost(0, 0),
        name="keep",
    )(value)


def swap(value, axis, size, step):
    return lax.ppermute(value, axis, [(i, i ^ step) for i in range(size)])


def shards(adj_tiles, tile_counts, tile_cols, features, weight, upstream):
    n_row, n_col = lax.axis_size("row"), lax.axis_size("col")
    assert n_row & (n_row - 1) == 0 and n_col & (n_col - 1) == 0 and n_row > 1
    adj, counts, cols = adj_tiles[0, 0], tile_counts[0, 0], tile_cols[0, 0]
    rows, depth = upstream.shape[0], features.shape[0]
    col_tiles = depth * n_row // adj.shape[1]
    chips = n_row // 2
    where = jnp.stack([lax.axis_index("row"), lax.axis_index("col")]).astype(jnp.int32)
    steps = [*range(n_col - 1, 0, -1), 0]

    dense = {}
    for i in range(0, n_col, 2):
        group = steps[i : i + 2]
        dense.update(zip(group, dense_rows(where, group, counts, cols, adj, rows, col_tiles)))
    blocks = [dense[s] for s in steps]

    away = gate([swap(features, "row", n_row, 2 * s) for s in range(chips - 1, 0, -1)], blocks)
    even = [features, *away[::-1]]
    odd = [swap(shard, "row", n_row, 1) for shard in even]
    halves = forward(where, blocks, even, 0, [], jnp.float32)

    came = []
    for s, block, half in zip(steps[:-1], blocks, halves):
        share = forward(where, [block], odd, 1, [half], jnp.bfloat16)[0]
        came.append(swap(share, "col", n_col, s))
    mine = forward(where, blocks[-1:], odd, 1, halves[-1:], jnp.float32)
    scale = 1.0 / math.sqrt(rows * n_row * n_col)
    hidden, piece, part = middle([*mine, *came], weight, upstream, scale)

    pieces = {s: swap(piece, "col", n_col, s) for s in steps[:-1]}
    pieces[0] = piece
    kept, sent = split(where, part, n_row)
    cores = [[i for i in range(n_row) if i % 2 == core] for core in range(2)]
    part = lax.all_gather(kept + swap(sent, "row", n_row, 1), "row", axis_index_groups=cores)
    part = lax.all_gather(own(where, part, part.shape[1] // chips), "col")
    part = lax.all_gather(sum([part[i] for i in range(1, n_col)], part[0]), "row", axis=0, tiled=True)
    weight_grad = keep(part)

    soon, late = [0, 1], steps[:-2]
    early = backward(
        where, [dense[s] for s in soon], [pieces[s] for s in soon], 0, n_row, n_row, depth, None, jnp.float32
    )
    last = functools.partial(backward, where, [dense[s] for s in late], [pieces[s] for s in late])
    sent = last(0, chips, n_row, depth, early, jnp.bfloat16, [weight_grad])
    kept = last(chips, chips, n_row, depth, early, jnp.float32)
    came = swap(sent, "row", n_row, 1)
    summed = [(kept[s] + came[s].astype(jnp.float32)).astype(jnp.bfloat16) for s in range(1, chips)]
    parts = [swap(summed[s - 1], "row", n_row, 2 * s) for s in range(chips - 1, 0, -1)]

    return hidden, weight_grad, finish(kept, came, parts)


def solution(mesh):
    placed = (
        P("row", "col", None, None, None),
        P("row", "col", None),
        P("row", "col", None),
        P(("col", "row"), None),
        P(),
        P(("row", "col"), None),
    )
    return jax.shard_map(
        shards,
        mesh=mesh,
        in_specs=placed,
        out_specs=(P(("row", "col"), None), P(), P(("col", "row"), None)),
        check_vma=False,
    )
```

```python
import functools
import math

import jax
import jax.numpy as jnp
from jax import lax
from jax.experimental import pallas as pl
from jax.experimental.pallas import tpu as pltpu
from jax.sharding import PartitionSpec as P


MIB = 1024 * 1024
SCALARS = pl.BlockSpec(memory_space=pltpu.SMEM)
WHOLE = pl.BlockSpec(memory_space=pltpu.VMEM)
UNREAD = pl.BlockSpec(memory_space=pl.ANY)


def params(mib):
    return pltpu.CompilerParams(vmem_limit_bytes=mib * MIB)


def cost(flops, moved, exps=0):
    return pl.CostEstimate(flops=flops, bytes_accessed=moved, transcendentals=exps)


def near(value):
    return pltpu.with_memory_space_constraint(value, pltpu.VMEM)


def dense_kernel(where, counts, cols, adj_ref, *refs, steps, window):
    outs, (held, total, sems) = refs[: len(steps)], refs[len(steps) :]
    slots, tile, _ = adj_ref.shape
    per = outs[0].shape[0] // tile
    width = outs[0].shape[1]

    plans = []
    for i, step in enumerate(steps):
        first = (where[1] ^ step) * per
        start = lax.fori_loop(0, first, lambda t, s: s + counts[t], jnp.int32(0))
        for u in range(per):
            count = counts[first + u]
            base = jnp.minimum(start, slots - window)
            fetch = pltpu.make_async_copy(
                adj_ref.at[pl.ds(base, window)], held.at[i * per + u], sems.at[i * per + u]
            )
            fetch.start()
            plans.append((start, start - base, count, fetch))
            start = start + count

    for i, out_ref in enumerate(outs):
        out_ref[...] = jnp.zeros_like(out_ref)
    for n, (start, shift, count, fetch) in enumerate(plans):
        out_ref = outs[n // per]
        rows = pl.ds((n % per) * tile, tile)
        fetch.wait()

        def place(j):
            c = cols[start + j]
            out_ref[rows, pl.ds(pl.multiple_of(c * tile, tile), tile)] = held[n, shift + j]
            return lax.shift_left(jnp.int32(1), c)

        def four(i, state):
            seen, twice = state
            for v in range(4):
                bit = place(4 * i + v)
                twice = twice | (seen & bit)
                seen = seen | bit
            return seen, twice

        def one(j, state):
            seen, twice = state
            bit = place(j)
            return seen | bit, twice | (seen & bit)

        groups = lax.div(count, 4)
        state = lax.fori_loop(0, groups, four, (jnp.int32(0), jnp.int32(0)))
        seen, twice = lax.fori_loop(4 * groups, count, one, state)
        repeated = (twice != 0) if width // tile <= 32 else (count > 0)

        @pl.when(repeated)
        def _():
            total[...] = jnp.zeros_like(total)

            def add(j, carry):
                here = pl.ds(pl.multiple_of(cols[start + j] * tile, tile), tile)
                total[:, here] += held[n, shift + j].astype(jnp.float32)
                return carry

            lax.fori_loop(0, count, add, 0)
            out_ref[rows, :] = total[...].astype(out_ref.dtype)


def dense_rows(where, steps, counts, cols, adj, rows, col_tiles):
    slots, tile, _ = adj.shape
    window = min(col_tiles, slots)
    width = col_tiles * tile
    tiles = rows // tile * len(steps)
    return pl.pallas_call(
        functools.partial(dense_kernel, steps=steps, window=window),
        out_shape=[pltpu.VMEM((rows, width), adj.dtype) for _ in steps],
        in_specs=[SCALARS, SCALARS, SCALARS, pl.BlockSpec(memory_space=pltpu.HBM)],
        out_specs=[WHOLE] * len(steps),
        scratch_shapes=[
            pltpu.VMEM((tiles, window, tile, tile), adj.dtype),
            pltpu.VMEM((tile, width), jnp.float32),
            pltpu.SemaphoreType.DMA((tiles,)),
        ],
        compiler_params=params(16),
        cost_estimate=cost(0, 5 * len(steps) * rows * width),
        name="dense_rows",
    )(where, counts, cols, pltpu.with_memory_space_constraint(adj, pltpu.HBM))


def forward_kernel(where, *refs, blocks, count, odd, before):
    dense, shards, sums = refs[:blocks], refs[blocks : blocks + count], refs[blocks + count :]
    depth = shards[0].shape[0]
    for i, a_ref in enumerate(dense):
        value = sums[i][...] if before else None
        for k, shard in enumerate(shards):
            cols = pl.ds(pl.multiple_of((where[0] ^ (2 * k + odd)) * depth, depth), depth)
            part = jnp.dot(a_ref[:, cols], shard[...], preferred_element_type=jnp.float32)
            value = part if value is None else value + part
        out_ref = sums[blocks + i if before else i]
        out_ref[...] = value.astype(out_ref.dtype)


def forward(where, dense, shards, odd, before, kind):
    rows, width = dense[0].shape[0], shards[0].shape[1]
    blocks, count = len(dense), len(shards)
    operands = [near(x) for x in [*dense, *shards, *before]]
    return pl.pallas_call(
        functools.partial(forward_kernel, blocks=blocks, count=count, odd=odd, before=bool(before)),
        out_shape=[pltpu.VMEM((rows, width), kind)] * blocks,
        in_specs=[SCALARS] + [WHOLE] * len(operands),
        out_specs=[WHOLE] * blocks,
        compiler_params=params(10),
        cost_estimate=cost(blocks * dense[0].size * width, blocks * dense[0].size),
        name="forward_rows",
    )(where, *operands)


def middle_kernel(*refs, scale, came):
    parts = refs[: came + 1]
    weight_ref, up_ref, hidden_ref, grad_ref, wgrad_ref = refs[came + 1 :]
    agg = parts[0][...].astype(jnp.float32)
    for part in parts[1:]:
        agg = agg + part[...].astype(jnp.float32)
    agg = agg.astype(jnp.bfloat16)
    weight = weight_ref[...]
    pre = jnp.dot(agg, weight, preferred_element_type=jnp.float32)
    sig = jax.nn.sigmoid(pre)
    hidden_ref[...] = (pre * sig).astype(jnp.bfloat16)
    pre_grad = (up_ref[...].astype(jnp.float32) * sig * (1.0 + pre * (1.0 - sig))).astype(jnp.bfloat16)
    grad_ref[...] = lax.dot_general(
        weight, pre_grad, (((1,), (1,)), ((), ())), preferred_element_type=jnp.float32
    ).astype(jnp.bfloat16)
    wgrad_ref[...] = scale * lax.dot_general(
        agg, pre_grad, (((0,), (0,)), ((), ())), preferred_element_type=jnp.float32
    )


def middle(parts, weight, upstream, scale):
    rows, width = upstream.shape
    return pl.pallas_call(
        functools.partial(middle_kernel, scale=scale, came=len(parts) - 1),
        out_shape=(
            jax.ShapeDtypeStruct((rows, width), jnp.bfloat16),
            jax.ShapeDtypeStruct((width, rows), jnp.bfloat16),
            jax.ShapeDtypeStruct((width, width), jnp.float32),
        ),
        compiler_params=params(16),
        cost_estimate=cost(6 * rows * width * width, 10 * rows * width, rows * width),
        name="middle",
    )(*parts, weight, upstream)


def backward_kernel(where, *refs, count, first, before, n_row):
    dense, pieces = refs[:count], refs[count : 2 * count]
    out_ref = refs[-1]
    columns, _, depth = out_ref.shape
    half = n_row // 2

    def one(j, carry):
        at = first + j
        step = 2 * lax.rem(at, half) + (at < half).astype(jnp.int32)
        cols = pl.ds(pl.multiple_of((where[0] ^ step) * depth, depth), depth)
        value = refs[2 * count][at] if before else None
        for a_ref, piece in zip(dense, pieces):
            part = jnp.dot(piece[...], a_ref[:, cols], preferred_element_type=jnp.float32)
            value = part if value is None else value + part
        out_ref[j] = value.astype(out_ref.dtype)
        return carry

    lax.fori_loop(0, columns, one, 0)


def backward(where, dense, pieces, first, columns, n_row, depth, before, kind, after=()):
    count = len(pieces)
    width, rows = pieces[0].shape
    operands = [near(x) for x in [*dense, *pieces] + ([] if before is None else [before])]
    return pl.pallas_call(
        functools.partial(
            backward_kernel, count=count, first=first, before=before is not None, n_row=n_row
        ),
        out_shape=pltpu.VMEM((columns, width, depth), kind),
        in_specs=[SCALARS] + [WHOLE] * len(operands) + [UNREAD] * len(after),
        out_specs=WHOLE,
        compiler_params=params(10),
        cost_estimate=cost(0, 0),
        name="backward_cols",
    )(where, *operands, *after)


def finish_kernel(*refs):
    parts, out_ref = refs[:-1], refs[-1]
    value = parts[0][0].astype(jnp.float32) + parts[1][0].astype(jnp.float32)
    for part in parts[2:]:
        value = value + part[...].astype(jnp.float32)
    out_ref[...] = value.T.astype(out_ref.dtype)


def finish(kept, came, parts):
    _, width, rows = kept.shape
    own = pl.BlockSpec((1, width, rows), lambda i: (0, 0, 0))
    part = pl.BlockSpec((width, rows), lambda i: (0, 0))
    return pl.pallas_call(
        finish_kernel,
        out_shape=jax.ShapeDtypeStruct((rows, width), jnp.bfloat16),
        grid=(1,),
        in_specs=[own, own] + [part] * len(parts),
        out_specs=pl.BlockSpec((rows, width), lambda i: (0, 0)),
        compiler_params=params(12),
        cost_estimate=cost(len(parts) * rows * width, 4 * len(parts) * rows * width),
        name="finish",
    )(kept, came, *parts)


def gate(values, after):
    count = len(values)
    return pl.pallas_call(
        lambda *refs: None,
        out_shape=[pltpu.VMEM(x.shape, x.dtype) for x in values],
        in_specs=[WHOLE] * count + [UNREAD] * len(after),
        out_specs=[WHOLE] * count,
        input_output_aliases={i: i for i in range(count)},
        compiler_params=params(4),
        cost_estimate=cost(0, 0),
        name="gate",
    )(*map(near, values), *after)


def total_kernel(*refs):
    parts, out_ref = refs[:-1], refs[-1]
    rows = out_ref.shape[0]
    value = None
    for part in parts:
        for i in range(part.shape[0] // rows):
            term = part[pl.ds(i * rows, rows), :].astype(jnp.float32)
            value = term if value is None else value + term
    out_ref[...] = value.astype(out_ref.dtype)


def total(parts, rows, kind):
    return pl.pallas_call(
        total_kernel,
        out_shape=jax.ShapeDtypeStruct((rows, parts[0].shape[1]), kind),
        compiler_params=params(10),
        cost_estimate=cost(0, 0),
        name="total",
    )(*parts)


def swap(value, axis, size, step):
    return lax.ppermute(value, axis, [(i, i ^ step) for i in range(size)])


def shards(adj_tiles, tile_counts, tile_cols, features, weight, upstream):
    n_row, n_col = lax.axis_size("row"), lax.axis_size("col")
    assert n_row & (n_row - 1) == 0 and n_col & (n_col - 1) == 0 and n_row > 1
    adj, counts, cols = adj_tiles[0, 0], tile_counts[0, 0], tile_cols[0, 0]
    rows, depth = upstream.shape[0], features.shape[0]
    col_tiles = depth * n_row // adj.shape[1]
    chips = n_row // 2
    where = jnp.stack([lax.axis_index("row"), lax.axis_index("col")]).astype(jnp.int32)
    steps = [*range(n_col - 1, 0, -1), 0]

    dense = {}
    for i in range(0, n_col, 2):
        group = steps[i : i + 2]
        dense.update(zip(group, dense_rows(where, group, counts, cols, adj, rows, col_tiles)))
    blocks = [dense[s] for s in steps]

    away = gate([swap(features, "row", n_row, 2 * s) for s in range(chips - 1, 0, -1)], blocks)
    even = [features, *away[::-1]]
    odd = [swap(shard, "row", n_row, 1) for shard in even]
    halves = forward(where, blocks, even, 0, [], jnp.float32)

    came = []
    for s, block, half in zip(steps[:-1], blocks, halves):
        share = forward(where, [block], odd, 1, [half], jnp.bfloat16)[0]
        came.append(swap(share, "col", n_col, s))
    own = forward(where, blocks[-1:], odd, 1, halves[-1:], jnp.float32)
    scale = 1.0 / math.sqrt(rows * n_row * n_col)
    hidden, piece, part = middle([*own, *came], weight, upstream, scale)

    pieces = {s: swap(piece, "col", n_col, s) for s in steps[:-1]}
    pieces[0] = piece
    cores = [[i for i in range(n_row) if i % 2 == core] for core in range(2)]
    part = (part + swap(part, "row", n_row, 1)).astype(jnp.bfloat16)
    gathered = lax.all_gather(part, "row", axis_index_groups=cores, tiled=True)
    part = total([gathered], part.shape[0], jnp.bfloat16)

    soon, late = [0, 1], steps[:-2]
    early = backward(
        where, [dense[s] for s in soon], [pieces[s] for s in soon], 0, n_row, n_row, depth, None, jnp.float32
    )
    last = functools.partial(backward, where, [dense[s] for s in late], [pieces[s] for s in late])
    sent = last(0, chips, n_row, depth, early, jnp.bfloat16, [part])
    kept = last(chips, chips, n_row, depth, early, jnp.float32)
    came = swap(sent, "row", n_row, 1)
    summed = [(kept[s] + came[s].astype(jnp.float32)).astype(jnp.bfloat16) for s in range(1, chips)]
    parts = [swap(summed[s - 1], "row", n_row, 2 * s) for s in range(chips - 1, 0, -1)]

    part = gate([part], [kept])[0]
    weight_grad = total([part] + [swap(part, "col", n_col, s) for s in steps[:-1]], part.shape[0], jnp.float32)
    return hidden, weight_grad, finish(kept, came, parts)


def solution(mesh):
    placed = (
        P("row", "col", None, None, None),
        P("row", "col", None),
        P("row", "col", None),
        P(("col", "row"), None),
        P(),
        P(("row", "col"), None),
    )
    return jax.shard_map(
        shards,
        mesh=mesh,
        in_specs=placed,
        out_specs=(P(("row", "col"), None), P(), P(("col", "row"), None)),
        check_vma=False,
    )
```

```python
import functools
import math

import jax
import jax.numpy as jnp
from jax import lax
from jax.experimental import pallas as pl
from jax.experimental.pallas import tpu as pltpu
from jax.sharding import PartitionSpec as P


MIB = 1024 * 1024
SCALARS = pl.BlockSpec(memory_space=pltpu.SMEM)
WHOLE = pl.BlockSpec(memory_space=pltpu.VMEM)
UNREAD = pl.BlockSpec(memory_space=pl.ANY)


def params(mib):
    return pltpu.CompilerParams(vmem_limit_bytes=mib * MIB)


def cost(flops, moved, exps=0):
    return pl.CostEstimate(flops=flops, bytes_accessed=moved, transcendentals=exps)


def near(value):
    return pltpu.with_memory_space_constraint(value, pltpu.VMEM)


def dense_kernel(where, counts, cols, adj_ref, *refs, steps, window):
    outs, (held, total, sems) = refs[: len(steps)], refs[len(steps) :]
    slots, tile, _ = adj_ref.shape
    per = outs[0].shape[0] // tile
    width = outs[0].shape[1]

    plans = []
    for i, step in enumerate(steps):
        first = (where[1] ^ step) * per
        start = lax.fori_loop(0, first, lambda t, s: s + counts[t], jnp.int32(0))
        for u in range(per):
            count = counts[first + u]
            base = jnp.minimum(start, slots - window)
            fetch = pltpu.make_async_copy(
                adj_ref.at[pl.ds(base, window)], held.at[i * per + u], sems.at[i * per + u]
            )
            fetch.start()
            plans.append((start, start - base, count, fetch))
            start = start + count

    for i, out_ref in enumerate(outs):
        out_ref[...] = jnp.zeros_like(out_ref)
    for n, (start, shift, count, fetch) in enumerate(plans):
        out_ref = outs[n // per]
        rows = pl.ds((n % per) * tile, tile)
        fetch.wait()

        def place(j):
            c = cols[start + j]
            out_ref[rows, pl.ds(pl.multiple_of(c * tile, tile), tile)] = held[n, shift + j]
            return lax.shift_left(jnp.int32(1), c)

        def four(i, state):
            seen, twice = state
            for v in range(4):
                bit = place(4 * i + v)
                twice = twice | (seen & bit)
                seen = seen | bit
            return seen, twice

        def one(j, state):
            seen, twice = state
            bit = place(j)
            return seen | bit, twice | (seen & bit)

        groups = lax.div(count, 4)
        state = lax.fori_loop(0, groups, four, (jnp.int32(0), jnp.int32(0)))
        seen, twice = lax.fori_loop(4 * groups, count, one, state)
        repeated = (twice != 0) if width // tile <= 32 else (count > 0)

        @pl.when(repeated)
        def _():
            total[...] = jnp.zeros_like(total)

            def add(j, carry):
                here = pl.ds(pl.multiple_of(cols[start + j] * tile, tile), tile)
                total[:, here] += held[n, shift + j].astype(jnp.float32)
                return carry

            lax.fori_loop(0, count, add, 0)
            out_ref[rows, :] = total[...].astype(out_ref.dtype)


def dense_rows(where, steps, counts, cols, adj, rows, col_tiles):
    slots, tile, _ = adj.shape
    window = min(col_tiles, slots)
    width = col_tiles * tile
    tiles = rows // tile * len(steps)
    return pl.pallas_call(
        functools.partial(dense_kernel, steps=steps, window=window),
        out_shape=[pltpu.VMEM((rows, width), adj.dtype) for _ in steps],
        in_specs=[SCALARS, SCALARS, SCALARS, pl.BlockSpec(memory_space=pltpu.HBM)],
        out_specs=[WHOLE] * len(steps),
        scratch_shapes=[
            pltpu.VMEM((tiles, window, tile, tile), adj.dtype),
            pltpu.VMEM((tile, width), jnp.float32),
            pltpu.SemaphoreType.DMA((tiles,)),
        ],
        compiler_params=params(26),
        cost_estimate=cost(0, 5 * len(steps) * rows * width),
        name="dense_rows",
    )(where, counts, cols, pltpu.with_memory_space_constraint(adj, pltpu.HBM))


def forward_kernel(where, a_ref, *refs, first, step):
    shards, out_ref, before = refs[:-1], refs[-1], None
    if first:
        shards, before = shards[:-1], shards[-1]
    depth = shards[0].shape[0]
    value = None if before is None else before[...]
    for k, shard in enumerate(shards):
        cols = pl.ds(pl.multiple_of((where[0] ^ (first + step * k)) * depth, depth), depth)
        part = jnp.dot(a_ref[:, cols], shard[...], preferred_element_type=jnp.float32)
        value = part if value is None else value + part
    out_ref[...] = value.astype(out_ref.dtype)


def forward(where, dense, shards, first, step, before, kind):
    rows, width = dense.shape[0], shards[0].shape[1]
    operands = [near(x) for x in [dense, *shards, *before]]
    flops = 2 * rows * dense.shape[1] * width
    return pl.pallas_call(
        functools.partial(forward_kernel, first=first, step=step),
        out_shape=pltpu.VMEM((rows, width), kind),
        in_specs=[SCALARS] + [WHOLE] * len(operands),
        out_specs=WHOLE,
        compiler_params=params(10),
        cost_estimate=cost(flops, dense.size * 2),
        name="forward_rows",
    )(where, *operands)


def middle_kernel(*refs, scale, came):
    parts = refs[: came + 1]
    weight_ref, up_ref, hidden_ref, grad_ref, wgrad_ref = refs[came + 1 :]
    agg = parts[0][...].astype(jnp.float32)
    for part in parts[1:]:
        agg = agg + part[...].astype(jnp.float32)
    agg = agg.astype(jnp.bfloat16)
    weight = weight_ref[...]
    pre = jnp.dot(agg, weight, preferred_element_type=jnp.float32)
    sig = jax.nn.sigmoid(pre)
    hidden_ref[...] = (pre * sig).astype(jnp.bfloat16)
    pre_grad = (up_ref[...].astype(jnp.float32) * sig * (1.0 + pre * (1.0 - sig))).astype(jnp.bfloat16)
    grad_ref[...] = lax.dot_general(
        weight, pre_grad, (((1,), (1,)), ((), ())), preferred_element_type=jnp.float32
    ).astype(jnp.bfloat16)
    wgrad_ref[...] = scale * lax.dot_general(
        agg, pre_grad, (((0,), (0,)), ((), ())), preferred_element_type=jnp.float32
    )


def middle(parts, weight, upstream, scale):
    rows, width = upstream.shape
    return pl.pallas_call(
        functools.partial(middle_kernel, scale=scale, came=len(parts) - 1),
        out_shape=(
            jax.ShapeDtypeStruct((rows, width), jnp.bfloat16),
            jax.ShapeDtypeStruct((width, rows), jnp.bfloat16),
            jax.ShapeDtypeStruct((width, width), jnp.float32),
        ),
        compiler_params=params(16),
        cost_estimate=cost(6 * rows * width * width, 10 * rows * width, rows * width),
        name="middle",
    )(*parts, weight, upstream)


def backward_kernel(where, *refs, count, first, before, n_row):
    dense, pieces = refs[:count], refs[count : 2 * count]
    out_ref = refs[-1]
    columns, _, depth = out_ref.shape
    half = n_row // 2

    def one(j, carry):
        at = first + j
        step = 2 * lax.rem(at, half) + (at < half).astype(jnp.int32)
        cols = pl.ds(pl.multiple_of((where[0] ^ step) * depth, depth), depth)
        value = refs[2 * count][at] if before else None
        for a_ref, piece in zip(dense, pieces):
            part = jnp.dot(piece[...], a_ref[:, cols], preferred_element_type=jnp.float32)
            value = part if value is None else value + part
        out_ref[j] = value.astype(out_ref.dtype)
        return carry

    lax.fori_loop(0, columns, one, 0)


def backward(where, dense, pieces, first, columns, n_row, depth, before, kind, after=()):
    count = len(pieces)
    width, rows = pieces[0].shape
    operands = [near(x) for x in [*dense, *pieces] + ([] if before is None else [before])]
    return pl.pallas_call(
        functools.partial(
            backward_kernel, count=count, first=first, before=before is not None, n_row=n_row
        ),
        out_shape=pltpu.VMEM((columns, width, depth), kind),
        in_specs=[SCALARS] + [WHOLE] * len(operands) + [UNREAD] * len(after),
        out_specs=WHOLE,
        compiler_params=params(10),
        cost_estimate=cost(0, 0),
        name="backward_cols",
    )(where, *operands, *after)


def finish_kernel(*refs):
    parts, out_ref = refs[:-1], refs[-1]
    value = parts[0][0].astype(jnp.float32) + parts[1][0].astype(jnp.float32)
    for part in parts[2:]:
        value = value + part[...].astype(jnp.float32)
    out_ref[...] = value.T.astype(out_ref.dtype)


def finish(kept, came, parts):
    _, width, rows = kept.shape
    own = pl.BlockSpec((1, width, rows), lambda i: (0, 0, 0))
    part = pl.BlockSpec((width, rows), lambda i: (0, 0))
    return pl.pallas_call(
        finish_kernel,
        out_shape=jax.ShapeDtypeStruct((rows, width), jnp.bfloat16),
        grid=(1,),
        in_specs=[own, own] + [part] * len(parts),
        out_specs=pl.BlockSpec((rows, width), lambda i: (0, 0)),
        compiler_params=params(12),
        cost_estimate=cost(len(parts) * rows * width, 4 * len(parts) * rows * width),
        name="finish",
    )(kept, came, *parts)


def gate(values, after):
    count = len(values)
    return pl.pallas_call(
        lambda *refs: None,
        out_shape=[pltpu.VMEM(x.shape, x.dtype) for x in values],
        in_specs=[WHOLE] * count + [UNREAD] * len(after),
        out_specs=[WHOLE] * count,
        input_output_aliases={i: i for i in range(count)},
        compiler_params=params(4),
        cost_estimate=cost(0, 0),
        name="gate",
    )(*map(near, values), *after)


def total_kernel(*refs, count):
    parts, out_ref = refs[:count], refs[-1]
    rows = out_ref.shape[0]
    value = None
    for part in parts:
        for i in range(part.shape[0] // rows):
            term = part[pl.ds(i * rows, rows), :].astype(jnp.float32)
            value = term if value is None else value + term
    out_ref[...] = value.astype(out_ref.dtype)


def total(parts, rows, kind, after=()):
    return pl.pallas_call(
        functools.partial(total_kernel, count=len(parts)),
        out_shape=jax.ShapeDtypeStruct((rows, parts[0].shape[1]), kind),
        in_specs=[WHOLE] * len(parts) + [UNREAD] * len(after),
        compiler_params=params(10),
        cost_estimate=cost(0, 0),
        name="total",
    )(*parts, *after)


def swap(value, axis, size, step):
    return lax.ppermute(value, axis, [(i, i ^ step) for i in range(size)])


def shards(adj_tiles, tile_counts, tile_cols, features, weight, upstream):
    n_row, n_col = lax.axis_size("row"), lax.axis_size("col")
    assert n_row & (n_row - 1) == 0 and n_col & (n_col - 1) == 0 and n_row > 1
    adj, counts, cols = adj_tiles[0, 0], tile_counts[0, 0], tile_cols[0, 0]
    rows, depth = upstream.shape[0], features.shape[0]
    col_tiles = depth * n_row // adj.shape[1]
    chips = n_row // 2
    where = jnp.stack([lax.axis_index("row"), lax.axis_index("col")]).astype(jnp.int32)
    steps = [*range(n_col - 1, 0, -1), 0]

    blocks = dense_rows(where, steps, counts, cols, adj, rows, col_tiles)
    dense = dict(zip(steps, blocks))

    away = gate([swap(features, "row", n_row, 2 * s) for s in range(chips - 1, 0, -1)], blocks)
    even = [features, *away[::-1]]
    odd = [swap(shard, "row", n_row, 1) for shard in even]
    parts = [shard for pair in zip(even, odd) for shard in pair]

    half = forward(where, blocks[0], even, 0, 2, [], jnp.float32)
    shares = [forward(where, blocks[0], odd, 1, 2, [half], jnp.bfloat16)]
    shares += [forward(where, block, parts, 0, 1, [], jnp.bfloat16) for block in blocks[1:-1]]
    came = [swap(share, "col", n_col, s) for s, share in zip(steps, shares)]
    mine = forward(where, blocks[-1], parts, 0, 1, [], jnp.float32)
    scale = 1.0 / math.sqrt(rows * n_row * n_col)
    hidden, piece, part = middle([mine, *came], weight, upstream, scale)

    pieces = {s: swap(piece, "col", n_col, s) for s in steps[:-1]}
    pieces[0] = piece
    cores = [[i for i in range(n_row) if i % 2 == core] for core in range(2)]
    part = (part + swap(part, "row", n_row, 1)).astype(jnp.bfloat16)
    gathered = lax.all_gather(part, "row", axis_index_groups=cores, tiled=True)
    part = total([gathered], part.shape[0], jnp.bfloat16)

    soon, late = [0, 1], steps[:-2]
    early = backward(
        where, [dense[s] for s in soon], [pieces[s] for s in soon], 0, n_row, n_row, depth, None, jnp.float32
    )
    last = functools.partial(backward, where, [dense[s] for s in late], [pieces[s] for s in late])
    sent = last(0, chips, n_row, depth, early, jnp.bfloat16, [part])
    kept = last(chips, chips, n_row, depth, early, jnp.float32)
    came = swap(sent, "row", n_row, 1)
    summed = [(kept[s] + came[s].astype(jnp.float32)).astype(jnp.bfloat16) for s in range(1, chips)]
    parts = [swap(summed[s - 1], "row", n_row, 2 * s) for s in range(chips - 1, 0, -1)]

    feature_grad = finish(kept, came, parts)
    for s in range(n_col.bit_length() - 2):
        part = total([part, swap(part, "col", n_col, 1 << s)], part.shape[0], jnp.bfloat16, [kept])
    came = swap(part, "col", n_col, n_col // 2)
    done = pltpu.with_memory_space_constraint(feature_grad, pltpu.HBM)
    weight_grad = total([part, came], part.shape[0], jnp.float32, [done])
    return hidden, weight_grad, feature_grad


def solution(mesh):
    placed = (
        P("row", "col", None, None, None),
        P("row", "col", None),
        P("row", "col", None),
        P(("col", "row"), None),
        P(),
        P(("row", "col"), None),
    )
    return jax.shard_map(
        shards,
        mesh=mesh,
        in_specs=placed,
        out_specs=(P(("row", "col"), None), P(), P(("col", "row"), None)),
        check_vma=False,
    )
```

```python
import functools
import math

import jax
import jax.numpy as jnp
from jax import lax
from jax.experimental import pallas as pl
from jax.experimental.pallas import tpu as pltpu
from jax.sharding import PartitionSpec as P


MIB = 1024 * 1024
SCALARS = pl.BlockSpec(memory_space=pltpu.SMEM)
WHOLE = pl.BlockSpec(memory_space=pltpu.VMEM)
UNREAD = pl.BlockSpec(memory_space=pl.ANY)


def params(mib):
    return pltpu.CompilerParams(vmem_limit_bytes=mib * MIB)


def cost(flops, moved, exps=0):
    return pl.CostEstimate(flops=flops, bytes_accessed=moved, transcendentals=exps)


def near(value):
    return pltpu.with_memory_space_constraint(value, pltpu.VMEM)


def dense_kernel(where, counts, cols, adj_ref, *refs, steps, window):
    outs, (held, total, sems) = refs[: len(steps)], refs[len(steps) :]
    slots, tile, _ = adj_ref.shape
    per = outs[0].shape[0] // tile
    width = outs[0].shape[1]

    plans = []
    for i, step in enumerate(steps):
        first = (where[1] ^ step) * per
        start = lax.fori_loop(0, first, lambda t, s: s + counts[t], jnp.int32(0))
        for u in range(per):
            count = counts[first + u]
            base = jnp.minimum(start, slots - window)
            fetch = pltpu.make_async_copy(
                adj_ref.at[pl.ds(base, window)], held.at[i * per + u], sems.at[i * per + u]
            )
            fetch.start()
            plans.append((start, start - base, count, fetch))
            start = start + count

    for i, out_ref in enumerate(outs):
        out_ref[...] = jnp.zeros_like(out_ref)
    for n, (start, shift, count, fetch) in enumerate(plans):
        out_ref = outs[n // per]
        rows = pl.ds((n % per) * tile, tile)
        fetch.wait()

        def place(j):
            c = cols[start + j]
            out_ref[rows, pl.ds(pl.multiple_of(c * tile, tile), tile)] = held[n, shift + j]
            return lax.shift_left(jnp.int32(1), c)

        def four(i, state):
            seen, twice = state
            for v in range(4):
                bit = place(4 * i + v)
                twice = twice | (seen & bit)
                seen = seen | bit
            return seen, twice

        def one(j, state):
            seen, twice = state
            bit = place(j)
            return seen | bit, twice | (seen & bit)

        groups = lax.div(count, 4)
        state = lax.fori_loop(0, groups, four, (jnp.int32(0), jnp.int32(0)))
        seen, twice = lax.fori_loop(4 * groups, count, one, state)
        repeated = (twice != 0) if width // tile <= 32 else (count > 0)

        @pl.when(repeated)
        def _():
            total[...] = jnp.zeros_like(total)

            def add(j, carry):
                here = pl.ds(pl.multiple_of(cols[start + j] * tile, tile), tile)
                total[:, here] += held[n, shift + j].astype(jnp.float32)
                return carry

            lax.fori_loop(0, count, add, 0)
            out_ref[rows, :] = total[...].astype(out_ref.dtype)


def dense_rows(where, steps, counts, cols, adj, rows, col_tiles):
    slots, tile, _ = adj.shape
    window = min(col_tiles, slots)
    width = col_tiles * tile
    tiles = rows // tile * len(steps)
    return pl.pallas_call(
        functools.partial(dense_kernel, steps=steps, window=window),
        out_shape=[pltpu.VMEM((rows, width), adj.dtype) for _ in steps],
        in_specs=[SCALARS, SCALARS, SCALARS, pl.BlockSpec(memory_space=pltpu.HBM)],
        out_specs=[WHOLE] * len(steps),
        scratch_shapes=[
            pltpu.VMEM((tiles, window, tile, tile), adj.dtype),
            pltpu.VMEM((tile, width), jnp.float32),
            pltpu.SemaphoreType.DMA((tiles,)),
        ],
        compiler_params=params(26),
        cost_estimate=cost(0, 5 * len(steps) * rows * width),
        name="dense_rows",
    )(where, *[pltpu.with_memory_space_constraint(x, pltpu.HBM) for x in (counts, cols, adj)])


def forward_kernel(where, a_ref, *refs, first, step):
    shards, out_ref, before = refs[:-1], refs[-1], None
    if first:
        shards, before = shards[:-1], shards[-1]
    depth = shards[0].shape[0]
    value = None if before is None else before[...]
    for k, shard in enumerate(shards):
        cols = pl.ds(pl.multiple_of((where[0] ^ (first + step * k)) * depth, depth), depth)
        part = jnp.dot(a_ref[:, cols], shard[...], preferred_element_type=jnp.float32)
        value = part if value is None else value + part
    out_ref[...] = value.astype(out_ref.dtype)


def forward(where, dense, shards, first, step, before, kind):
    rows, width = dense.shape[0], shards[0].shape[1]
    operands = [near(x) for x in [dense, *shards, *before]]
    flops = 2 * rows * dense.shape[1] * width
    return pl.pallas_call(
        functools.partial(forward_kernel, first=first, step=step),
        out_shape=pltpu.VMEM((rows, width), kind),
        in_specs=[SCALARS] + [WHOLE] * len(operands),
        out_specs=WHOLE,
        compiler_params=params(10),
        cost_estimate=cost(flops, dense.size * 2),
        name="forward_rows",
    )(where, *operands)


def middle_kernel(*refs, scale, came):
    parts = refs[: came + 1]
    weight_ref, up_ref, hidden_ref, grad_ref, wgrad_ref = refs[came + 1 :]
    agg = parts[0][...].astype(jnp.float32)
    for part in parts[1:]:
        agg = agg + part[...].astype(jnp.float32)
    agg = agg.astype(jnp.bfloat16)
    weight = weight_ref[...]
    pre = jnp.dot(agg, weight, preferred_element_type=jnp.float32)
    sig = jax.nn.sigmoid(pre)
    hidden_ref[...] = (pre * sig).astype(jnp.bfloat16)
    pre_grad = (up_ref[...].astype(jnp.float32) * sig * (1.0 + pre * (1.0 - sig))).astype(jnp.bfloat16)
    grad_ref[...] = lax.dot_general(
        weight, pre_grad, (((1,), (1,)), ((), ())), preferred_element_type=jnp.float32
    ).astype(jnp.bfloat16)
    wgrad_ref[...] = scale * lax.dot_general(
        agg, pre_grad, (((0,), (0,)), ((), ())), preferred_element_type=jnp.float32
    )


def middle(parts, weight, upstream, scale):
    rows, width = upstream.shape
    return pl.pallas_call(
        functools.partial(middle_kernel, scale=scale, came=len(parts) - 1),
        out_shape=(
            jax.ShapeDtypeStruct((rows, width), jnp.bfloat16),
            jax.ShapeDtypeStruct((width, rows), jnp.bfloat16),
            jax.ShapeDtypeStruct((width, width), jnp.float32),
        ),
        compiler_params=params(16),
        cost_estimate=cost(6 * rows * width * width, 10 * rows * width, rows * width),
        name="middle",
    )(*parts, weight, upstream)


def backward_kernel(where, *refs, count, steps, before):
    dense, pieces = refs[:count], refs[count : 2 * count]
    out_ref = refs[-1]
    columns, _, depth = out_ref.shape

    def one(j, carry):
        step = jnp.int32(steps[0])
        for i in range(1, len(steps)):
            step = jnp.where(j == i, steps[i], step)
        cols = pl.ds(pl.multiple_of((where[0] ^ step) * depth, depth), depth)
        value = refs[2 * count][step] if before else None
        for a_ref, piece in zip(dense, pieces):
            part = jnp.dot(piece[...], a_ref[:, cols], preferred_element_type=jnp.float32)
            value = part if value is None else value + part
        out_ref[j] = value.astype(out_ref.dtype)
        return carry

    lax.fori_loop(0, columns, one, 0)


def backward(where, dense, pieces, steps, depth, before, kind, after=()):
    count = len(pieces)
    width, _ = pieces[0].shape
    operands = [near(x) for x in [*dense, *pieces] + ([] if before is None else [before])]
    return pl.pallas_call(
        functools.partial(backward_kernel, count=count, steps=steps, before=before is not None),
        out_shape=pltpu.VMEM((len(steps), width, depth), kind),
        in_specs=[SCALARS] + [WHOLE] * len(operands) + [UNREAD] * len(after),
        out_specs=WHOLE,
        compiler_params=params(10),
        cost_estimate=cost(0, 0),
        name="backward_cols",
    )(where, *operands, *after)


def finish_kernel(*refs):
    parts, out_ref = refs[:-1], refs[-1]
    value = parts[0][0].astype(jnp.float32) + parts[1][0].astype(jnp.float32)
    for part in parts[2:]:
        value = value + part[...].astype(jnp.float32)
    out_ref[...] = value.T.astype(out_ref.dtype)


def finish(kept, came, parts):
    _, width, rows = kept.shape
    own = pl.BlockSpec((1, width, rows), lambda i: (0, 0, 0))
    part = pl.BlockSpec((width, rows), lambda i: (0, 0))
    return pl.pallas_call(
        finish_kernel,
        out_shape=jax.ShapeDtypeStruct((rows, width), jnp.bfloat16),
        grid=(1,),
        in_specs=[own, own] + [part] * len(parts),
        out_specs=pl.BlockSpec((rows, width), lambda i: (0, 0)),
        compiler_params=params(12),
        cost_estimate=cost(len(parts) * rows * width, 4 * len(parts) * rows * width),
        name="finish",
    )(kept, came, *parts)


def gate(values, after):
    count = len(values)
    return pl.pallas_call(
        lambda *refs: None,
        out_shape=[pltpu.VMEM(x.shape, x.dtype) for x in values],
        in_specs=[WHOLE] * count + [UNREAD] * len(after),
        out_specs=[WHOLE] * count,
        input_output_aliases={i: i for i in range(count)},
        compiler_params=params(4),
        cost_estimate=cost(0, 0),
        name="gate",
    )(*map(near, values), *after)


def total_kernel(*refs, count):
    parts, out_ref = refs[:count], refs[-1]
    rows = out_ref.shape[0]
    value = None
    for part in parts:
        for i in range(part.shape[0] // rows):
            term = part[pl.ds(i * rows, rows), :].astype(jnp.float32)
            value = term if value is None else value + term
    out_ref[...] = value.astype(out_ref.dtype)


def total(parts, rows, kind, after=()):
    return pl.pallas_call(
        functools.partial(total_kernel, count=len(parts)),
        out_shape=jax.ShapeDtypeStruct((rows, parts[0].shape[1]), kind),
        in_specs=[WHOLE] * len(parts) + [UNREAD] * len(after),
        compiler_params=params(10),
        cost_estimate=cost(0, 0),
        name="total",
    )(*parts, *after)


def swap(value, axis, size, step):
    return lax.ppermute(value, axis, [(i, i ^ step) for i in range(size)])


def shards(adj_tiles, tile_counts, tile_cols, features, weight, upstream):
    n_row, n_col = lax.axis_size("row"), lax.axis_size("col")
    assert n_row & (n_row - 1) == 0 and n_col & (n_col - 1) == 0 and n_row > 1
    adj, counts, cols = adj_tiles[0, 0], tile_counts[0, 0], tile_cols[0, 0]
    rows, depth = upstream.shape[0], features.shape[0]
    col_tiles = depth * n_row // adj.shape[1]
    chips = n_row // 2
    where = jnp.stack([lax.axis_index("row"), lax.axis_index("col")]).astype(jnp.int32)
    steps = [*range(n_col - 1, 0, -1), 0]

    blocks = dense_rows(where, steps, counts, cols, adj, rows, col_tiles)
    dense = dict(zip(steps, blocks))

    away = gate([swap(features, "row", n_row, 2 * s) for s in range(chips - 1, 0, -1)], blocks)
    even = [features, *away[::-1]]
    odd = [swap(shard, "row", n_row, 1) for shard in even]
    parts = [shard for pair in zip(even, odd) for shard in pair]

    half = forward(where, blocks[0], even, 0, 2, [], jnp.float32)
    shares = [forward(where, blocks[0], odd, 1, 2, [half], jnp.bfloat16)]
    shares += [forward(where, block, parts, 0, 1, [], jnp.bfloat16) for block in blocks[1:-1]]
    came = [swap(share, "col", n_col, s) for s, share in zip(steps, shares)]
    mine = forward(where, blocks[-1], parts, 0, 1, [], jnp.float32)
    scale = 1.0 / math.sqrt(rows * n_row * n_col)
    hidden, piece, part = middle([mine, *came], weight, upstream, scale)

    pieces = {s: swap(piece, "col", n_col, s) for s in steps[:-1]}
    pieces[0] = piece
    cores = [[i for i in range(n_row) if i % 2 == core] for core in range(2)]
    part = (part + swap(part, "row", n_row, 1)).astype(jnp.bfloat16)
    gathered = lax.all_gather(part, "row", axis_index_groups=cores, tiled=True)
    part = total([gathered], part.shape[0], jnp.bfloat16)

    every = list(range(n_row))
    sums = None
    for group in [[0, 1], *[[s] for s in range(2, n_col - 1)]]:
        sums = backward(where, [dense[s] for s in group], [pieces[s] for s in group], every, depth, sums, jnp.float32)
    last = functools.partial(backward, where, [dense[n_col - 1]], [pieces[n_col - 1]])
    sent = last(every[1::2], depth, sums, jnp.bfloat16, [part])
    kept = last(every[::2], depth, sums, jnp.float32)
    came = swap(sent, "row", n_row, 1)
    summed = [(kept[c] + came[c].astype(jnp.float32)).astype(jnp.bfloat16) for c in range(1, chips)]
    parts = [swap(summed[c - 1], "row", n_row, 2 * c) for c in range(chips - 1, 0, -1)]

    feature_grad = finish(kept, came, parts)
    for s in range(n_col.bit_length() - 2):
        part = total([part, swap(part, "col", n_col, 1 << s)], part.shape[0], jnp.bfloat16, [kept])
    came = swap(part, "col", n_col, n_col // 2)
    done = pltpu.with_memory_space_constraint(feature_grad, pltpu.HBM)
    weight_grad = total([part, came], part.shape[0], jnp.float32, [done])
    return hidden, weight_grad, feature_grad


def solution(mesh):
    placed = (
        P("row", "col", None, None, None),
        P("row", "col", None),
        P("row", "col", None),
        P(("col", "row"), None),
        P(),
        P(("row", "col"), None),
    )
    return jax.shard_map(
        shards,
        mesh=mesh,
        in_specs=placed,
        out_specs=(P(("row", "col"), None), P(), P(("col", "row"), None)),
        check_vma=False,
    )
```

```python
import functools
import math

import jax
import jax.numpy as jnp
from jax import lax
from jax.experimental import pallas as pl
from jax.experimental.pallas import tpu as pltpu
from jax.sharding import PartitionSpec as P


MIB = 1024 * 1024
SCALARS = pl.BlockSpec(memory_space=pltpu.SMEM)
WHOLE = pl.BlockSpec(memory_space=pltpu.VMEM)
UNREAD = pl.BlockSpec(memory_space=pl.ANY)


def params(mib):
    return pltpu.CompilerParams(vmem_limit_bytes=mib * MIB)


def cost(flops, moved, exps=0):
    return pl.CostEstimate(flops=flops, bytes_accessed=moved, transcendentals=exps)


def near(value):
    return pltpu.with_memory_space_constraint(value, pltpu.VMEM)


def dense_kernel(where, counts, cols, adj_ref, features_ref, *refs, steps, window):
    outs, (copied_ref, held, total, sems) = refs[: len(steps)], refs[len(steps) :]
    slots, tile, _ = adj_ref.shape
    per = outs[0].shape[0] // tile
    width = outs[0].shape[1]

    plans = []
    for i, step in enumerate(steps):
        first = (where[1] ^ step) * per
        start = lax.fori_loop(0, first, lambda t, s: s + counts[t], jnp.int32(0))
        for u in range(per):
            count = counts[first + u]
            base = jnp.minimum(start, slots - window)
            fetch = pltpu.make_async_copy(
                adj_ref.at[pl.ds(base, window)], held.at[i * per + u], sems.at[i * per + u]
            )
            fetch.start()
            plans.append((start, start - base, count, fetch))
            start = start + count
    copied = pltpu.make_async_copy(features_ref, copied_ref, sems.at[len(plans)])
    copied.start()

    for i, out_ref in enumerate(outs):
        out_ref[...] = jnp.zeros_like(out_ref)
    for n, (start, shift, count, fetch) in enumerate(plans):
        out_ref = outs[n // per]
        rows = pl.ds((n % per) * tile, tile)
        fetch.wait()

        def place(j):
            c = cols[start + j]
            out_ref[rows, pl.ds(pl.multiple_of(c * tile, tile), tile)] = held[n, shift + j]
            return lax.shift_left(jnp.int32(1), c)

        def four(i, state):
            seen, twice = state
            for v in range(4):
                bit = place(4 * i + v)
                twice = twice | (seen & bit)
                seen = seen | bit
            return seen, twice

        def one(j, state):
            seen, twice = state
            bit = place(j)
            return seen | bit, twice | (seen & bit)

        groups = lax.div(count, 4)
        state = lax.fori_loop(0, groups, four, (jnp.int32(0), jnp.int32(0)))
        seen, twice = lax.fori_loop(4 * groups, count, one, state)
        repeated = (twice != 0) if width // tile <= 32 else (count > 0)

        @pl.when(repeated)
        def _():
            total[...] = jnp.zeros_like(total)

            def add(j, carry):
                here = pl.ds(pl.multiple_of(cols[start + j] * tile, tile), tile)
                total[:, here] += held[n, shift + j].astype(jnp.float32)
                return carry

            lax.fori_loop(0, count, add, 0)
            out_ref[rows, :] = total[...].astype(out_ref.dtype)

    copied.wait()


def dense_rows(where, steps, counts, cols, adj, features, rows, col_tiles):
    slots, tile, _ = adj.shape
    window = min(col_tiles, slots)
    width = col_tiles * tile
    tiles = rows // tile * len(steps)
    return pl.pallas_call(
        functools.partial(dense_kernel, steps=steps, window=window),
        out_shape=[pltpu.VMEM((rows, width), adj.dtype) for _ in steps]
        + [pltpu.VMEM(features.shape, features.dtype)],
        in_specs=[SCALARS] * 3 + [pl.BlockSpec(memory_space=pltpu.HBM)] * 2,
        out_specs=[WHOLE] * (len(steps) + 1),
        scratch_shapes=[
            pltpu.VMEM((tiles, window, tile, tile), adj.dtype),
            pltpu.VMEM((tile, width), jnp.float32),
            pltpu.SemaphoreType.DMA((tiles + 1,)),
        ],
        compiler_params=params(26),
        cost_estimate=cost(0, 5 * len(steps) * rows * width),
        name="dense_rows",
    )(where, *[pltpu.with_memory_space_constraint(x, pltpu.HBM) for x in (counts, cols, adj, features)])


def forward_kernel(where, a_ref, *refs, first, step):
    shards, out_ref, before = refs[:-1], refs[-1], None
    if first:
        shards, before = shards[:-1], shards[-1]
    depth = shards[0].shape[0]
    value = None if before is None else before[...]
    for k, shard in enumerate(shards):
        cols = pl.ds(pl.multiple_of((where[0] ^ (first + step * k)) * depth, depth), depth)
        part = jnp.dot(a_ref[:, cols], shard[...], preferred_element_type=jnp.float32)
        value = part if value is None else value + part
    out_ref[...] = value.astype(out_ref.dtype)


def forward(where, dense, shards, first, step, before, kind):
    rows, width = dense.shape[0], shards[0].shape[1]
    operands = [near(x) for x in [dense, *shards, *before]]
    flops = 2 * rows * dense.shape[1] * width
    return pl.pallas_call(
        functools.partial(forward_kernel, first=first, step=step),
        out_shape=pltpu.VMEM((rows, width), kind),
        in_specs=[SCALARS] + [WHOLE] * len(operands),
        out_specs=WHOLE,
        compiler_params=params(10),
        cost_estimate=cost(flops, dense.size * 2),
        name="forward_rows",
    )(where, *operands)


def middle_kernel(*refs, scale, came):
    parts = refs[: came + 1]
    weight_ref, up_ref, hidden_ref, grad_ref, wgrad_ref = refs[came + 1 :]
    agg = parts[0][...].astype(jnp.float32)
    for part in parts[1:]:
        agg = agg + part[...].astype(jnp.float32)
    agg = agg.astype(jnp.bfloat16)
    weight = weight_ref[...]
    pre = jnp.dot(agg, weight, preferred_element_type=jnp.float32)
    sig = jax.nn.sigmoid(pre)
    hidden_ref[...] = (pre * sig).astype(jnp.bfloat16)
    pre_grad = (up_ref[...].astype(jnp.float32) * sig * (1.0 + pre * (1.0 - sig))).astype(jnp.bfloat16)
    grad_ref[...] = lax.dot_general(
        weight, pre_grad, (((1,), (1,)), ((), ())), preferred_element_type=jnp.float32
    ).astype(jnp.bfloat16)
    wgrad_ref[...] = scale * lax.dot_general(
        agg, pre_grad, (((0,), (0,)), ((), ())), preferred_element_type=jnp.float32
    )


def middle(parts, weight, upstream, scale):
    rows, width = upstream.shape
    return pl.pallas_call(
        functools.partial(middle_kernel, scale=scale, came=len(parts) - 1),
        out_shape=(
            jax.ShapeDtypeStruct((rows, width), jnp.bfloat16),
            jax.ShapeDtypeStruct((width, rows), jnp.bfloat16),
            jax.ShapeDtypeStruct((width, width), jnp.float32),
        ),
        compiler_params=params(16),
        cost_estimate=cost(6 * rows * width * width, 10 * rows * width, rows * width),
        name="middle",
    )(*parts, weight, upstream)


def backward_kernel(where, *refs, count, steps, before):
    dense, pieces = refs[:count], refs[count : 2 * count]
    out_ref = refs[-1]
    columns, _, depth = out_ref.shape

    def one(j, carry):
        step = jnp.int32(steps[0])
        for i in range(1, len(steps)):
            step = jnp.where(j == i, steps[i], step)
        cols = pl.ds(pl.multiple_of((where[0] ^ step) * depth, depth), depth)
        value = refs[2 * count][step] if before else None
        for a_ref, piece in zip(dense, pieces):
            part = jnp.dot(piece[...], a_ref[:, cols], preferred_element_type=jnp.float32)
            value = part if value is None else value + part
        out_ref[j] = value.astype(out_ref.dtype)
        return carry

    lax.fori_loop(0, columns, one, 0)


def backward(where, dense, pieces, steps, depth, before, kind, after=()):
    count = len(pieces)
    width, _ = pieces[0].shape
    operands = [near(x) for x in [*dense, *pieces] + ([] if before is None else [before])]
    return pl.pallas_call(
        functools.partial(backward_kernel, count=count, steps=steps, before=before is not None),
        out_shape=pltpu.VMEM((len(steps), width, depth), kind),
        in_specs=[SCALARS] + [WHOLE] * len(operands) + [UNREAD] * len(after),
        out_specs=WHOLE,
        compiler_params=params(10),
        cost_estimate=cost(0, 0),
        name="backward_cols",
    )(where, *operands, *after)


def finish_kernel(*refs):
    parts, out_ref = refs[:-1], refs[-1]
    value = parts[0][0].astype(jnp.float32) + parts[1][0].astype(jnp.float32)
    for part in parts[2:]:
        value = value + part[...].astype(jnp.float32)
    out_ref[...] = value.T.astype(out_ref.dtype)


def finish(kept, came, parts):
    _, width, rows = kept.shape
    own = pl.BlockSpec((1, width, rows), lambda i: (0, 0, 0))
    part = pl.BlockSpec((width, rows), lambda i: (0, 0))
    return pl.pallas_call(
        finish_kernel,
        out_shape=jax.ShapeDtypeStruct((rows, width), jnp.bfloat16),
        grid=(1,),
        in_specs=[own, own] + [part] * len(parts),
        out_specs=pl.BlockSpec((rows, width), lambda i: (0, 0)),
        compiler_params=params(12),
        cost_estimate=cost(len(parts) * rows * width, 4 * len(parts) * rows * width),
        name="finish",
    )(kept, came, *parts)


def gate(values, after):
    count = len(values)
    return pl.pallas_call(
        lambda *refs: None,
        out_shape=[pltpu.VMEM(x.shape, x.dtype) for x in values],
        in_specs=[WHOLE] * count + [UNREAD] * len(after),
        out_specs=[WHOLE] * count,
        input_output_aliases={i: i for i in range(count)},
        compiler_params=params(4),
        cost_estimate=cost(0, 0),
        name="gate",
    )(*map(near, values), *after)


def total_kernel(*refs, count):
    parts, out_ref = refs[:count], refs[-1]
    rows = out_ref.shape[0]
    value = None
    for part in parts:
        for i in range(part.shape[0] // rows):
            term = part[pl.ds(i * rows, rows), :].astype(jnp.float32)
            value = term if value is None else value + term
    out_ref[...] = value.astype(out_ref.dtype)


def total(parts, rows, kind, after=()):
    return pl.pallas_call(
        functools.partial(total_kernel, count=len(parts)),
        out_shape=jax.ShapeDtypeStruct((rows, parts[0].shape[1]), kind),
        in_specs=[WHOLE] * len(parts) + [UNREAD] * len(after),
        compiler_params=params(10),
        cost_estimate=cost(0, 0),
        name="total",
    )(*parts, *after)


def swap(value, axis, size, step):
    return lax.ppermute(value, axis, [(i, i ^ step) for i in range(size)])


def shards(adj_tiles, tile_counts, tile_cols, features, weight, upstream):
    n_row, n_col = lax.axis_size("row"), lax.axis_size("col")
    assert n_row & (n_row - 1) == 0 and n_col & (n_col - 1) == 0 and n_row > 1
    adj, counts, cols = adj_tiles[0, 0], tile_counts[0, 0], tile_cols[0, 0]
    rows, depth = upstream.shape[0], features.shape[0]
    col_tiles = depth * n_row // adj.shape[1]
    chips = n_row // 2
    where = jnp.stack([lax.axis_index("row"), lax.axis_index("col")]).astype(jnp.int32)
    steps = [*range(n_col - 1, 0, -1), 0]

    *blocks, near_features = dense_rows(where, steps, counts, cols, adj, features, rows, col_tiles)
    dense = dict(zip(steps, blocks))

    away = gate([swap(features, "row", n_row, 2 * s) for s in range(chips - 1, 0, -1)], blocks)
    odd = [swap(shard, "row", n_row, 1) for shard in [features, *away[::-1]]]
    even = [near_features, *away[::-1]]
    parts = [shard for pair in zip(even, odd) for shard in pair]

    half = forward(where, blocks[2], even, 0, 2, [], jnp.float32)
    shares = [forward(where, block, parts, 0, 1, [], jnp.bfloat16) for block in blocks[:-1]]
    shares[2] = forward(where, blocks[2], odd, 1, 2, [half], jnp.bfloat16)
    came = [swap(share, "col", n_col, s) for s, share in zip(steps, shares)]
    mine = forward(where, blocks[-1], parts, 0, 1, [], jnp.float32)
    scale = 1.0 / math.sqrt(rows * n_row * n_col)
    hidden, piece, part = middle([mine, *came], weight, upstream, scale)

    pieces = {s: swap(piece, "col", n_col, s) for s in steps[:-1]}
    pieces[0] = piece
    cores = [[i for i in range(n_row) if i % 2 == core] for core in range(2)]
    part = (part + swap(part, "row", n_row, 1)).astype(jnp.bfloat16)
    gathered = lax.all_gather(part, "row", axis_index_groups=cores, tiled=True)
    part = total([gathered], part.shape[0], jnp.bfloat16)

    every = list(range(n_row))
    sums, latest = None, n_col // 2
    for group in [[0, 1], *[[s] for s in range(n_col - 1, 1, -1) if s != latest]]:
        sums = backward(where, [dense[s] for s in group], [pieces[s] for s in group], every, depth, sums, jnp.float32)
    last = functools.partial(backward, where, [dense[latest]], [pieces[latest]])
    sent = last(every[1::2], depth, sums, jnp.bfloat16, [part])
    kept = last(every[::2], depth, sums, jnp.float32)
    came = swap(sent, "row", n_row, 1)
    summed = [(kept[c] + came[c].astype(jnp.float32)).astype(jnp.bfloat16) for c in range(1, chips)]
    parts = [swap(summed[c - 1], "row", n_row, 2 * c) for c in range(chips - 1, 0, -1)]

    feature_grad = finish(kept, came, parts)
    for s in range(n_col.bit_length() - 2):
        part = total([part, swap(part, "col", n_col, 1 << s)], part.shape[0], jnp.bfloat16, [kept])
    came = swap(part, "col", n_col, n_col // 2)
    done = pltpu.with_memory_space_constraint(feature_grad, pltpu.HBM)
    weight_grad = total([part, came], part.shape[0], jnp.float32, [done])
    return hidden, weight_grad, feature_grad


def solution(mesh):
    placed = (
        P("row", "col", None, None, None),
        P("row", "col", None),
        P("row", "col", None),
        P(("col", "row"), None),
        P(),
        P(("row", "col"), None),
    )
    return jax.shard_map(
        shards,
        mesh=mesh,
        in_specs=placed,
        out_specs=(P(("row", "col"), None), P(), P(("col", "row"), None)),
        check_vma=False,
    )
```

```python
import functools
import math

import jax
import jax.numpy as jnp
from jax import lax
from jax.experimental import pallas as pl
from jax.experimental.pallas import tpu as pltpu
from jax.sharding import PartitionSpec as P


MIB = 1024 * 1024
SCALARS = pl.BlockSpec(memory_space=pltpu.SMEM)
WHOLE = pl.BlockSpec(memory_space=pltpu.VMEM)
UNREAD = pl.BlockSpec(memory_space=pl.ANY)


def params(mib):
    return pltpu.CompilerParams(vmem_limit_bytes=mib * MIB)


def cost(flops, moved, exps=0):
    return pl.CostEstimate(flops=flops, bytes_accessed=moved, transcendentals=exps)


def near(value):
    return pltpu.with_memory_space_constraint(value, pltpu.VMEM)


def dense_kernel(where, counts, cols, adj_ref, features_ref, *refs, steps, window):
    outs, (copied_ref, held, total, sems) = refs[: len(steps)], refs[len(steps) :]
    slots, tile, _ = adj_ref.shape
    per = outs[0].shape[0] // tile
    width = outs[0].shape[1]

    plans = []
    for i, step in enumerate(steps):
        first = (where[1] ^ step) * per
        start = lax.fori_loop(0, first, lambda t, s: s + counts[t], jnp.int32(0))
        for u in range(per):
            count = counts[first + u]
            base = jnp.minimum(start, slots - window)
            fetch = pltpu.make_async_copy(
                adj_ref.at[pl.ds(base, window)], held.at[i * per + u], sems.at[i * per + u]
            )
            fetch.start()
            plans.append((start, start - base, count, fetch))
            start = start + count
    copied = pltpu.make_async_copy(features_ref, copied_ref, sems.at[len(plans)])
    copied.start()

    for i, out_ref in enumerate(outs):
        out_ref[...] = jnp.zeros_like(out_ref)
    for n, (start, shift, count, fetch) in enumerate(plans):
        out_ref = outs[n // per]
        rows = pl.ds((n % per) * tile, tile)
        fetch.wait()

        def place(j):
            c = cols[start + j]
            out_ref[rows, pl.ds(pl.multiple_of(c * tile, tile), tile)] = held[n, shift + j]
            return lax.shift_left(jnp.int32(1), c)

        def four(i, state):
            seen, twice = state
            for v in range(4):
                bit = place(4 * i + v)
                twice = twice | (seen & bit)
                seen = seen | bit
            return seen, twice

        def one(j, state):
            seen, twice = state
            bit = place(j)
            return seen | bit, twice | (seen & bit)

        groups = lax.div(count, 4)
        state = lax.fori_loop(0, groups, four, (jnp.int32(0), jnp.int32(0)))
        seen, twice = lax.fori_loop(4 * groups, count, one, state)
        repeated = (twice != 0) if width // tile <= 32 else (count > 0)

        @pl.when(repeated)
        def _():
            total[...] = jnp.zeros_like(total)

            def add(j, carry):
                here = pl.ds(pl.multiple_of(cols[start + j] * tile, tile), tile)
                total[:, here] += held[n, shift + j].astype(jnp.float32)
                return carry

            lax.fori_loop(0, count, add, 0)
            out_ref[rows, :] = total[...].astype(out_ref.dtype)

    copied.wait()


def dense_rows(where, steps, counts, cols, adj, features, rows, col_tiles):
    slots, tile, _ = adj.shape
    window = min(col_tiles, slots)
    width = col_tiles * tile
    tiles = rows // tile * len(steps)
    return pl.pallas_call(
        functools.partial(dense_kernel, steps=steps, window=window),
        out_shape=[pltpu.VMEM((rows, width), adj.dtype) for _ in steps]
        + [pltpu.VMEM(features.shape, features.dtype)],
        in_specs=[SCALARS] * 3 + [pl.BlockSpec(memory_space=pltpu.HBM)] * 2,
        out_specs=[WHOLE] * (len(steps) + 1),
        scratch_shapes=[
            pltpu.VMEM((tiles, window, tile, tile), adj.dtype),
            pltpu.VMEM((tile, width), jnp.float32),
            pltpu.SemaphoreType.DMA((tiles + 1,)),
        ],
        compiler_params=params(26),
        cost_estimate=cost(0, 5 * len(steps) * rows * width),
        name="dense_rows",
    )(where, *[pltpu.with_memory_space_constraint(x, pltpu.HBM) for x in (counts, cols, adj, features)])


def forward_kernel(where, a_ref, *refs, first, step):
    shards, out_ref, before = refs[:-1], refs[-1], None
    if first:
        shards, before = shards[:-1], shards[-1]
    depth = shards[0].shape[0]
    value = None if before is None else before[...]
    for k, shard in enumerate(shards):
        cols = pl.ds(pl.multiple_of((where[0] ^ (first + step * k)) * depth, depth), depth)
        part = jnp.dot(a_ref[:, cols], shard[...], preferred_element_type=jnp.float32)
        value = part if value is None else value + part
    out_ref[...] = value.astype(out_ref.dtype)


def forward(where, dense, shards, first, step, before, kind):
    rows, width = dense.shape[0], shards[0].shape[1]
    operands = [near(x) for x in [dense, *shards, *before]]
    flops = 2 * rows * dense.shape[1] * width
    return pl.pallas_call(
        functools.partial(forward_kernel, first=first, step=step),
        out_shape=pltpu.VMEM((rows, width), kind),
        in_specs=[SCALARS] + [WHOLE] * len(operands),
        out_specs=WHOLE,
        compiler_params=params(10),
        cost_estimate=cost(flops, dense.size * 2),
        name="forward_rows",
    )(where, *operands)


def middle_kernel(*refs, scale, came):
    parts = refs[: came + 1]
    weight_ref, up_ref, hidden_ref, grad_ref, wgrad_ref = refs[came + 1 :]
    agg = parts[0][...].astype(jnp.float32)
    for part in parts[1:]:
        agg = agg + part[...].astype(jnp.float32)
    agg = agg.astype(jnp.bfloat16)
    weight = weight_ref[...]
    pre = jnp.dot(agg, weight, preferred_element_type=jnp.float32)
    sig = jax.nn.sigmoid(pre)
    hidden_ref[...] = (pre * sig).astype(jnp.bfloat16)
    pre_grad = (up_ref[...].astype(jnp.float32) * sig * (1.0 + pre * (1.0 - sig))).astype(jnp.bfloat16)
    grad_ref[...] = lax.dot_general(
        weight, pre_grad, (((1,), (1,)), ((), ())), preferred_element_type=jnp.float32
    ).astype(jnp.bfloat16)
    wgrad_ref[...] = scale * lax.dot_general(
        agg, pre_grad, (((0,), (0,)), ((), ())), preferred_element_type=jnp.float32
    )


def middle(parts, weight, upstream, scale):
    rows, width = upstream.shape
    return pl.pallas_call(
        functools.partial(middle_kernel, scale=scale, came=len(parts) - 1),
        out_shape=(
            jax.ShapeDtypeStruct((rows, width), jnp.bfloat16),
            jax.ShapeDtypeStruct((width, rows), jnp.bfloat16),
            jax.ShapeDtypeStruct((width, width), jnp.float32),
        ),
        compiler_params=params(16),
        cost_estimate=cost(6 * rows * width * width, 10 * rows * width, rows * width),
        name="middle",
    )(*parts, weight, upstream)


def backward_kernel(where, *refs, count, steps, before):
    dense, pieces = refs[:count], refs[count : 2 * count]
    out_ref = refs[-1]
    columns, _, depth = out_ref.shape

    def one(j, carry):
        step = jnp.int32(steps[0])
        for i in range(1, len(steps)):
            step = jnp.where(j == i, steps[i], step)
        cols = pl.ds(pl.multiple_of((where[0] ^ step) * depth, depth), depth)
        value = refs[2 * count][step] if before else None
        for a_ref, piece in zip(dense, pieces):
            part = jnp.dot(piece[...], a_ref[:, cols], preferred_element_type=jnp.float32)
            value = part if value is None else value + part
        out_ref[j] = value.astype(out_ref.dtype)
        return carry

    lax.fori_loop(0, columns, one, 0)


def backward(where, dense, pieces, steps, depth, before, kind, after=()):
    count = len(pieces)
    width, _ = pieces[0].shape
    operands = [near(x) for x in [*dense, *pieces] + ([] if before is None else [before])]
    return pl.pallas_call(
        functools.partial(backward_kernel, count=count, steps=steps, before=before is not None),
        out_shape=pltpu.VMEM((len(steps), width, depth), kind),
        in_specs=[SCALARS] + [WHOLE] * len(operands) + [UNREAD] * len(after),
        out_specs=WHOLE,
        compiler_params=params(10),
        cost_estimate=cost(0, 0),
        name="backward_cols",
    )(where, *operands, *after)


def finish_kernel(*refs):
    parts, out_ref = refs[:-1], refs[-1]
    value = parts[0][0].astype(jnp.float32) + parts[1][0].astype(jnp.float32)
    for part in parts[2:]:
        value = value + part[...].astype(jnp.float32)
    out_ref[...] = value.astype(out_ref.dtype).T


def finish(kept, came, parts):
    _, width, rows = kept.shape
    own = pl.BlockSpec((1, width, rows), lambda i: (0, 0, 0))
    part = pl.BlockSpec((width, rows), lambda i: (0, 0))
    return pl.pallas_call(
        finish_kernel,
        out_shape=jax.ShapeDtypeStruct((rows, width), jnp.bfloat16),
        grid=(1,),
        in_specs=[own, own] + [part] * len(parts),
        out_specs=pl.BlockSpec((rows, width), lambda i: (0, 0)),
        compiler_params=params(12),
        cost_estimate=cost(len(parts) * rows * width, 4 * len(parts) * rows * width),
        name="finish",
    )(kept, came, *parts)


def gate(values, after):
    count = len(values)
    return pl.pallas_call(
        lambda *refs: None,
        out_shape=[pltpu.VMEM(x.shape, x.dtype) for x in values],
        in_specs=[WHOLE] * count + [UNREAD] * len(after),
        out_specs=[WHOLE] * count,
        input_output_aliases={i: i for i in range(count)},
        compiler_params=params(4),
        cost_estimate=cost(0, 0),
        name="gate",
    )(*map(near, values), *after)


def total_kernel(*refs, count):
    parts, out_ref = refs[:count], refs[-1]
    rows = out_ref.shape[0]
    value = None
    for part in parts:
        for i in range(part.shape[0] // rows):
            term = part[pl.ds(i * rows, rows), :].astype(jnp.float32)
            value = term if value is None else value + term
    out_ref[...] = value.astype(out_ref.dtype)


def total(parts, rows, kind, after=()):
    return pl.pallas_call(
        functools.partial(total_kernel, count=len(parts)),
        out_shape=jax.ShapeDtypeStruct((rows, parts[0].shape[1]), kind),
        in_specs=[WHOLE] * len(parts) + [UNREAD] * len(after),
        compiler_params=params(10),
        cost_estimate=cost(0, 0),
        name="total",
    )(*parts, *after)


def swap(value, axis, size, step):
    return lax.ppermute(value, axis, [(i, i ^ step) for i in range(size)])


def shards(adj_tiles, tile_counts, tile_cols, features, weight, upstream):
    n_row, n_col = lax.axis_size("row"), lax.axis_size("col")
    assert n_row & (n_row - 1) == 0 and n_col & (n_col - 1) == 0 and n_row > 1
    adj, counts, cols = adj_tiles[0, 0], tile_counts[0, 0], tile_cols[0, 0]
    rows, depth = upstream.shape[0], features.shape[0]
    col_tiles = depth * n_row // adj.shape[1]
    chips = n_row // 2
    where = jnp.stack([lax.axis_index("row"), lax.axis_index("col")]).astype(jnp.int32)
    steps = [*range(n_col - 1, 0, -1), 0]

    *blocks, near_features = dense_rows(where, steps, counts, cols, adj, features, rows, col_tiles)
    dense = dict(zip(steps, blocks))

    away = gate([swap(features, "row", n_row, 2 * s) for s in range(chips - 1, 0, -1)], blocks)
    odd = [swap(shard, "row", n_row, 1) for shard in [features, *away[::-1]]]
    even = [near_features, *away[::-1]]
    parts = [shard for pair in zip(even, odd) for shard in pair]

    half = forward(where, blocks[2], even, 0, 2, [], jnp.float32)
    shares = [forward(where, block, parts, 0, 1, [], jnp.bfloat16) for block in blocks[:-1]]
    shares[2] = forward(where, blocks[2], odd, 1, 2, [half], jnp.bfloat16)
    came = [swap(share, "col", n_col, s) for s, share in zip(steps, shares)]
    mine = forward(where, blocks[-1], parts, 0, 1, [], jnp.float32)
    scale = 1.0 / math.sqrt(rows * n_row * n_col)
    hidden, piece, part = middle([mine, *came], weight, upstream, scale)

    pieces = {s: swap(piece, "col", n_col, s) for s in steps[:-1]}
    pieces[0] = piece
    cores = [[i for i in range(n_row) if i % 2 == core] for core in range(2)]
    part = (part + swap(part, "row", n_row, 1)).astype(jnp.bfloat16)
    gathered = lax.all_gather(part, "row", axis_index_groups=cores, tiled=True)
    part = total([gathered], part.shape[0], jnp.bfloat16)

    every = list(range(n_row))
    sums, latest = None, n_col - 1
    for group in [[0, 1], *[[s] for s in range(2, n_col - 1)]]:
        sums = backward(where, [dense[s] for s in group], [pieces[s] for s in group], every, depth, sums, jnp.float32)
    last = functools.partial(backward, where, [dense[latest]], [pieces[latest]])
    sent = last(every[1::2], depth, sums, jnp.bfloat16, [part])
    kept = last(every[::2], depth, sums, jnp.float32)
    came = swap(sent, "row", n_row, 1)
    summed = [(kept[c] + came[c].astype(jnp.float32)).astype(jnp.bfloat16) for c in range(1, chips)]
    parts = [swap(summed[c - 1], "row", n_row, 2 * c) for c in range(1, chips)]

    feature_grad = finish(kept, came, parts)
    for s in range(n_col.bit_length() - 2):
        part = total([part, swap(part, "col", n_col, 1 << s)], part.shape[0], jnp.bfloat16, [kept])
    came = swap(part, "col", n_col, n_col // 2)
    weight_grad = total([part, came], part.shape[0], jnp.float32)
    return hidden, weight_grad, feature_grad


def solution(mesh):
    placed = (
        P("row", "col", None, None, None),
        P("row", "col", None),
        P("row", "col", None),
        P(("col", "row"), None),
        P(),
        P(("row", "col"), None),
    )
    return jax.shard_map(
        shards,
        mesh=mesh,
        in_specs=placed,
        out_specs=(P(("row", "col"), None), P(), P(("col", "row"), None)),
        check_vma=False,
    )
```

```python
import functools
import math

import jax
import jax.numpy as jnp
from jax import lax
from jax.experimental import pallas as pl
from jax.experimental.pallas import tpu as pltpu
from jax.sharding import PartitionSpec as P


MIB = 1024 * 1024
SCALARS = pl.BlockSpec(memory_space=pltpu.SMEM)
WHOLE = pl.BlockSpec(memory_space=pltpu.VMEM)
UNREAD = pl.BlockSpec(memory_space=pl.ANY)


def params(mib):
    return pltpu.CompilerParams(vmem_limit_bytes=mib * MIB)


def cost(flops, moved, exps=0):
    return pl.CostEstimate(flops=flops, bytes_accessed=moved, transcendentals=exps)


def near(value):
    return pltpu.with_memory_space_constraint(value, pltpu.VMEM)


def dense_kernel(where, counts, cols, adj_ref, features_ref, *refs, steps, window):
    outs, (copied_ref, held, total, sems) = refs[: len(steps)], refs[len(steps) :]
    slots, tile, _ = adj_ref.shape
    per = outs[0].shape[0] // tile
    width = outs[0].shape[1]

    plans = []
    for i, step in enumerate(steps):
        first = (where[1] ^ step) * per
        start = lax.fori_loop(0, first, lambda t, s: s + counts[t], jnp.int32(0))
        for u in range(per):
            count = counts[first + u]
            base = jnp.minimum(start, slots - window)
            fetch = pltpu.make_async_copy(
                adj_ref.at[pl.ds(base, window)], held.at[i * per + u], sems.at[i * per + u]
            )
            fetch.start()
            plans.append((start, start - base, count, fetch))
            start = start + count
    copied = pltpu.make_async_copy(features_ref, copied_ref, sems.at[len(plans)])
    copied.start()

    for i, out_ref in enumerate(outs):
        out_ref[...] = jnp.zeros_like(out_ref)
    for n, (start, shift, count, fetch) in enumerate(plans):
        out_ref = outs[n // per]
        rows = pl.ds((n % per) * tile, tile)
        fetch.wait()

        def place(j):
            c = cols[start + j]
            out_ref[rows, pl.ds(pl.multiple_of(c * tile, tile), tile)] = held[n, shift + j]
            return lax.shift_left(jnp.int32(1), c)

        def four(i, state):
            seen, twice = state
            for v in range(4):
                bit = place(4 * i + v)
                twice = twice | (seen & bit)
                seen = seen | bit
            return seen, twice

        def one(j, state):
            seen, twice = state
            bit = place(j)
            return seen | bit, twice | (seen & bit)

        groups = lax.div(count, 4)
        state = lax.fori_loop(0, groups, four, (jnp.int32(0), jnp.int32(0)))
        seen, twice = lax.fori_loop(4 * groups, count, one, state)
        repeated = (twice != 0) if width // tile <= 32 else (count > 0)

        @pl.when(repeated)
        def _():
            total[...] = jnp.zeros_like(total)

            def add(j, carry):
                here = pl.ds(pl.multiple_of(cols[start + j] * tile, tile), tile)
                total[:, here] += held[n, shift + j].astype(jnp.float32)
                return carry

            lax.fori_loop(0, count, add, 0)
            out_ref[rows, :] = total[...].astype(out_ref.dtype)

    copied.wait()


def dense_rows(where, steps, counts, cols, adj, features, rows, col_tiles):
    slots, tile, _ = adj.shape
    window = min(col_tiles, slots)
    width = col_tiles * tile
    tiles = rows // tile * len(steps)
    return pl.pallas_call(
        functools.partial(dense_kernel, steps=steps, window=window),
        out_shape=[pltpu.VMEM((rows, width), adj.dtype) for _ in steps]
        + [pltpu.VMEM(features.shape, features.dtype)],
        in_specs=[SCALARS] * 3 + [pl.BlockSpec(memory_space=pltpu.HBM)] * 2,
        out_specs=[WHOLE] * (len(steps) + 1),
        scratch_shapes=[
            pltpu.VMEM((tiles, window, tile, tile), adj.dtype),
            pltpu.VMEM((tile, width), jnp.float32),
            pltpu.SemaphoreType.DMA((tiles + 1,)),
        ],
        compiler_params=params(26),
        cost_estimate=cost(0, 5 * len(steps) * rows * width),
        name="dense_rows",
    )(where, *[pltpu.with_memory_space_constraint(x, pltpu.HBM) for x in (counts, cols, adj, features)])


def forward_kernel(where, a_ref, *refs, first, step):
    shards, out_ref, before = refs[:-1], refs[-1], None
    if first:
        shards, before = shards[:-1], shards[-1]
    depth = shards[0].shape[0]
    value = None if before is None else before[...]
    for k, shard in enumerate(shards):
        cols = pl.ds(pl.multiple_of((where[0] ^ (first + step * k)) * depth, depth), depth)
        part = jnp.dot(a_ref[:, cols], shard[...], preferred_element_type=jnp.float32)
        value = part if value is None else value + part
    out_ref[...] = value.astype(out_ref.dtype)


def forward(where, dense, shards, first, step, before, kind):
    rows, width = dense.shape[0], shards[0].shape[1]
    operands = [near(x) for x in [dense, *shards, *before]]
    flops = 2 * rows * dense.shape[1] * width
    return pl.pallas_call(
        functools.partial(forward_kernel, first=first, step=step),
        out_shape=pltpu.VMEM((rows, width), kind),
        in_specs=[SCALARS] + [WHOLE] * len(operands),
        out_specs=WHOLE,
        compiler_params=params(10),
        cost_estimate=cost(flops, dense.size * 2),
        name="forward_rows",
    )(where, *operands)


def middle_kernel(*refs, scale, came):
    parts = refs[: came + 1]
    weight_ref, up_ref, hidden_ref, grad_ref, wgrad_ref = refs[came + 1 :]
    agg = parts[0][...].astype(jnp.float32)
    for part in parts[1:]:
        agg = agg + part[...].astype(jnp.float32)
    agg = agg.astype(jnp.bfloat16)
    weight = weight_ref[...]
    pre = jnp.dot(agg, weight, preferred_element_type=jnp.float32)
    sig = jax.nn.sigmoid(pre)
    hidden_ref[...] = (pre * sig).astype(jnp.bfloat16)
    pre_grad = (up_ref[...].astype(jnp.float32) * sig * (1.0 + pre * (1.0 - sig))).astype(jnp.bfloat16)
    grad_ref[...] = lax.dot_general(
        weight, pre_grad, (((1,), (1,)), ((), ())), preferred_element_type=jnp.float32
    ).astype(jnp.bfloat16)
    wgrad_ref[...] = scale * lax.dot_general(
        agg, pre_grad, (((0,), (0,)), ((), ())), preferred_element_type=jnp.float32
    )


def middle(parts, weight, upstream, scale):
    rows, width = upstream.shape
    return pl.pallas_call(
        functools.partial(middle_kernel, scale=scale, came=len(parts) - 1),
        out_shape=(
            jax.ShapeDtypeStruct((rows, width), jnp.bfloat16),
            jax.ShapeDtypeStruct((width, rows), jnp.bfloat16),
            jax.ShapeDtypeStruct((width, width), jnp.float32),
        ),
        compiler_params=params(16),
        cost_estimate=cost(6 * rows * width * width, 10 * rows * width, rows * width),
        name="middle",
    )(*parts, weight, upstream)


def backward_kernel(where, *refs, count, steps, before):
    dense, pieces = refs[:count], refs[count : 2 * count]
    out_ref = refs[-1]
    columns, _, depth = out_ref.shape

    def one(j, carry):
        step = jnp.int32(steps[0])
        for i in range(1, len(steps)):
            step = jnp.where(j == i, steps[i], step)
        cols = pl.ds(pl.multiple_of((where[0] ^ step) * depth, depth), depth)
        value = refs[2 * count][step] if before else None
        for a_ref, piece in zip(dense, pieces):
            part = jnp.dot(piece[...], a_ref[:, cols], preferred_element_type=jnp.float32)
            value = part if value is None else value + part
        out_ref[j] = value.astype(out_ref.dtype)
        return carry

    lax.fori_loop(0, columns, one, 0)


def backward(where, dense, pieces, steps, depth, before, kind, after=()):
    count = len(pieces)
    width, _ = pieces[0].shape
    operands = [near(x) for x in [*dense, *pieces] + ([] if before is None else [before])]
    return pl.pallas_call(
        functools.partial(backward_kernel, count=count, steps=steps, before=before is not None),
        out_shape=pltpu.VMEM((len(steps), width, depth), kind),
        in_specs=[SCALARS] + [WHOLE] * len(operands) + [UNREAD] * len(after),
        out_specs=WHOLE,
        compiler_params=params(10),
        cost_estimate=cost(0, 0),
        name="backward_cols",
    )(where, *operands, *after)


def finish_kernel(*refs):
    parts, out_ref = refs[:-1], refs[-1]
    value = parts[0][0].astype(jnp.float32) + parts[1][0].astype(jnp.float32)
    for part in parts[2:]:
        value = value + part[...].astype(jnp.float32)
    out_ref[...] = value.astype(out_ref.dtype).T


def finish(kept, came, parts):
    _, width, rows = kept.shape
    own = pl.BlockSpec((1, width, rows), lambda i: (0, 0, 0))
    part = pl.BlockSpec((width, rows), lambda i: (0, 0))
    return pl.pallas_call(
        finish_kernel,
        out_shape=jax.ShapeDtypeStruct((rows, width), jnp.bfloat16),
        grid=(1,),
        in_specs=[own, own] + [part] * len(parts),
        out_specs=pl.BlockSpec((rows, width), lambda i: (0, 0)),
        compiler_params=params(12),
        cost_estimate=cost(len(parts) * rows * width, 4 * len(parts) * rows * width),
        name="finish",
    )(kept, came, *parts)


def gate(values, after):
    count = len(values)
    return pl.pallas_call(
        lambda *refs: None,
        out_shape=[pltpu.VMEM(x.shape, x.dtype) for x in values],
        in_specs=[WHOLE] * count + [UNREAD] * len(after),
        out_specs=[WHOLE] * count,
        input_output_aliases={i: i for i in range(count)},
        compiler_params=params(4),
        cost_estimate=cost(0, 0),
        name="gate",
    )(*map(near, values), *after)


def total_kernel(*refs, count):
    parts, out_ref = refs[:count], refs[-1]
    rows = out_ref.shape[0]
    value = None
    for part in parts:
        for i in range(part.shape[0] // rows):
            term = part[pl.ds(i * rows, rows), :].astype(jnp.float32)
            value = term if value is None else value + term
    out_ref[...] = value.astype(out_ref.dtype)


def total(parts, rows, kind, after=()):
    return pl.pallas_call(
        functools.partial(total_kernel, count=len(parts)),
        out_shape=jax.ShapeDtypeStruct((rows, parts[0].shape[1]), kind),
        in_specs=[WHOLE] * len(parts) + [UNREAD] * len(after),
        compiler_params=params(10),
        cost_estimate=cost(0, 0),
        name="total",
    )(*parts, *after)


def swap(value, axis, size, step):
    return lax.ppermute(value, axis, [(i, i ^ step) for i in range(size)])


def shards(adj_tiles, tile_counts, tile_cols, features, weight, upstream):
    n_row, n_col = lax.axis_size("row"), lax.axis_size("col")
    assert n_row & (n_row - 1) == 0 and n_col & (n_col - 1) == 0 and n_row > 1
    adj, counts, cols = adj_tiles[0, 0], tile_counts[0, 0], tile_cols[0, 0]
    rows, depth = upstream.shape[0], features.shape[0]
    col_tiles = depth * n_row // adj.shape[1]
    chips = n_row // 2
    where = jnp.stack([lax.axis_index("row"), lax.axis_index("col")]).astype(jnp.int32)
    line = n_col == 4
    steps = [*range(n_col - 1, 0, -1), 0]

    *blocks, near_features = dense_rows(where, steps, counts, cols, adj, features, rows, col_tiles)
    dense = dict(zip(steps, blocks))

    away = gate([swap(features, "row", n_row, 2 * s) for s in range(chips - 1, 0, -1)], blocks)
    odd = [swap(shard, "row", n_row, 1) for shard in [features, *away[::-1]]]
    even = [near_features, *away[::-1]]
    parts = [shard for pair in zip(even, odd) for shard in pair]

    half = forward(where, dense[n_col - 1], even, 0, 2, [], jnp.float32)
    shares = {n_col - 1: forward(where, dense[n_col - 1], odd, 1, 2, [half], jnp.bfloat16)}
    for s in steps[1:-1]:
        shares[s] = forward(where, dense[s], parts, 0, 1, [], jnp.bfloat16)
    if line:
        relayed = lax.ppermute(shares[3], "col", [(0, 1), (3, 2)])
        came = [lax.ppermute(shares[3], "col", [(1, 2), (2, 1)])]
        joined = (shares[2].astype(jnp.float32) + relayed.astype(jnp.float32)).astype(jnp.bfloat16)
        came += [swap(joined, "col", n_col, 2), swap(shares[1], "col", n_col, 1)]
    else:
        came = [swap(share, "col", n_col, s) for s, share in shares.items()]
    mine = forward(where, dense[0], parts, 0, 1, [], jnp.float32)
    scale = 1.0 / math.sqrt(rows * n_row * n_col)
    hidden, piece, part = middle([mine, *came], weight, upstream, scale)

    cores = [[i for i in range(n_row) if i % 2 == core] for core in range(2)]
    part = (part + swap(part, "row", n_row, 1)).astype(jnp.bfloat16)
    gathered = lax.all_gather(part, "row", axis_index_groups=cores, tiled=True)
    part = total([gathered], part.shape[0], jnp.bfloat16)
    if line:
        pieces = {s: swap(piece, "col", n_col, s) for s in (1, 2)}
        pieces[0], pieces[2] = gate([piece, pieces[2]], [part])
        beside = lax.ppermute(pieces[0], "col", [(1, 2), (2, 1)])
        pieces[3] = beside + lax.ppermute(pieces[2], "col", [(1, 0), (2, 3)])
    else:
        pieces = {s: swap(piece, "col", n_col, s) for s in steps[:-1]}
        pieces[0] = piece

    every = list(range(n_row))
    sums, latest = None, n_col - 1
    for group in [list(range(n_col - 1))]:
        sums = backward(where, [dense[s] for s in group], [pieces[s] for s in group], every, depth, sums, jnp.float32)
    last = functools.partial(backward, where, [dense[latest]], [pieces[latest]])
    sent = last(every[1::2], depth, sums, jnp.bfloat16, [part])
    kept = last(every[::2], depth, sums, jnp.float32)
    came = swap(sent, "row", n_row, 1)
    summed = [(kept[c] + came[c].astype(jnp.float32)).astype(jnp.bfloat16) for c in range(1, chips)]
    parts = [swap(summed[c - 1], "row", n_row, 2 * c) for c in range(1, chips)]

    feature_grad = finish(kept, came, parts)
    for s in range(n_col.bit_length() - 2):
        part = total([part, swap(part, "col", n_col, 1 << s)], part.shape[0], jnp.bfloat16, [kept])
    came = swap(part, "col", n_col, n_col // 2)
    weight_grad = total([part, came], part.shape[0], jnp.float32)
    return hidden, weight_grad, feature_grad


def solution(mesh):
    placed = (
        P("row", "col", None, None, None),
        P("row", "col", None),
        P("row", "col", None),
        P(("col", "row"), None),
        P(),
        P(("row", "col"), None),
    )
    return jax.shard_map(
        shards,
        mesh=mesh,
        in_specs=placed,
        out_specs=(P(("row", "col"), None), P(), P(("col", "row"), None)),
        check_vma=False,
    )
```

```python
import functools
import math

import jax
import jax.numpy as jnp
from jax import lax
from jax.experimental import pallas as pl
from jax.experimental.pallas import tpu as pltpu
from jax.sharding import PartitionSpec as P


MIB = 1024 * 1024
SCALARS = pl.BlockSpec(memory_space=pltpu.SMEM)
WHOLE = pl.BlockSpec(memory_space=pltpu.VMEM)
UNREAD = pl.BlockSpec(memory_space=pl.ANY)


def params(mib):
    return pltpu.CompilerParams(vmem_limit_bytes=mib * MIB)


def cost(flops, moved, exps=0):
    return pl.CostEstimate(flops=flops, bytes_accessed=moved, transcendentals=exps)


def near(value):
    return pltpu.with_memory_space_constraint(value, pltpu.VMEM)


def dense_kernel(where, counts, cols, adj_ref, features_ref, *refs, steps, window):
    outs, (copied_ref, held, total, sems) = refs[: len(steps)], refs[len(steps) :]
    slots, tile, _ = adj_ref.shape
    per = outs[0].shape[0] // tile
    width = outs[0].shape[1]

    plans = []
    for i, step in enumerate(steps):
        first = (where[1] ^ step) * per
        start = lax.fori_loop(0, first, lambda t, s: s + counts[t], jnp.int32(0))
        for u in range(per):
            count = counts[first + u]
            base = jnp.minimum(start, slots - window)
            fetch = pltpu.make_async_copy(
                adj_ref.at[pl.ds(base, window)], held.at[i * per + u], sems.at[i * per + u]
            )
            fetch.start()
            plans.append((start, start - base, count, fetch))
            start = start + count
    copied = pltpu.make_async_copy(features_ref, copied_ref, sems.at[len(plans)])
    copied.start()

    for i, out_ref in enumerate(outs):
        out_ref[...] = jnp.zeros_like(out_ref)
    for n, (start, shift, count, fetch) in enumerate(plans):
        out_ref = outs[n // per]
        rows = pl.ds((n % per) * tile, tile)
        fetch.wait()

        def place(j):
            c = cols[start + j]
            out_ref[rows, pl.ds(pl.multiple_of(c * tile, tile), tile)] = held[n, shift + j]
            return lax.shift_left(jnp.int32(1), c)

        def four(i, state):
            seen, twice = state
            for v in range(4):
                bit = place(4 * i + v)
                twice = twice | (seen & bit)
                seen = seen | bit
            return seen, twice

        def one(j, state):
            seen, twice = state
            bit = place(j)
            return seen | bit, twice | (seen & bit)

        groups = lax.div(count, 4)
        state = lax.fori_loop(0, groups, four, (jnp.int32(0), jnp.int32(0)))
        seen, twice = lax.fori_loop(4 * groups, count, one, state)
        repeated = (twice != 0) if width // tile <= 32 else (count > 0)

        @pl.when(repeated)
        def _():
            total[...] = jnp.zeros_like(total)

            def add(j, carry):
                here = pl.ds(pl.multiple_of(cols[start + j] * tile, tile), tile)
                total[:, here] += held[n, shift + j].astype(jnp.float32)
                return carry

            lax.fori_loop(0, count, add, 0)
            out_ref[rows, :] = total[...].astype(out_ref.dtype)

    copied.wait()


def dense_rows(where, steps, counts, cols, adj, features, rows, col_tiles):
    slots, tile, _ = adj.shape
    window = min(col_tiles, slots)
    width = col_tiles * tile
    tiles = rows // tile * len(steps)
    return pl.pallas_call(
        functools.partial(dense_kernel, steps=steps, window=window),
        out_shape=[pltpu.VMEM((rows, width), adj.dtype) for _ in steps]
        + [pltpu.VMEM(features.shape, features.dtype)],
        in_specs=[SCALARS] * 3 + [pl.BlockSpec(memory_space=pltpu.HBM)] * 2,
        out_specs=[WHOLE] * (len(steps) + 1),
        scratch_shapes=[
            pltpu.VMEM((tiles, window, tile, tile), adj.dtype),
            pltpu.VMEM((tile, width), jnp.float32),
            pltpu.SemaphoreType.DMA((tiles + 1,)),
        ],
        compiler_params=params(26),
        cost_estimate=cost(0, 5 * len(steps) * rows * width),
        name="dense_rows",
    )(where, *[pltpu.with_memory_space_constraint(x, pltpu.HBM) for x in (counts, cols, adj, features)])


def forward_kernel(where, a_ref, *refs, first, step):
    shards, out_ref, before = refs[:-1], refs[-1], None
    if first:
        shards, before = shards[:-1], shards[-1]
    depth = shards[0].shape[0]
    value = None if before is None else before[...]
    for k, shard in enumerate(shards):
        cols = pl.ds(pl.multiple_of((where[0] ^ (first + step * k)) * depth, depth), depth)
        part = jnp.dot(a_ref[:, cols], shard[...], preferred_element_type=jnp.float32)
        value = part if value is None else value + part
    out_ref[...] = value.astype(out_ref.dtype)


def forward(where, dense, shards, first, step, before, kind):
    rows, width = dense.shape[0], shards[0].shape[1]
    operands = [near(x) for x in [dense, *shards, *before]]
    flops = 2 * rows * dense.shape[1] * width
    return pl.pallas_call(
        functools.partial(forward_kernel, first=first, step=step),
        out_shape=pltpu.VMEM((rows, width), kind),
        in_specs=[SCALARS] + [WHOLE] * len(operands),
        out_specs=WHOLE,
        compiler_params=params(10),
        cost_estimate=cost(flops, dense.size * 2),
        name="forward_rows",
    )(where, *operands)


def middle_kernel(*refs, scale, came):
    parts = refs[: came + 1]
    weight_ref, up_ref, hidden_ref, grad_ref, wgrad_ref = refs[came + 1 :]
    agg = parts[0][...].astype(jnp.float32)
    for part in parts[1:]:
        agg = agg + part[...].astype(jnp.float32)
    agg = agg.astype(jnp.bfloat16)
    weight = weight_ref[...]
    pre = jnp.dot(agg, weight, preferred_element_type=jnp.float32)
    sig = jax.nn.sigmoid(pre)
    hidden_ref[...] = (pre * sig).astype(jnp.bfloat16)
    pre_grad = (up_ref[...].astype(jnp.float32) * sig * (1.0 + pre * (1.0 - sig))).astype(jnp.bfloat16)
    grad_ref[...] = lax.dot_general(
        weight, pre_grad, (((1,), (1,)), ((), ())), preferred_element_type=jnp.float32
    ).astype(jnp.bfloat16)
    wgrad_ref[...] = scale * lax.dot_general(
        agg, pre_grad, (((0,), (0,)), ((), ())), preferred_element_type=jnp.float32
    )


def middle(parts, weight, upstream, scale):
    rows, width = upstream.shape
    return pl.pallas_call(
        functools.partial(middle_kernel, scale=scale, came=len(parts) - 1),
        out_shape=(
            jax.ShapeDtypeStruct((rows, width), jnp.bfloat16),
            jax.ShapeDtypeStruct((width, rows), jnp.bfloat16),
            jax.ShapeDtypeStruct((width, width), jnp.float32),
        ),
        compiler_params=params(16),
        cost_estimate=cost(6 * rows * width * width, 10 * rows * width, rows * width),
        name="middle",
    )(*parts, weight, upstream)


def backward_kernel(where, *refs, count, steps, before):
    dense, pieces = refs[:count], refs[count : 2 * count]
    out_ref = refs[-1]
    columns, _, depth = out_ref.shape

    def one(j, carry):
        step = jnp.int32(steps[0])
        for i in range(1, len(steps)):
            step = jnp.where(j == i, steps[i], step)
        cols = pl.ds(pl.multiple_of((where[0] ^ step) * depth, depth), depth)
        value = refs[2 * count][step] if before else None
        for a_ref, piece in zip(dense, pieces):
            part = jnp.dot(piece[...], a_ref[:, cols], preferred_element_type=jnp.float32)
            value = part if value is None else value + part
        out_ref[j] = value.astype(out_ref.dtype)
        return carry

    lax.fori_loop(0, columns, one, 0)


def backward(where, dense, pieces, steps, depth, before, kind, after=()):
    count = len(pieces)
    width, _ = pieces[0].shape
    operands = [near(x) for x in [*dense, *pieces] + ([] if before is None else [before])]
    return pl.pallas_call(
        functools.partial(backward_kernel, count=count, steps=steps, before=before is not None),
        out_shape=pltpu.VMEM((len(steps), width, depth), kind),
        in_specs=[SCALARS] + [WHOLE] * len(operands) + [UNREAD] * len(after),
        out_specs=WHOLE,
        compiler_params=params(10),
        cost_estimate=cost(0, 0),
        name="backward_cols",
    )(where, *operands, *after)


def finish_kernel(*refs):
    parts, out_ref = refs[:-1], refs[-1]
    value = parts[0][0].astype(jnp.float32) + parts[1][0].astype(jnp.float32)
    for part in parts[2:]:
        value = value + part[...].astype(jnp.float32)
    out_ref[...] = value.astype(out_ref.dtype).T


def finish(kept, came, parts):
    _, width, rows = kept.shape
    own = pl.BlockSpec((1, width, rows), lambda i: (0, 0, 0))
    part = pl.BlockSpec((width, rows), lambda i: (0, 0))
    return pl.pallas_call(
        finish_kernel,
        out_shape=jax.ShapeDtypeStruct((rows, width), jnp.bfloat16),
        grid=(1,),
        in_specs=[own, own] + [part] * len(parts),
        out_specs=pl.BlockSpec((rows, width), lambda i: (0, 0)),
        compiler_params=params(12),
        cost_estimate=cost(len(parts) * rows * width, 4 * len(parts) * rows * width),
        name="finish",
    )(kept, came, *parts)


def gate(values, after):
    count = len(values)
    return pl.pallas_call(
        lambda *refs: None,
        out_shape=[pltpu.VMEM(x.shape, x.dtype) for x in values],
        in_specs=[WHOLE] * count + [UNREAD] * len(after),
        out_specs=[WHOLE] * count,
        input_output_aliases={i: i for i in range(count)},
        compiler_params=params(4),
        cost_estimate=cost(0, 0),
        name="gate",
    )(*map(near, values), *after)


def total_kernel(*refs, count):
    parts, out_ref = refs[:count], refs[-1]
    rows = out_ref.shape[0]
    value = None
    for part in parts:
        for i in range(part.shape[0] // rows):
            term = part[pl.ds(i * rows, rows), :].astype(jnp.float32)
            value = term if value is None else value + term
    out_ref[...] = value.astype(out_ref.dtype)


def total(parts, rows, kind, after=()):
    return pl.pallas_call(
        functools.partial(total_kernel, count=len(parts)),
        out_shape=jax.ShapeDtypeStruct((rows, parts[0].shape[1]), kind),
        in_specs=[WHOLE] * len(parts) + [UNREAD] * len(after),
        compiler_params=params(10),
        cost_estimate=cost(0, 0),
        name="total",
    )(*parts, *after)


def swap(value, axis, size, step):
    return lax.ppermute(value, axis, [(i, i ^ step) for i in range(size)])


def shards(adj_tiles, tile_counts, tile_cols, features, weight, upstream):
    n_row, n_col = lax.axis_size("row"), lax.axis_size("col")
    assert n_row & (n_row - 1) == 0 and n_col & (n_col - 1) == 0 and n_row > 1
    adj, counts, cols = adj_tiles[0, 0], tile_counts[0, 0], tile_cols[0, 0]
    rows, depth = upstream.shape[0], features.shape[0]
    col_tiles = depth * n_row // adj.shape[1]
    chips = n_row // 2
    where = jnp.stack([lax.axis_index("row"), lax.axis_index("col")]).astype(jnp.int32)
    line = n_col == 4
    steps = [*range(n_col - 1, 0, -1), 0]

    *blocks, near_features = dense_rows(where, steps, counts, cols, adj, features, rows, col_tiles)
    dense = dict(zip(steps, blocks))

    away = gate([swap(features, "row", n_row, 2 * s) for s in range(chips - 1, 0, -1)], blocks)
    odd = [swap(shard, "row", n_row, 1) for shard in [features, *away[::-1]]]
    even = [near_features, *away[::-1]]
    parts = [shard for pair in zip(even, odd) for shard in pair]

    half = forward(where, dense[n_col - 1], even, 0, 2, [], jnp.float32)
    shares = {n_col - 1: forward(where, dense[n_col - 1], odd, 1, 2, [half], jnp.bfloat16)}
    for s in steps[1:-1]:
        shares[s] = forward(where, dense[s], parts, 0, 1, [], jnp.bfloat16)
    if line:
        relayed = lax.ppermute(shares[3], "col", [(0, 1), (3, 2)])
        came = [lax.ppermute(shares[3], "col", [(1, 2), (2, 1)])]
        joined = (shares[2].astype(jnp.float32) + relayed.astype(jnp.float32)).astype(jnp.bfloat16)
        joined, shares[1] = gate([joined, shares[1]], [])
        came += [swap(joined, "col", n_col, 2), swap(shares[1], "col", n_col, 1)]
    else:
        came = [swap(share, "col", n_col, s) for s, share in shares.items()]
    mine = forward(where, dense[0], parts, 0, 1, [], jnp.float32)
    scale = 1.0 / math.sqrt(rows * n_row * n_col)
    hidden, piece, part = middle([mine, *came], weight, upstream, scale)

    cores = [[i for i in range(n_row) if i % 2 == core] for core in range(2)]
    part = (part + swap(part, "row", n_row, 1)).astype(jnp.bfloat16)
    gathered = lax.all_gather(part, "row", axis_index_groups=cores, tiled=True)
    part = total([gathered], part.shape[0], jnp.bfloat16)
    if line:
        pieces = {s: swap(piece, "col", n_col, s) for s in (2, 1)}
        pieces[0], pieces[2] = gate([piece, pieces[2]], [part])
        relayed = lax.ppermute(pieces[2], "col", [(1, 0), (2, 3)])
        pieces[3] = relayed + lax.ppermute(pieces[0], "col", [(1, 2), (2, 1)])
    else:
        pieces = {s: swap(piece, "col", n_col, s) for s in steps[:-1]}
        pieces[0] = piece

    every = list(range(n_row))
    sums, latest = None, n_col - 1
    for group in [list(range(n_col - 1))]:
        sums = backward(where, [dense[s] for s in group], [pieces[s] for s in group], every, depth, sums, jnp.float32)
    last = functools.partial(backward, where, [dense[latest]], [pieces[latest]])
    sent = last(every[1::2], depth, sums, jnp.bfloat16, [part])
    kept = last(every[::2], depth, sums, jnp.float32)
    came = swap(sent, "row", n_row, 1)
    summed = [(kept[c] + came[c].astype(jnp.float32)).astype(jnp.bfloat16) for c in range(1, chips)]
    parts = [swap(summed[c - 1], "row", n_row, 2 * c) for c in range(1, chips)]

    feature_grad = finish(kept, came, parts)
    for s in range(n_col.bit_length() - 2):
        part = total([part, swap(part, "col", n_col, 1 << s)], part.shape[0], jnp.bfloat16, [kept])
    came = swap(part, "col", n_col, n_col // 2)
    weight_grad = total([part, came], part.shape[0], jnp.float32)
    return hidden, weight_grad, feature_grad


def solution(mesh):
    placed = (
        P("row", "col", None, None, None),
        P("row", "col", None),
        P("row", "col", None),
        P(("col", "row"), None),
        P(),
        P(("row", "col"), None),
    )
    return jax.shard_map(
        shards,
        mesh=mesh,
        in_specs=placed,
        out_specs=(P(("row", "col"), None), P(), P(("col", "row"), None)),
        check_vma=False,
    )
```

```python
import functools
import math

import jax
import jax.numpy as jnp
from jax import lax
from jax.experimental import pallas as pl
from jax.experimental.pallas import tpu as pltpu
from jax.sharding import PartitionSpec as P


MIB = 1024 * 1024
SCALARS = pl.BlockSpec(memory_space=pltpu.SMEM)
WHOLE = pl.BlockSpec(memory_space=pltpu.VMEM)
UNREAD = pl.BlockSpec(memory_space=pl.ANY)


def params(mib):
    return pltpu.CompilerParams(vmem_limit_bytes=mib * MIB)


def cost(flops, moved, exps=0):
    return pl.CostEstimate(flops=flops, bytes_accessed=moved, transcendentals=exps)


def near(value):
    return pltpu.with_memory_space_constraint(value, pltpu.VMEM)


def dense_kernel(where, counts, cols, adj_ref, features_ref, *refs, steps, window):
    outs, (copied_ref, held, total, sems) = refs[: len(steps)], refs[len(steps) :]
    slots, tile, _ = adj_ref.shape
    per = outs[0].shape[0] // tile
    width = outs[0].shape[1]

    plans = []
    for i, step in enumerate(steps):
        first = (where[1] ^ step) * per
        start = lax.fori_loop(0, first, lambda t, s: s + counts[t], jnp.int32(0))
        for u in range(per):
            count = counts[first + u]
            base = jnp.minimum(start, slots - window)
            fetch = pltpu.make_async_copy(
                adj_ref.at[pl.ds(base, window)], held.at[i * per + u], sems.at[i * per + u]
            )
            fetch.start()
            plans.append((start, start - base, count, fetch))
            start = start + count
    copied = pltpu.make_async_copy(features_ref, copied_ref, sems.at[len(plans)])
    copied.start()

    for i, out_ref in enumerate(outs):
        out_ref[...] = jnp.zeros_like(out_ref)
    for n, (start, shift, count, fetch) in enumerate(plans):
        out_ref = outs[n // per]
        rows = pl.ds((n % per) * tile, tile)
        fetch.wait()

        def place(j):
            c = cols[start + j]
            out_ref[rows, pl.ds(pl.multiple_of(c * tile, tile), tile)] = held[n, shift + j]
            return lax.shift_left(jnp.int32(1), c)

        def four(i, state):
            seen, twice = state
            for v in range(4):
                bit = place(4 * i + v)
                twice = twice | (seen & bit)
                seen = seen | bit
            return seen, twice

        def one(j, state):
            seen, twice = state
            bit = place(j)
            return seen | bit, twice | (seen & bit)

        groups = lax.div(count, 4)
        state = lax.fori_loop(0, groups, four, (jnp.int32(0), jnp.int32(0)))
        seen, twice = lax.fori_loop(4 * groups, count, one, state)
        repeated = (twice != 0) if width // tile <= 32 else (count > 0)

        @pl.when(repeated)
        def _():
            total[...] = jnp.zeros_like(total)

            def add(j, carry):
                here = pl.ds(pl.multiple_of(cols[start + j] * tile, tile), tile)
                total[:, here] += held[n, shift + j].astype(jnp.float32)
                return carry

            lax.fori_loop(0, count, add, 0)
            out_ref[rows, :] = total[...].astype(out_ref.dtype)

    copied.wait()


def dense_rows(where, steps, counts, cols, adj, features, rows, col_tiles):
    slots, tile, _ = adj.shape
    window = min(col_tiles, slots)
    width = col_tiles * tile
    tiles = rows // tile * len(steps)
    return pl.pallas_call(
        functools.partial(dense_kernel, steps=steps, window=window),
        out_shape=[pltpu.VMEM((rows, width), adj.dtype) for _ in steps]
        + [pltpu.VMEM(features.shape, features.dtype)],
        in_specs=[SCALARS] * 3 + [pl.BlockSpec(memory_space=pltpu.HBM)] * 2,
        out_specs=[WHOLE] * (len(steps) + 1),
        scratch_shapes=[
            pltpu.VMEM((tiles, window, tile, tile), adj.dtype),
            pltpu.VMEM((tile, width), jnp.float32),
            pltpu.SemaphoreType.DMA((tiles + 1,)),
        ],
        compiler_params=params(26),
        cost_estimate=cost(0, 5 * len(steps) * rows * width),
        name="dense_rows",
    )(where, *[pltpu.with_memory_space_constraint(x, pltpu.HBM) for x in (counts, cols, adj, features)])


def forward_kernel(where, a_ref, *refs, steps, before):
    shards, out_ref = refs[: len(steps)], refs[-1]
    depth = shards[0].shape[0]
    value = refs[len(steps)][...] if before else None
    for step, shard in zip(steps, shards):
        cols = pl.ds(pl.multiple_of((where[0] ^ step) * depth, depth), depth)
        part = jnp.dot(a_ref[:, cols], shard[...], preferred_element_type=jnp.float32)
        value = part if value is None else value + part
    out_ref[...] = value.astype(out_ref.dtype)


def forward(where, dense, shards, steps, before, kind):
    rows, width = dense.shape[0], shards[0].shape[1]
    operands = [near(x) for x in [dense, *[shards[s] for s in steps], *before]]
    return pl.pallas_call(
        functools.partial(forward_kernel, steps=steps, before=bool(before)),
        out_shape=pltpu.VMEM((rows, width), kind),
        in_specs=[SCALARS] + [WHOLE] * len(operands),
        out_specs=WHOLE,
        compiler_params=params(10),
        cost_estimate=cost(2 * dense.size * width, dense.size * 2),
        name="forward_rows",
    )(where, *operands)


def middle_kernel(*refs, scale, came):
    parts = refs[: came + 1]
    weight_ref, up_ref, hidden_ref, grad_ref, wgrad_ref = refs[came + 1 :]
    agg = parts[0][...].astype(jnp.float32)
    for part in parts[1:]:
        agg = agg + part[...].astype(jnp.float32)
    agg = agg.astype(jnp.bfloat16)
    weight = weight_ref[...]
    pre = jnp.dot(agg, weight, preferred_element_type=jnp.float32)
    sig = jax.nn.sigmoid(pre)
    hidden_ref[...] = (pre * sig).astype(jnp.bfloat16)
    pre_grad = (up_ref[...].astype(jnp.float32) * sig * (1.0 + pre * (1.0 - sig))).astype(jnp.bfloat16)
    grad_ref[...] = lax.dot_general(
        weight, pre_grad, (((1,), (1,)), ((), ())), preferred_element_type=jnp.float32
    ).astype(jnp.bfloat16)
    wgrad_ref[...] = scale * lax.dot_general(
        agg, pre_grad, (((0,), (0,)), ((), ())), preferred_element_type=jnp.float32
    )


def middle(parts, weight, upstream, scale):
    rows, width = upstream.shape
    return pl.pallas_call(
        functools.partial(middle_kernel, scale=scale, came=len(parts) - 1),
        out_shape=(
            jax.ShapeDtypeStruct((rows, width), jnp.bfloat16),
            jax.ShapeDtypeStruct((width, rows), jnp.bfloat16),
            jax.ShapeDtypeStruct((width, width), jnp.float32),
        ),
        compiler_params=params(16),
        cost_estimate=cost(6 * rows * width * width, 10 * rows * width, rows * width),
        name="middle",
    )(*parts, weight, upstream)


def backward_kernel(where, *refs, count, steps, before):
    dense, pieces = refs[:count], refs[count : 2 * count]
    out_ref = refs[-1]
    depth = out_ref.shape[2]

    for j, step in enumerate(steps):
        cols = pl.ds(pl.multiple_of((where[0] ^ step) * depth, depth), depth)
        value = refs[2 * count][step] if before else None
        for a_ref, piece in zip(dense, pieces):
            part = jnp.dot(piece[...], a_ref[:, cols], preferred_element_type=jnp.float32)
            value = part if value is None else value + part
        out_ref[j] = value.astype(out_ref.dtype)


def backward(where, dense, pieces, steps, depth, before, kind, after=()):
    count = len(pieces)
    width, _ = pieces[0].shape
    operands = [near(x) for x in [*dense, *pieces] + ([] if before is None else [before])]
    return pl.pallas_call(
        functools.partial(backward_kernel, count=count, steps=steps, before=before is not None),
        out_shape=pltpu.VMEM((len(steps), width, depth), kind),
        in_specs=[SCALARS] + [WHOLE] * len(operands) + [UNREAD] * len(after),
        out_specs=WHOLE,
        compiler_params=params(10),
        cost_estimate=cost(0, 0),
        name="backward_cols",
    )(where, *operands, *after)


def finish_kernel(*refs):
    parts, out_ref = refs[:-1], refs[-1]
    value = parts[0][...].astype(jnp.float32)
    for part in parts[1:]:
        value = value + part[...].astype(jnp.float32)
    out_ref[...] = value.astype(out_ref.dtype).T


def finish(parts):
    width, rows = parts[0].shape
    return pl.pallas_call(
        finish_kernel,
        out_shape=jax.ShapeDtypeStruct((rows, width), jnp.bfloat16),
        compiler_params=params(12),
        cost_estimate=cost(len(parts) * rows * width, 4 * len(parts) * rows * width),
        name="finish",
    )(*parts)


def gate(values, after):
    count = len(values)
    return pl.pallas_call(
        lambda *refs: None,
        out_shape=[pltpu.VMEM(x.shape, x.dtype) for x in values],
        in_specs=[WHOLE] * count + [UNREAD] * len(after),
        out_specs=[WHOLE] * count,
        input_output_aliases={i: i for i in range(count)},
        compiler_params=params(4),
        cost_estimate=cost(0, 0),
        name="gate",
    )(*map(near, values), *after)


def total_kernel(*refs, count):
    parts, out_ref = refs[:count], refs[-1]
    rows = out_ref.shape[0]
    value = None
    for part in parts:
        for i in range(part.shape[0] // rows):
            term = part[pl.ds(i * rows, rows), :].astype(jnp.float32)
            value = term if value is None else value + term
    out_ref[...] = value.astype(out_ref.dtype)


def total(parts, rows, kind, after=()):
    return pl.pallas_call(
        functools.partial(total_kernel, count=len(parts)),
        out_shape=jax.ShapeDtypeStruct((rows, parts[0].shape[1]), kind),
        in_specs=[WHOLE] * len(parts) + [UNREAD] * len(after),
        compiler_params=params(10),
        cost_estimate=cost(0, 0),
        name="total",
    )(*parts, *after)


def swap(value, axis, size, step):
    return lax.ppermute(value, axis, [(i, i ^ step) for i in range(size)])


def shards(adj_tiles, tile_counts, tile_cols, features, weight, upstream):
    n_row, n_col = lax.axis_size("row"), lax.axis_size("col")
    assert n_row & (n_row - 1) == 0 and n_col & (n_col - 1) == 0 and n_row > 1
    adj, counts, cols = adj_tiles[0, 0], tile_counts[0, 0], tile_cols[0, 0]
    rows, depth = upstream.shape[0], features.shape[0]
    col_tiles = depth * n_row // adj.shape[1]
    chips = n_row // 2
    where = jnp.stack([lax.axis_index("row"), lax.axis_index("col")]).astype(jnp.int32)
    line = n_col == 4
    steps = [*range(n_col - 1, 0, -1), 0]

    *blocks, near_features = dense_rows(where, steps, counts, cols, adj, features, rows, col_tiles)
    dense = dict(zip(steps, blocks))

    far = n_col - 1
    every = list(range(n_row))
    away = gate([swap(features, "row", n_row, 2 * c) for c in range(chips - 1, 0, -1)], blocks)[::-1]
    parts = {0: near_features, 1: swap(features, "row", n_row, 1)}
    for c, shard in enumerate(away, 1):
        parts.update({2 * c: shard, 2 * c + 1: swap(shard, "row", n_row, 1)})

    half = forward(where, dense[far], parts, every[::2], [], jnp.float32)
    first = forward(where, dense[far], parts, every[1::2], [half], jnp.bfloat16)
    shares = {far: first}
    for s in steps[1:-1]:
        shares[s] = forward(where, dense[s], parts, every, [], jnp.bfloat16)
    if line:
        relayed = lax.ppermute(shares[3], "col", [(0, 1), (3, 2)])
        came = [lax.ppermute(shares[3], "col", [(1, 2), (2, 1)])]
        joined = (shares[2].astype(jnp.float32) + relayed.astype(jnp.float32)).astype(jnp.bfloat16)
        came += [swap(joined, "col", n_col, 2), swap(shares[1], "col", n_col, 1)]
    else:
        came = [swap(share, "col", n_col, s) for s, share in shares.items()]
    mine = forward(where, dense[0], parts, every, [], jnp.float32)
    scale = 1.0 / math.sqrt(rows * n_row * n_col)
    hidden, piece, part = middle([mine, *came], weight, upstream, scale)

    cores = [[i for i in range(n_row) if i % 2 == core] for core in range(2)]
    part = (part + swap(part, "row", n_row, 1)).astype(jnp.bfloat16)
    gathered = lax.all_gather(part, "row", axis_index_groups=cores, tiled=True)
    part = total([gathered], part.shape[0], jnp.bfloat16)
    if line:
        pieces = {s: swap(piece, "col", n_col, s) for s in (1, 2)}
        pieces[0], pieces[2] = gate([piece, pieces[2]], [part])
        beside = lax.ppermute(pieces[0], "col", [(1, 2), (2, 1)])
        pieces[3] = beside + lax.ppermute(pieces[2], "col", [(1, 0), (2, 3)])
    else:
        pieces = {s: swap(piece, "col", n_col, s) for s in steps[:-1]}
        pieces[0] = piece

    sums, latest = None, n_col - 1
    for group in [list(range(n_col - 1))]:
        sums = backward(where, [dense[s] for s in group], [pieces[s] for s in group], every, depth, sums, jnp.float32)
    last = functools.partial(backward, where, [dense[latest]], [pieces[latest]])
    sent = last(every[1::2], depth, sums, jnp.bfloat16, [part])
    kept = last(every[::2], depth, sums, jnp.float32)
    came = swap(sent, "row", n_row, 1)
    own, *summed = [kept[c] + came[c].astype(jnp.float32) for c in range(chips)]
    summed = [value.astype(jnp.bfloat16) for value in summed]
    parts = [swap(summed[c - 1], "row", n_row, 2 * c) for c in range(1, chips)]

    feature_grad = finish([own, *parts])
    for s in range(n_col.bit_length() - 2):
        part = total([part, swap(part, "col", n_col, 1 << s)], part.shape[0], jnp.bfloat16, [kept])
    came = swap(part, "col", n_col, n_col // 2)
    weight_grad = total([part, came], part.shape[0], jnp.float32)
    return hidden, weight_grad, feature_grad


def solution(mesh):
    placed = (
        P("row", "col", None, None, None),
        P("row", "col", None),
        P("row", "col", None),
        P(("col", "row"), None),
        P(),
        P(("row", "col"), None),
    )
    return jax.shard_map(
        shards,
        mesh=mesh,
        in_specs=placed,
        out_specs=(P(("row", "col"), None), P(), P(("col", "row"), None)),
        check_vma=False,
    )
```

```python
import functools
import math

import jax
import jax.numpy as jnp
from jax import lax
from jax.experimental import pallas as pl
from jax.experimental.pallas import tpu as pltpu
from jax.sharding import PartitionSpec as P


MIB = 1024 * 1024
SCALARS = pl.BlockSpec(memory_space=pltpu.SMEM)
WHOLE = pl.BlockSpec(memory_space=pltpu.VMEM)
UNREAD = pl.BlockSpec(memory_space=pl.ANY)


def params(mib):
    return pltpu.CompilerParams(vmem_limit_bytes=mib * MIB)


def cost(flops, moved, exps=0):
    return pl.CostEstimate(flops=flops, bytes_accessed=moved, transcendentals=exps)


def near(value):
    return pltpu.with_memory_space_constraint(value, pltpu.VMEM)


def dense_kernel(where, counts, cols, adj_ref, features_ref, *refs, steps, window):
    outs, (copied_ref, held, total, sems) = refs[: len(steps)], refs[len(steps) :]
    slots, tile, _ = adj_ref.shape
    per = outs[0].shape[0] // tile
    width = outs[0].shape[1]

    plans = []
    for i, step in enumerate(steps):
        first = (where[1] ^ step) * per
        start = lax.fori_loop(0, first, lambda t, s: s + counts[t], jnp.int32(0))
        for u in range(per):
            count = counts[first + u]
            base = jnp.minimum(start, slots - window)
            fetch = pltpu.make_async_copy(
                adj_ref.at[pl.ds(base, window)], held.at[i * per + u], sems.at[i * per + u]
            )
            fetch.start()
            plans.append((start, start - base, count, fetch))
            start = start + count
    copied = pltpu.make_async_copy(features_ref, copied_ref, sems.at[len(plans)])
    copied.start()

    for i, out_ref in enumerate(outs):
        out_ref[...] = jnp.zeros_like(out_ref)
    for n, (start, shift, count, fetch) in enumerate(plans):
        out_ref = outs[n // per]
        rows = pl.ds((n % per) * tile, tile)
        fetch.wait()

        def place(j):
            c = cols[start + j]
            out_ref[rows, pl.ds(pl.multiple_of(c * tile, tile), tile)] = held[n, shift + j]
            return lax.shift_left(jnp.int32(1), c)

        def four(i, state):
            seen, twice = state
            for v in range(4):
                bit = place(4 * i + v)
                twice = twice | (seen & bit)
                seen = seen | bit
            return seen, twice

        def one(j, state):
            seen, twice = state
            bit = place(j)
            return seen | bit, twice | (seen & bit)

        groups = lax.div(count, 4)
        state = lax.fori_loop(0, groups, four, (jnp.int32(0), jnp.int32(0)))
        seen, twice = lax.fori_loop(4 * groups, count, one, state)
        repeated = (twice != 0) if width // tile <= 32 else (count > 0)

        @pl.when(repeated)
        def _():
            total[...] = jnp.zeros_like(total)

            def add(j, carry):
                here = pl.ds(pl.multiple_of(cols[start + j] * tile, tile), tile)
                total[:, here] += held[n, shift + j].astype(jnp.float32)
                return carry

            lax.fori_loop(0, count, add, 0)
            out_ref[rows, :] = total[...].astype(out_ref.dtype)

    copied.wait()


def dense_rows(where, steps, counts, cols, adj, features, rows, col_tiles):
    slots, tile, _ = adj.shape
    window = min(col_tiles, slots)
    width = col_tiles * tile
    tiles = rows // tile * len(steps)
    return pl.pallas_call(
        functools.partial(dense_kernel, steps=steps, window=window),
        out_shape=[pltpu.VMEM((rows, width), adj.dtype) for _ in steps]
        + [pltpu.VMEM(features.shape, features.dtype)],
        in_specs=[SCALARS] * 3 + [pl.BlockSpec(memory_space=pltpu.HBM)] * 2,
        out_specs=[WHOLE] * (len(steps) + 1),
        scratch_shapes=[
            pltpu.VMEM((tiles, window, tile, tile), adj.dtype),
            pltpu.VMEM((tile, width), jnp.float32),
            pltpu.SemaphoreType.DMA((tiles + 1,)),
        ],
        compiler_params=params(26),
        cost_estimate=cost(0, 5 * len(steps) * rows * width),
        name="dense_rows",
    )(where, *[pltpu.with_memory_space_constraint(x, pltpu.HBM) for x in (counts, cols, adj, features)])


def forward_kernel(where, a_ref, *refs, steps, before):
    shards, out_ref = refs[: len(steps)], refs[-1]
    depth = shards[0].shape[0]
    value = refs[len(steps)][...] if before else None
    for step, shard in zip(steps, shards):
        cols = pl.ds(pl.multiple_of((where[0] ^ step) * depth, depth), depth)
        part = jnp.dot(a_ref[:, cols], shard[...], preferred_element_type=jnp.float32)
        value = part if value is None else value + part
    out_ref[...] = value.astype(out_ref.dtype)


def forward(where, dense, shards, steps, before, kind):
    rows, width = dense.shape[0], shards[0].shape[1]
    operands = [near(x) for x in [dense, *[shards[s] for s in steps], *before]]
    return pl.pallas_call(
        functools.partial(forward_kernel, steps=steps, before=bool(before)),
        out_shape=pltpu.VMEM((rows, width), kind),
        in_specs=[SCALARS] + [WHOLE] * len(operands),
        out_specs=WHOLE,
        compiler_params=params(10),
        cost_estimate=cost(2 * dense.size * width, dense.size * 2),
        name="forward_rows",
    )(where, *operands)


def middle_kernel(*refs, scale, came):
    parts = refs[: came + 1]
    weight_ref, up_ref, hidden_ref, grad_ref, wgrad_ref = refs[came + 1 :]
    agg = parts[0][...].astype(jnp.float32)
    for part in parts[1:]:
        agg = agg + part[...].astype(jnp.float32)
    agg = agg.astype(jnp.bfloat16)
    weight = weight_ref[...]
    pre = jnp.dot(agg, weight, preferred_element_type=jnp.float32)
    sig = jax.nn.sigmoid(pre)
    hidden_ref[...] = (pre * sig).astype(jnp.bfloat16)
    pre_grad = (up_ref[...].astype(jnp.float32) * sig * (1.0 + pre * (1.0 - sig))).astype(jnp.bfloat16)
    grad_ref[...] = lax.dot_general(
        weight, pre_grad, (((1,), (1,)), ((), ())), preferred_element_type=jnp.float32
    ).astype(jnp.bfloat16)
    wgrad_ref[...] = scale * lax.dot_general(
        agg, pre_grad, (((0,), (0,)), ((), ())), preferred_element_type=jnp.float32
    )


def middle(parts, weight, upstream, scale):
    rows, width = upstream.shape
    return pl.pallas_call(
        functools.partial(middle_kernel, scale=scale, came=len(parts) - 1),
        out_shape=(
            jax.ShapeDtypeStruct((rows, width), jnp.bfloat16),
            jax.ShapeDtypeStruct((width, rows), jnp.bfloat16),
            jax.ShapeDtypeStruct((width, width), jnp.float32),
        ),
        compiler_params=params(16),
        cost_estimate=cost(6 * rows * width * width, 10 * rows * width, rows * width),
        name="middle",
    )(*parts, weight, upstream)


def backward_kernel(where, *refs, count, steps, before):
    dense, pieces = refs[:count], refs[count : 2 * count]
    out_ref = refs[-1]
    depth = out_ref.shape[2]

    for j, step in enumerate(steps):
        cols = pl.ds(pl.multiple_of((where[0] ^ step) * depth, depth), depth)
        value = refs[2 * count][step] if before else None
        for a_ref, piece in zip(dense, pieces):
            part = jnp.dot(piece[...], a_ref[:, cols], preferred_element_type=jnp.float32)
            value = part if value is None else value + part
        out_ref[j] = value.astype(out_ref.dtype)


def backward(where, dense, pieces, steps, depth, before, kind, after=()):
    count = len(pieces)
    width, _ = pieces[0].shape
    operands = [near(x) for x in [*dense, *pieces] + ([] if before is None else [before])]
    return pl.pallas_call(
        functools.partial(backward_kernel, count=count, steps=steps, before=before is not None),
        out_shape=pltpu.VMEM((len(steps), width, depth), kind),
        in_specs=[SCALARS] + [WHOLE] * len(operands) + [UNREAD] * len(after),
        out_specs=WHOLE,
        compiler_params=params(10),
        cost_estimate=cost(0, 0),
        name="backward_cols",
    )(where, *operands, *after)


def meet_kernel(where, kept_ref, came_ref, own_ref, corner_ref, first_ref, second_ref):
    core = where[0] & 1
    own_ref[...] = kept_ref[0] + came_ref[0].astype(jnp.float32)
    corner_ref[...] = (kept_ref[3] + came_ref[3].astype(jnp.float32)).astype(corner_ref.dtype)
    first_ref[...] = (kept_ref[1 + core] + came_ref[1 + core].astype(jnp.float32)).astype(first_ref.dtype)
    second_ref[...] = kept_ref[2 - core] + came_ref[2 - core].astype(jnp.float32)


def meet(where, kept, came):
    shape = kept.shape[1:]
    kinds = [jnp.float32, came.dtype, came.dtype, jnp.float32]
    return pl.pallas_call(
        meet_kernel,
        out_shape=[pltpu.VMEM(shape, kind) for kind in kinds],
        in_specs=[SCALARS, WHOLE, WHOLE],
        out_specs=[WHOLE] * 4,
        compiler_params=params(10),
        cost_estimate=cost(0, 0),
        name="meet",
    )(where, near(kept), near(came))


def finish_kernel(*refs):
    parts, out_ref = refs[:-1], refs[-1]
    value = parts[0][...].astype(jnp.float32)
    for part in parts[1:]:
        value = value + part[...].astype(jnp.float32)
    out_ref[...] = value.astype(out_ref.dtype).T


def finish(parts):
    width, rows = parts[0].shape
    return pl.pallas_call(
        finish_kernel,
        out_shape=jax.ShapeDtypeStruct((rows, width), jnp.bfloat16),
        compiler_params=params(12),
        cost_estimate=cost(len(parts) * rows * width, 4 * len(parts) * rows * width),
        name="finish",
    )(*parts)


def gate(values, after):
    count = len(values)
    return pl.pallas_call(
        lambda *refs: None,
        out_shape=[pltpu.VMEM(x.shape, x.dtype) for x in values],
        in_specs=[WHOLE] * count + [UNREAD] * len(after),
        out_specs=[WHOLE] * count,
        input_output_aliases={i: i for i in range(count)},
        compiler_params=params(4),
        cost_estimate=cost(0, 0),
        name="gate",
    )(*map(near, values), *after)


def total_kernel(*refs, count):
    parts, out_ref = refs[:count], refs[-1]
    rows = out_ref.shape[0]
    value = None
    for part in parts:
        for i in range(part.shape[0] // rows):
            term = part[pl.ds(i * rows, rows), :].astype(jnp.float32)
            value = term if value is None else value + term
    out_ref[...] = value.astype(out_ref.dtype)


def total(parts, rows, kind, after=()):
    return pl.pallas_call(
        functools.partial(total_kernel, count=len(parts)),
        out_shape=jax.ShapeDtypeStruct((rows, parts[0].shape[1]), kind),
        in_specs=[WHOLE] * len(parts) + [UNREAD] * len(after),
        compiler_params=params(10),
        cost_estimate=cost(0, 0),
        name="total",
    )(*parts, *after)


def swap(value, axis, size, step):
    return lax.ppermute(value, axis, [(i, i ^ step) for i in range(size)])


def shards(adj_tiles, tile_counts, tile_cols, features, weight, upstream):
    n_row, n_col = lax.axis_size("row"), lax.axis_size("col")
    assert n_row & (n_row - 1) == 0 and n_col & (n_col - 1) == 0 and n_row > 1
    adj, counts, cols = adj_tiles[0, 0], tile_counts[0, 0], tile_cols[0, 0]
    rows, depth = upstream.shape[0], features.shape[0]
    col_tiles = depth * n_row // adj.shape[1]
    chips = n_row // 2
    where = jnp.stack([lax.axis_index("row"), lax.axis_index("col")]).astype(jnp.int32)
    line = n_col == 4
    steps = [*range(n_col - 1, 0, -1), 0]

    *blocks, near_features = dense_rows(where, steps, counts, cols, adj, features, rows, col_tiles)
    dense = dict(zip(steps, blocks))

    far = n_col - 1
    every = list(range(n_row))
    away = gate([swap(features, "row", n_row, 2 * c) for c in range(chips - 1, 0, -1)], blocks)[::-1]
    parts = {0: near_features, 1: swap(features, "row", n_row, 1)}
    for c, shard in enumerate(away, 1):
        parts.update({2 * c: shard, 2 * c + 1: swap(shard, "row", n_row, 1)})

    half = forward(where, dense[far], parts, every[::2], [], jnp.float32)
    first = forward(where, dense[far], parts, every[1::2], [half], jnp.bfloat16)
    shares = {far: first}
    for s in steps[1:-1]:
        shares[s] = forward(where, dense[s], parts, every, [], jnp.bfloat16)
    if line:
        relayed = lax.ppermute(shares[3], "col", [(0, 1), (3, 2)])
        came = [lax.ppermute(shares[3], "col", [(1, 2), (2, 1)])]
        joined = (shares[2].astype(jnp.float32) + relayed.astype(jnp.float32)).astype(jnp.bfloat16)
        came += [swap(joined, "col", n_col, 2), swap(shares[1], "col", n_col, 1)]
    else:
        came = [swap(share, "col", n_col, s) for s, share in shares.items()]
    mine = forward(where, dense[0], parts, every, [], jnp.float32)
    scale = 1.0 / math.sqrt(rows * n_row * n_col)
    hidden, piece, part = middle([mine, *came], weight, upstream, scale)

    cores = [[i for i in range(n_row) if i % 2 == core] for core in range(2)]
    part = (part + swap(part, "row", n_row, 1)).astype(jnp.bfloat16)
    gathered = lax.all_gather(part, "row", axis_index_groups=cores, tiled=True)
    part = total([gathered], part.shape[0], jnp.bfloat16)
    if line:
        pieces = {s: swap(piece, "col", n_col, s) for s in (1, 2)}
        pieces[0], pieces[2] = gate([piece, pieces[2]], [part])
        beside = lax.ppermute(pieces[0], "col", [(1, 2), (2, 1)])
        pieces[3] = beside + lax.ppermute(pieces[2], "col", [(1, 0), (2, 3)])
    else:
        pieces = {s: swap(piece, "col", n_col, s) for s in steps[:-1]}
        pieces[0] = piece

    sums, latest = None, n_col - 1
    for group in [list(range(n_col - 1))]:
        sums = backward(where, [dense[s] for s in group], [pieces[s] for s in group], every, depth, sums, jnp.float32)
    last = functools.partial(backward, where, [dense[latest]], [pieces[latest]])
    sent = last(every[1::2], depth, sums, jnp.bfloat16, [part])
    kept = last(every[::2], depth, sums, jnp.float32)
    came = swap(sent, "row", n_row, 1)
    if chips == 4:
        own, corner, first, second = meet(where, kept, came)
        there = [(i, i ^ (2 if i % 2 == 0 else 4)) for i in range(n_row)]
        across = [(i, i ^ (4 if i % 2 == 0 else 2)) for i in range(n_row)]
        corner = lax.ppermute(corner, "row", there)
        second = (second + corner.astype(jnp.float32)).astype(jnp.bfloat16)
        parts = [lax.ppermute(first, "row", there), lax.ppermute(second, "row", across)]
    else:
        own, *summed = [kept[c] + came[c].astype(jnp.float32) for c in range(chips)]
        parts = [swap(summed[c - 1].astype(jnp.bfloat16), "row", n_row, 2 * c) for c in range(1, chips)]

    feature_grad = finish([own, *parts])
    for s in range(n_col.bit_length() - 2):
        part = total([part, swap(part, "col", n_col, 1 << s)], part.shape[0], jnp.bfloat16, [kept])
    came = swap(part, "col", n_col, n_col // 2)
    weight_grad = total([part, came], part.shape[0], jnp.float32)
    return hidden, weight_grad, feature_grad


def solution(mesh):
    placed = (
        P("row", "col", None, None, None),
        P("row", "col", None),
        P("row", "col", None),
        P(("col", "row"), None),
        P(),
        P(("row", "col"), None),
    )
    return jax.shard_map(
        shards,
        mesh=mesh,
        in_specs=placed,
        out_specs=(P(("row", "col"), None), P(), P(("col", "row"), None)),
        check_vma=False,
    )
```

```python
import functools
import math

import jax
import jax.numpy as jnp
from jax import lax
from jax.experimental import pallas as pl
from jax.experimental.pallas import tpu as pltpu
from jax.sharding import PartitionSpec as P


MIB = 1024 * 1024
SCALARS = pl.BlockSpec(memory_space=pltpu.SMEM)
WHOLE = pl.BlockSpec(memory_space=pltpu.VMEM)
UNREAD = pl.BlockSpec(memory_space=pl.ANY)


def params(mib):
    return pltpu.CompilerParams(vmem_limit_bytes=mib * MIB)


def cost(flops, moved, exps=0):
    return pl.CostEstimate(flops=flops, bytes_accessed=moved, transcendentals=exps)


def near(value):
    return pltpu.with_memory_space_constraint(value, pltpu.VMEM)


def dense_kernel(where, counts, cols, adj_ref, features_ref, *refs, steps, window):
    outs, (copied_ref, held, total, sems) = refs[: len(steps)], refs[len(steps) :]
    slots, tile, _ = adj_ref.shape
    per = outs[0].shape[0] // tile
    width = outs[0].shape[1]

    plans = []
    for i, step in enumerate(steps):
        first = (where[1] ^ step) * per
        start = lax.fori_loop(0, first, lambda t, s: s + counts[t], jnp.int32(0))
        for u in range(per):
            count = counts[first + u]
            base = jnp.minimum(start, slots - window)
            fetch = pltpu.make_async_copy(
                adj_ref.at[pl.ds(base, window)], held.at[i * per + u], sems.at[i * per + u]
            )
            fetch.start()
            plans.append((start, start - base, count, fetch))
            start = start + count
    copied = pltpu.make_async_copy(features_ref, copied_ref, sems.at[len(plans)])
    copied.start()

    for i, out_ref in enumerate(outs):
        out_ref[...] = jnp.zeros_like(out_ref)
    for n, (start, shift, count, fetch) in enumerate(plans):
        out_ref = outs[n // per]
        rows = pl.ds((n % per) * tile, tile)
        fetch.wait()

        def place(j):
            c = cols[start + j]
            out_ref[rows, pl.ds(pl.multiple_of(c * tile, tile), tile)] = held[n, shift + j]
            return lax.shift_left(jnp.int32(1), c)

        def four(i, state):
            seen, twice = state
            for v in range(4):
                bit = place(4 * i + v)
                twice = twice | (seen & bit)
                seen = seen | bit
            return seen, twice

        def one(j, state):
            seen, twice = state
            bit = place(j)
            return seen | bit, twice | (seen & bit)

        groups = lax.div(count, 4)
        state = lax.fori_loop(0, groups, four, (jnp.int32(0), jnp.int32(0)))
        seen, twice = lax.fori_loop(4 * groups, count, one, state)
        repeated = (twice != 0) if width // tile <= 32 else (count > 0)

        @pl.when(repeated)
        def _():
            total[...] = jnp.zeros_like(total)

            def add(j, carry):
                here = pl.ds(pl.multiple_of(cols[start + j] * tile, tile), tile)
                total[:, here] += held[n, shift + j].astype(jnp.float32)
                return carry

            lax.fori_loop(0, count, add, 0)
            out_ref[rows, :] = total[...].astype(out_ref.dtype)

    copied.wait()


def dense_rows(where, steps, counts, cols, adj, features, rows, col_tiles):
    slots, tile, _ = adj.shape
    window = min(col_tiles, slots)
    width = col_tiles * tile
    tiles = rows // tile * len(steps)
    return pl.pallas_call(
        functools.partial(dense_kernel, steps=steps, window=window),
        out_shape=[pltpu.VMEM((rows, width), adj.dtype) for _ in steps]
        + [pltpu.VMEM(features.shape, features.dtype)],
        in_specs=[SCALARS] * 3 + [pl.BlockSpec(memory_space=pltpu.HBM)] * 2,
        out_specs=[WHOLE] * (len(steps) + 1),
        scratch_shapes=[
            pltpu.VMEM((tiles, window, tile, tile), adj.dtype),
            pltpu.VMEM((tile, width), jnp.float32),
            pltpu.SemaphoreType.DMA((tiles + 1,)),
        ],
        compiler_params=params(26),
        cost_estimate=cost(0, 5 * len(steps) * rows * width),
        name="dense_rows",
    )(where, *[pltpu.with_memory_space_constraint(x, pltpu.HBM) for x in (counts, cols, adj, features)])


def forward_kernel(where, a_ref, *refs, steps, before):
    shards, out_ref = refs[: len(steps)], refs[-1]
    depth = shards[0].shape[0]
    value = refs[len(steps)][...] if before else None
    for step, shard in zip(steps, shards):
        cols = pl.ds(pl.multiple_of((where[0] ^ step) * depth, depth), depth)
        part = jnp.dot(a_ref[:, cols], shard[...], preferred_element_type=jnp.float32)
        value = part if value is None else value + part
    out_ref[...] = value.astype(out_ref.dtype)


def forward(where, dense, shards, steps, before, kind):
    rows, width = dense.shape[0], shards[0].shape[1]
    operands = [near(x) for x in [dense, *[shards[s] for s in steps], *before]]
    return pl.pallas_call(
        functools.partial(forward_kernel, steps=steps, before=bool(before)),
        out_shape=pltpu.VMEM((rows, width), kind),
        in_specs=[SCALARS] + [WHOLE] * len(operands),
        out_specs=WHOLE,
        compiler_params=params(10),
        cost_estimate=cost(2 * dense.size * width, dense.size * 2),
        name="forward_rows",
    )(where, *operands)


def middle_kernel(*refs, scale, came):
    parts = refs[: came + 1]
    weight_ref, up_ref, hidden_ref, grad_ref, wgrad_ref = refs[came + 1 :]
    agg = parts[0][...].astype(jnp.float32)
    for part in parts[1:]:
        agg = agg + part[...].astype(jnp.float32)
    agg = agg.astype(jnp.bfloat16)
    weight = weight_ref[...]
    pre = jnp.dot(agg, weight, preferred_element_type=jnp.float32)
    sig = jax.nn.sigmoid(pre)
    hidden_ref[...] = (pre * sig).astype(jnp.bfloat16)
    pre_grad = (up_ref[...].astype(jnp.float32) * sig * (1.0 + pre * (1.0 - sig))).astype(jnp.bfloat16)
    grad_ref[...] = lax.dot_general(
        weight, pre_grad, (((1,), (1,)), ((), ())), preferred_element_type=jnp.float32
    ).astype(jnp.bfloat16)
    wgrad_ref[...] = scale * lax.dot_general(
        agg, pre_grad, (((0,), (0,)), ((), ())), preferred_element_type=jnp.float32
    )


def middle(parts, weight, upstream, scale):
    rows, width = upstream.shape
    return pl.pallas_call(
        functools.partial(middle_kernel, scale=scale, came=len(parts) - 1),
        out_shape=(
            jax.ShapeDtypeStruct((rows, width), jnp.bfloat16),
            jax.ShapeDtypeStruct((width, rows), jnp.bfloat16),
            jax.ShapeDtypeStruct((width, width), jnp.float32),
        ),
        compiler_params=params(16),
        cost_estimate=cost(6 * rows * width * width, 10 * rows * width, rows * width),
        name="middle",
    )(*parts, weight, upstream)


def backward_kernel(where, *refs, count, steps, before):
    dense, pieces = refs[:count], refs[count : 2 * count]
    out_ref = refs[-1]
    depth = out_ref.shape[2]

    for j, step in enumerate(steps):
        cols = pl.ds(pl.multiple_of((where[0] ^ step) * depth, depth), depth)
        value = refs[2 * count][step] if before else None
        for a_ref, piece in zip(dense, pieces):
            part = jnp.dot(piece[...], a_ref[:, cols], preferred_element_type=jnp.float32)
            value = part if value is None else value + part
        out_ref[j] = value.astype(out_ref.dtype)


def backward(where, dense, pieces, steps, depth, before, kind, after=()):
    count = len(pieces)
    width, _ = pieces[0].shape
    operands = [near(x) for x in [*dense, *pieces] + ([] if before is None else [before])]
    return pl.pallas_call(
        functools.partial(backward_kernel, count=count, steps=steps, before=before is not None),
        out_shape=pltpu.VMEM((len(steps), width, depth), kind),
        in_specs=[SCALARS] + [WHOLE] * len(operands) + [UNREAD] * len(after),
        out_specs=WHOLE,
        compiler_params=params(10),
        cost_estimate=cost(0, 0),
        name="backward_cols",
    )(where, *operands, *after)


def meet_kernel(where, kept_ref, came_ref, *refs):
    own_ref, corner_ref, first_ref, second_ref = refs[-4:]
    core = where[0] & 1
    own_ref[...] = kept_ref[0] + came_ref[0].astype(jnp.float32)
    corner_ref[...] = (kept_ref[3] + came_ref[3].astype(jnp.float32)).astype(corner_ref.dtype)
    first_ref[...] = (kept_ref[1 + core] + came_ref[1 + core].astype(jnp.float32)).astype(first_ref.dtype)
    second_ref[...] = kept_ref[2 - core] + came_ref[2 - core].astype(jnp.float32)


def meet(where, kept, came, after):
    shape = kept.shape[1:]
    kinds = [jnp.float32, came.dtype, came.dtype, jnp.float32]
    return pl.pallas_call(
        meet_kernel,
        out_shape=[pltpu.VMEM(shape, kind) for kind in kinds],
        in_specs=[SCALARS, WHOLE, WHOLE] + [UNREAD] * len(after),
        out_specs=[WHOLE] * 4,
        compiler_params=params(10),
        cost_estimate=cost(0, 0),
        name="meet",
    )(where, near(kept), near(came), *after)


def finish_kernel(*refs):
    parts, out_ref = refs[:-1], refs[-1]
    value = parts[0][...].astype(jnp.float32)
    for part in parts[1:]:
        value = value + part[...].astype(jnp.float32)
    out_ref[...] = value.astype(out_ref.dtype).T


def finish(parts):
    width, rows = parts[0].shape
    return pl.pallas_call(
        finish_kernel,
        out_shape=jax.ShapeDtypeStruct((rows, width), jnp.bfloat16),
        compiler_params=params(12),
        cost_estimate=cost(len(parts) * rows * width, 4 * len(parts) * rows * width),
        name="finish",
    )(*parts)


def gate(values, after):
    count = len(values)
    return pl.pallas_call(
        lambda *refs: None,
        out_shape=[pltpu.VMEM(x.shape, x.dtype) for x in values],
        in_specs=[WHOLE] * count + [UNREAD] * len(after),
        out_specs=[WHOLE] * count,
        input_output_aliases={i: i for i in range(count)},
        compiler_params=params(4),
        cost_estimate=cost(0, 0),
        name="gate",
    )(*map(near, values), *after)


def total_kernel(*refs, count):
    parts, out_ref = refs[:count], refs[-1]
    rows = out_ref.shape[0]
    value = None
    for part in parts:
        for i in range(part.shape[0] // rows):
            term = part[pl.ds(i * rows, rows), :].astype(jnp.float32)
            value = term if value is None else value + term
    out_ref[...] = value.astype(out_ref.dtype)


def total(parts, rows, kind, after=()):
    return pl.pallas_call(
        functools.partial(total_kernel, count=len(parts)),
        out_shape=jax.ShapeDtypeStruct((rows, parts[0].shape[1]), kind),
        in_specs=[WHOLE] * len(parts) + [UNREAD] * len(after),
        compiler_params=params(10),
        cost_estimate=cost(0, 0),
        name="total",
    )(*parts, *after)


def half_kernel(where, values_ref, out_ref):
    rows = out_ref.shape[0]
    value = None
    for i in range(values_ref.shape[0] // (2 * rows)):
        at = pl.ds(pl.multiple_of((2 * i + (where[0] & 1)) * rows, rows), rows)
        term = values_ref[at, :].astype(jnp.float32)
        value = term if value is None else value + term
    out_ref[...] = value.astype(out_ref.dtype)


def half_total(where, values, rows):
    return pl.pallas_call(
        half_kernel,
        out_shape=jax.ShapeDtypeStruct((rows, values.shape[1]), values.dtype),
        in_specs=[SCALARS, WHOLE],
        compiler_params=params(10),
        cost_estimate=cost(0, 0),
        name="half_total",
    )(where, values)


def join_kernel(where, own_ref, *refs):
    others, out_ref = refs[:-1], refs[-1]
    rows = own_ref.shape[0]
    core = where[0] & 1
    out_ref[pl.ds(pl.multiple_of(core * rows, rows), rows), :] = own_ref[...]
    part = rows // len(others)
    for i, other_ref in enumerate(others):
        out_ref[pl.ds(pl.multiple_of((1 - core) * rows + i * part, part), part), :] = other_ref[...]


def join(where, own, *others):
    rows, width = own.shape
    return pl.pallas_call(
        join_kernel,
        out_shape=jax.ShapeDtypeStruct((2 * rows, width), own.dtype),
        in_specs=[SCALARS] + [WHOLE] * (1 + len(others)),
        compiler_params=params(10),
        cost_estimate=cost(0, 0),
        name="join",
    )(where, own, *others)


def swap(value, axis, size, step):
    return lax.ppermute(value, axis, [(i, i ^ step) for i in range(size)])


def shards(adj_tiles, tile_counts, tile_cols, features, weight, upstream):
    n_row, n_col = lax.axis_size("row"), lax.axis_size("col")
    assert n_row & (n_row - 1) == 0 and n_col & (n_col - 1) == 0 and n_row > 1
    adj, counts, cols = adj_tiles[0, 0], tile_counts[0, 0], tile_cols[0, 0]
    rows, depth = upstream.shape[0], features.shape[0]
    col_tiles = depth * n_row // adj.shape[1]
    chips = n_row // 2
    where = jnp.stack([lax.axis_index("row"), lax.axis_index("col")]).astype(jnp.int32)
    line = n_col == 4
    steps = [*range(n_col - 1, 0, -1), 0]

    *blocks, near_features = dense_rows(where, steps, counts, cols, adj, features, rows, col_tiles)
    dense = dict(zip(steps, blocks))

    far = n_col - 1
    every = list(range(n_row))
    away = gate([swap(features, "row", n_row, 2 * c) for c in range(chips - 1, 0, -1)], blocks)[::-1]
    parts = {0: near_features, 1: swap(features, "row", n_row, 1)}
    for c, shard in enumerate(away, 1):
        parts.update({2 * c: shard, 2 * c + 1: swap(shard, "row", n_row, 1)})

    half = forward(where, dense[far], parts, every[::2], [], jnp.float32)
    first = forward(where, dense[far], parts, every[1::2], [half], jnp.bfloat16)
    shares = {far: first}
    for s in steps[1:-1]:
        shares[s] = forward(where, dense[s], parts, every, [], jnp.bfloat16)
    if line:
        relayed = lax.ppermute(shares[3], "col", [(0, 1), (3, 2)])
        came = [lax.ppermute(shares[3], "col", [(1, 2), (2, 1)])]
        joined = (shares[2].astype(jnp.float32) + relayed.astype(jnp.float32)).astype(jnp.bfloat16)
        came += [swap(joined, "col", n_col, 2), swap(shares[1], "col", n_col, 1)]
    else:
        came = [swap(share, "col", n_col, s) for s, share in shares.items()]
    mine = forward(where, dense[0], parts, every, [], jnp.float32)
    scale = 1.0 / math.sqrt(rows * n_row * n_col)
    hidden, piece, part = middle([mine, *came], weight, upstream, scale)

    cores = [[i for i in range(n_row) if i % 2 == core] for core in range(2)]
    part = (part + swap(part, "row", n_row, 1)).astype(jnp.bfloat16)
    gathered = lax.all_gather(part, "row", axis_index_groups=cores, tiled=True)
    part = half_total(where, gathered, part.shape[0] // 2)
    if line:
        pieces = {s: swap(piece, "col", n_col, s) for s in (1, 2)}
        pieces[0], pieces[2] = gate([piece, pieces[2]], [part])
        beside = lax.ppermute(pieces[0], "col", [(1, 2), (2, 1)])
        pieces[3] = beside + lax.ppermute(pieces[2], "col", [(1, 0), (2, 3)])
    else:
        pieces = {s: swap(piece, "col", n_col, s) for s in steps[:-1]}
        pieces[0] = piece

    sums, latest = None, n_col - 1
    for group in [list(range(n_col - 1))]:
        sums = backward(where, [dense[s] for s in group], [pieces[s] for s in group], every, depth, sums, jnp.float32)
    last = functools.partial(backward, where, [dense[latest]], [pieces[latest]])
    sent = last(every[1::2], depth, sums, jnp.bfloat16, [part])
    kept = last(every[::2], depth, sums, jnp.float32)
    came = swap(sent, "row", n_row, 1)
    for s in range(n_col.bit_length() - 2):
        part = total([part, swap(part, "col", n_col, 1 << s)], part.shape[0], jnp.bfloat16, [sent])
    after = []
    if chips == 4:
        own, corner, first, second = meet(where, kept, came, [part])
        there = [(i, i ^ (2 if i % 2 == 0 else 4)) for i in range(n_row)]
        across = [(i, i ^ (4 if i % 2 == 0 else 2)) for i in range(n_row)]
        corner = lax.ppermute(corner, "row", there)
        second = (second + corner.astype(jnp.float32)).astype(jnp.bfloat16)
        after = [second]
        parts = [lax.ppermute(first, "row", there), lax.ppermute(second, "row", across)]
    else:
        own, *summed = [kept[c] + came[c].astype(jnp.float32) for c in range(chips)]
        parts = [swap(summed[c - 1].astype(jnp.bfloat16), "row", n_row, 2 * c) for c in range(1, chips)]

    feature_grad = finish([own, *parts])
    part = total([part, swap(part, "col", n_col, n_col // 2)], part.shape[0], jnp.float32, after)
    top, low = part[: part.shape[0] // 2], part[part.shape[0] // 2 :]
    top_came = swap(top, "row", n_row, 1)
    low_came = swap(gate([low], [top_came])[0], "row", n_row, 1)
    weight_grad = join(where, part, top_came, low_came)
    return hidden, weight_grad, feature_grad


def solution(mesh):
    placed = (
        P("row", "col", None, None, None),
        P("row", "col", None),
        P("row", "col", None),
        P(("col", "row"), None),
        P(),
        P(("row", "col"), None),
    )
    return jax.shard_map(
        shards,
        mesh=mesh,
        in_specs=placed,
        out_specs=(P(("row", "col"), None), P(), P(("col", "row"), None)),
        check_vma=False,
    )
```

```python
import functools
import math

import jax
import jax.numpy as jnp
from jax import lax
from jax.experimental import pallas as pl
from jax.experimental.pallas import tpu as pltpu
from jax.sharding import PartitionSpec as P


MIB = 1024 * 1024
SCALARS = pl.BlockSpec(memory_space=pltpu.SMEM)
WHOLE = pl.BlockSpec(memory_space=pltpu.VMEM)
UNREAD = pl.BlockSpec(memory_space=pl.ANY)


def params(mib):
    return pltpu.CompilerParams(vmem_limit_bytes=mib * MIB)


def cost(flops, moved, exps=0):
    return pl.CostEstimate(flops=flops, bytes_accessed=moved, transcendentals=exps)


def near(value):
    return pltpu.with_memory_space_constraint(value, pltpu.VMEM)


def dense_kernel(where, counts, cols, adj_ref, features_ref, *refs, steps, window):
    outs, (copied_ref, held, total, sems) = refs[: len(steps)], refs[len(steps) :]
    slots, tile, _ = adj_ref.shape
    per = outs[0].shape[0] // tile
    width = outs[0].shape[1]

    plans = []
    for i, step in enumerate(steps):
        first = (where[1] ^ step) * per
        start = lax.fori_loop(0, first, lambda t, s: s + counts[t], jnp.int32(0))
        for u in range(per):
            count = counts[first + u]
            base = jnp.minimum(start, slots - window)
            fetch = pltpu.make_async_copy(
                adj_ref.at[pl.ds(base, window)], held.at[i * per + u], sems.at[i * per + u]
            )
            fetch.start()
            plans.append((start, start - base, count, fetch))
            start = start + count
    copied = pltpu.make_async_copy(features_ref, copied_ref, sems.at[len(plans)])
    copied.start()

    for i, out_ref in enumerate(outs):
        out_ref[...] = jnp.zeros_like(out_ref)
    for n, (start, shift, count, fetch) in enumerate(plans):
        out_ref = outs[n // per]
        rows = pl.ds((n % per) * tile, tile)
        fetch.wait()

        def place(j):
            c = cols[start + j]
            out_ref[rows, pl.ds(pl.multiple_of(c * tile, tile), tile)] = held[n, shift + j]
            return lax.shift_left(jnp.int32(1), c)

        def four(i, state):
            seen, twice = state
            for v in range(4):
                bit = place(4 * i + v)
                twice = twice | (seen & bit)
                seen = seen | bit
            return seen, twice

        def one(j, state):
            seen, twice = state
            bit = place(j)
            return seen | bit, twice | (seen & bit)

        groups = lax.div(count, 4)
        state = lax.fori_loop(0, groups, four, (jnp.int32(0), jnp.int32(0)))
        seen, twice = lax.fori_loop(4 * groups, count, one, state)
        repeated = (twice != 0) if width // tile <= 32 else (count > 0)

        @pl.when(repeated)
        def _():
            total[...] = jnp.zeros_like(total)

            def add(j, carry):
                here = pl.ds(pl.multiple_of(cols[start + j] * tile, tile), tile)
                total[:, here] += held[n, shift + j].astype(jnp.float32)
                return carry

            lax.fori_loop(0, count, add, 0)
            out_ref[rows, :] = total[...].astype(out_ref.dtype)

    copied.wait()


def dense_rows(where, steps, counts, cols, adj, features, rows, col_tiles):
    slots, tile, _ = adj.shape
    window = min(col_tiles, slots)
    width = col_tiles * tile
    tiles = rows // tile * len(steps)
    return pl.pallas_call(
        functools.partial(dense_kernel, steps=steps, window=window),
        out_shape=[pltpu.VMEM((rows, width), adj.dtype) for _ in steps]
        + [pltpu.VMEM(features.shape, features.dtype)],
        in_specs=[SCALARS] * 3 + [pl.BlockSpec(memory_space=pltpu.HBM)] * 2,
        out_specs=[WHOLE] * (len(steps) + 1),
        scratch_shapes=[
            pltpu.VMEM((tiles, window, tile, tile), adj.dtype),
            pltpu.VMEM((tile, width), jnp.float32),
            pltpu.SemaphoreType.DMA((tiles + 1,)),
        ],
        compiler_params=params(26),
        cost_estimate=cost(0, 5 * len(steps) * rows * width),
        name="dense_rows",
    )(where, *[pltpu.with_memory_space_constraint(x, pltpu.HBM) for x in (counts, cols, adj, features)])


def forward_kernel(where, a_ref, *refs, steps, before):
    shards, out_ref = refs[: len(steps)], refs[-1]
    depth = shards[0].shape[0]
    value = refs[len(steps)][...] if before else None
    for step, shard in zip(steps, shards):
        cols = pl.ds(pl.multiple_of((where[0] ^ step) * depth, depth), depth)
        part = jnp.dot(a_ref[:, cols], shard[...], preferred_element_type=jnp.float32)
        value = part if value is None else value + part
    out_ref[...] = value.astype(out_ref.dtype)


def forward(where, dense, shards, steps, before, kind):
    rows, width = dense.shape[0], shards[0].shape[1]
    operands = [near(x) for x in [dense, *[shards[s] for s in steps], *before]]
    return pl.pallas_call(
        functools.partial(forward_kernel, steps=steps, before=bool(before)),
        out_shape=pltpu.VMEM((rows, width), kind),
        in_specs=[SCALARS] + [WHOLE] * len(operands),
        out_specs=WHOLE,
        compiler_params=params(10),
        cost_estimate=cost(2 * dense.size * width, dense.size * 2),
        name="forward_rows",
    )(where, *operands)


def middle_kernel(*refs, scale, came):
    parts = refs[: came + 1]
    weight_ref, up_ref, hidden_ref, grad_ref, wgrad_ref = refs[came + 1 :]
    agg = parts[0][...].astype(jnp.float32)
    for part in parts[1:]:
        agg = agg + part[...].astype(jnp.float32)
    agg = agg.astype(jnp.bfloat16)
    weight = weight_ref[...]
    pre = jnp.dot(agg, weight, preferred_element_type=jnp.float32)
    sig = jax.nn.sigmoid(pre)
    hidden_ref[...] = (pre * sig).astype(jnp.bfloat16)
    pre_grad = (up_ref[...].astype(jnp.float32) * sig * (1.0 + pre * (1.0 - sig))).astype(jnp.bfloat16)
    grad_ref[...] = lax.dot_general(
        weight, pre_grad, (((1,), (1,)), ((), ())), preferred_element_type=jnp.float32
    ).astype(jnp.bfloat16)
    wgrad_ref[...] = scale * lax.dot_general(
        agg, pre_grad, (((0,), (0,)), ((), ())), preferred_element_type=jnp.float32
    )


def middle(parts, weight, upstream, scale):
    rows, width = upstream.shape
    return pl.pallas_call(
        functools.partial(middle_kernel, scale=scale, came=len(parts) - 1),
        out_shape=(
            jax.ShapeDtypeStruct((rows, width), jnp.bfloat16),
            jax.ShapeDtypeStruct((width, rows), jnp.bfloat16),
            jax.ShapeDtypeStruct((width, width), jnp.float32),
        ),
        compiler_params=params(16),
        cost_estimate=cost(6 * rows * width * width, 10 * rows * width, rows * width),
        name="middle",
    )(*parts, weight, upstream)


def backward_kernel(where, *refs, count, steps, before):
    dense, pieces = refs[:count], refs[count : 2 * count]
    out_ref = refs[-1]
    depth = out_ref.shape[2]

    for j, step in enumerate(steps):
        cols = pl.ds(pl.multiple_of((where[0] ^ step) * depth, depth), depth)
        value = refs[2 * count][step] if before else None
        for a_ref, piece in zip(dense, pieces):
            part = jnp.dot(piece[...], a_ref[:, cols], preferred_element_type=jnp.float32)
            value = part if value is None else value + part
        out_ref[j] = value.astype(out_ref.dtype)


def backward(where, dense, pieces, steps, depth, before, kind, after=()):
    count = len(pieces)
    width, _ = pieces[0].shape
    operands = [near(x) for x in [*dense, *pieces] + ([] if before is None else [before])]
    return pl.pallas_call(
        functools.partial(backward_kernel, count=count, steps=steps, before=before is not None),
        out_shape=pltpu.VMEM((len(steps), width, depth), kind),
        in_specs=[SCALARS] + [WHOLE] * len(operands) + [UNREAD] * len(after),
        out_specs=WHOLE,
        compiler_params=params(10),
        cost_estimate=cost(0, 0),
        name="backward_cols",
    )(where, *operands, *after)


def meet_kernel(where, kept_ref, came_ref, *refs):
    own_ref, corner_ref, first_ref, second_ref = refs[-4:]
    core = where[0] & 1
    own_ref[...] = kept_ref[0] + came_ref[0].astype(jnp.float32)
    corner_ref[...] = (kept_ref[3] + came_ref[3].astype(jnp.float32)).astype(corner_ref.dtype)
    first_ref[...] = (kept_ref[1 + core] + came_ref[1 + core].astype(jnp.float32)).astype(first_ref.dtype)
    second_ref[...] = kept_ref[2 - core] + came_ref[2 - core].astype(jnp.float32)


def meet(where, kept, came, after):
    shape = kept.shape[1:]
    kinds = [jnp.float32, came.dtype, came.dtype, jnp.float32]
    return pl.pallas_call(
        meet_kernel,
        out_shape=[pltpu.VMEM(shape, kind) for kind in kinds],
        in_specs=[SCALARS, WHOLE, WHOLE] + [UNREAD] * len(after),
        out_specs=[WHOLE] * 4,
        compiler_params=params(10),
        cost_estimate=cost(0, 0),
        name="meet",
    )(where, near(kept), near(came), *after)


def finish_kernel(*refs):
    parts, out_ref = refs[:-1], refs[-1]
    value = parts[0][...].astype(jnp.float32)
    for part in parts[1:]:
        value = value + part[...].astype(jnp.float32)
    out_ref[...] = value.astype(out_ref.dtype).T


def finish(parts):
    width, rows = parts[0].shape
    return pl.pallas_call(
        finish_kernel,
        out_shape=jax.ShapeDtypeStruct((rows, width), jnp.bfloat16),
        compiler_params=params(12),
        cost_estimate=cost(len(parts) * rows * width, 4 * len(parts) * rows * width),
        name="finish",
    )(*parts)


def gate(values, after):
    count = len(values)
    return pl.pallas_call(
        lambda *refs: None,
        out_shape=[pltpu.VMEM(x.shape, x.dtype) for x in values],
        in_specs=[WHOLE] * count + [UNREAD] * len(after),
        out_specs=[WHOLE] * count,
        input_output_aliases={i: i for i in range(count)},
        compiler_params=params(4),
        cost_estimate=cost(0, 0),
        name="gate",
    )(*map(near, values), *after)


def total_kernel(*refs, count):
    parts, out_ref = refs[:count], refs[-1]
    rows = out_ref.shape[0]
    value = None
    for part in parts:
        for i in range(part.shape[0] // rows):
            term = part[pl.ds(i * rows, rows), :].astype(jnp.float32)
            value = term if value is None else value + term
    out_ref[...] = value.astype(out_ref.dtype)


def total(parts, rows, kind, after=()):
    return pl.pallas_call(
        functools.partial(total_kernel, count=len(parts)),
        out_shape=jax.ShapeDtypeStruct((rows, parts[0].shape[1]), kind),
        in_specs=[WHOLE] * len(parts) + [UNREAD] * len(after),
        compiler_params=params(10),
        cost_estimate=cost(0, 0),
        name="total",
    )(*parts, *after)


def half_kernel(where, values_ref, out_ref):
    rows = out_ref.shape[0]
    value = None
    for i in range(values_ref.shape[0] // (2 * rows)):
        at = pl.ds(pl.multiple_of((2 * i + (where[0] & 1)) * rows, rows), rows)
        term = values_ref[at, :].astype(jnp.float32)
        value = term if value is None else value + term
    out_ref[...] = value.astype(out_ref.dtype)


def half_total(where, values, rows):
    return pl.pallas_call(
        half_kernel,
        out_shape=jax.ShapeDtypeStruct((rows, values.shape[1]), values.dtype),
        in_specs=[SCALARS, WHOLE],
        compiler_params=params(10),
        cost_estimate=cost(0, 0),
        name="half_total",
    )(where, values)


def join_kernel(where, own_ref, *refs):
    others, out_ref = refs[:-1], refs[-1]
    rows = own_ref.shape[0]
    core = where[0] & 1
    out_ref[pl.ds(pl.multiple_of(core * rows, rows), rows), :] = own_ref[...]
    part = rows // len(others)
    for i, other_ref in enumerate(others):
        out_ref[pl.ds(pl.multiple_of((1 - core) * rows + i * part, part), part), :] = other_ref[...]


def join(where, own, *others):
    rows, width = own.shape
    return pl.pallas_call(
        join_kernel,
        out_shape=jax.ShapeDtypeStruct((2 * rows, width), own.dtype),
        in_specs=[SCALARS] + [WHOLE] * (1 + len(others)),
        compiler_params=params(10),
        cost_estimate=cost(0, 0),
        name="join",
    )(where, own, *others)


def swap(value, axis, size, step):
    return lax.ppermute(value, axis, [(i, i ^ step) for i in range(size)])


def shards(adj_tiles, tile_counts, tile_cols, features, weight, upstream):
    n_row, n_col = lax.axis_size("row"), lax.axis_size("col")
    assert n_row & (n_row - 1) == 0 and n_col & (n_col - 1) == 0 and n_row > 1
    adj, counts, cols = adj_tiles[0, 0], tile_counts[0, 0], tile_cols[0, 0]
    rows, depth = upstream.shape[0], features.shape[0]
    col_tiles = depth * n_row // adj.shape[1]
    chips = n_row // 2
    where = jnp.stack([lax.axis_index("row"), lax.axis_index("col")]).astype(jnp.int32)
    line = n_col == 4
    steps = [*range(n_col - 1, 0, -1), 0]

    *blocks, near_features = dense_rows(where, steps, counts, cols, adj, features, rows, col_tiles)
    dense = dict(zip(steps, blocks))

    far = n_col - 1
    every = list(range(n_row))
    away = gate([swap(features, "row", n_row, 2 * c) for c in range(chips - 1, 0, -1)], blocks)[::-1]
    parts = {0: near_features, 1: swap(features, "row", n_row, 1)}
    for c, shard in enumerate(away, 1):
        parts.update({2 * c: shard, 2 * c + 1: swap(shard, "row", n_row, 1)})

    half = forward(where, dense[far], parts, every[::2], [], jnp.float32)
    first = forward(where, dense[far], parts, every[1::2], [half], jnp.bfloat16)
    shares = {far: first}
    for s in steps[1:-1]:
        shares[s] = forward(where, dense[s], parts, every, [], jnp.bfloat16)
    if line:
        relayed = lax.ppermute(shares[3], "col", [(0, 1), (3, 2)])
        came = [lax.ppermute(shares[3], "col", [(1, 2), (2, 1)])]
        joined = (shares[2].astype(jnp.float32) + relayed.astype(jnp.float32)).astype(jnp.bfloat16)
        came += [swap(joined, "col", n_col, 2), swap(shares[1], "col", n_col, 1)]
    else:
        came = [swap(share, "col", n_col, s) for s, share in shares.items()]
    mine = forward(where, dense[0], parts, every, [], jnp.float32)
    scale = 1.0 / math.sqrt(rows * n_row * n_col)
    hidden, piece, part = middle([mine, *came], weight, upstream, scale)

    cores = [[i for i in range(n_row) if i % 2 == core] for core in range(2)]
    part = (part + swap(part, "row", n_row, 1)).astype(jnp.bfloat16)
    gathered = lax.all_gather(part, "row", axis_index_groups=cores, tiled=True)
    part = half_total(where, gathered, part.shape[0] // 2)
    if line:
        pieces = {s: swap(piece, "col", n_col, s) for s in (1, 2)}
        pieces[0], pieces[2], part = gate([piece, pieces[2], part], [])
        beside = lax.ppermute(pieces[0], "col", [(1, 2), (2, 1)])
        pieces[3] = beside + lax.ppermute(pieces[2], "col", [(1, 0), (2, 3)])
    else:
        pieces = {s: swap(piece, "col", n_col, s) for s in steps[:-1]}
        pieces[0] = piece

    sums, latest = None, n_col - 1
    for group in [list(range(n_col - 1))]:
        sums = backward(where, [dense[s] for s in group], [pieces[s] for s in group], every, depth, sums, jnp.float32)
    for s in range(n_col.bit_length() - 2):
        part = total([part, swap(part, "col", n_col, 1 << s)], part.shape[0], jnp.bfloat16)
    last = functools.partial(backward, where, [dense[latest]], [pieces[latest]])
    sent = last(every[1::2], depth, sums, jnp.bfloat16, [part])
    kept = last(every[::2], depth, sums, jnp.float32)
    came = swap(sent, "row", n_row, 1)
    after = []
    if chips == 4:
        own, corner, first, second = meet(where, kept, came, [])
        there = [(i, i ^ (2 if i % 2 == 0 else 4)) for i in range(n_row)]
        across = [(i, i ^ (4 if i % 2 == 0 else 2)) for i in range(n_row)]
        corner = lax.ppermute(corner, "row", there)
        second = (second + corner.astype(jnp.float32)).astype(jnp.bfloat16)
        after = [second]
        parts = [lax.ppermute(first, "row", there), lax.ppermute(second, "row", across)]
    else:
        own, *summed = [kept[c] + came[c].astype(jnp.float32) for c in range(chips)]
        parts = [swap(summed[c - 1].astype(jnp.bfloat16), "row", n_row, 2 * c) for c in range(1, chips)]

    feature_grad = finish([own, *parts])
    part = total([part, swap(part, "col", n_col, n_col // 2)], part.shape[0], jnp.float32, after)
    top, low = part[: part.shape[0] // 2], part[part.shape[0] // 2 :]
    top_came = swap(top, "row", n_row, 1)
    low_came = swap(gate([low], [top_came])[0], "row", n_row, 1)
    weight_grad = join(where, part, top_came, low_came)
    return hidden, weight_grad, feature_grad


def solution(mesh):
    placed = (
        P("row", "col", None, None, None),
        P("row", "col", None),
        P("row", "col", None),
        P(("col", "row"), None),
        P(),
        P(("row", "col"), None),
    )
    return jax.shard_map(
        shards,
        mesh=mesh,
        in_specs=placed,
        out_specs=(P(("row", "col"), None), P(), P(("col", "row"), None)),
        check_vma=False,
    )
```

```python
import functools
import math

import jax
import jax.numpy as jnp
from jax import lax
from jax.experimental import pallas as pl
from jax.experimental.pallas import tpu as pltpu
from jax.sharding import PartitionSpec as P


MIB = 1024 * 1024
SCALARS = pl.BlockSpec(memory_space=pltpu.SMEM)
WHOLE = pl.BlockSpec(memory_space=pltpu.VMEM)
UNREAD = pl.BlockSpec(memory_space=pl.ANY)


def params(mib):
    return pltpu.CompilerParams(vmem_limit_bytes=mib * MIB)


def cost(flops, moved, exps=0):
    return pl.CostEstimate(flops=flops, bytes_accessed=moved, transcendentals=exps)


def near(value):
    return pltpu.with_memory_space_constraint(value, pltpu.VMEM)


def dense_kernel(where, counts, cols, adj_ref, features_ref, *refs, steps, window):
    outs, (copied_ref, held, total, sems) = refs[: len(steps)], refs[len(steps) :]
    slots, tile, _ = adj_ref.shape
    per = outs[0].shape[0] // tile
    width = outs[0].shape[1]

    plans = []
    for i, step in enumerate(steps):
        first = (where[1] ^ step) * per
        start = lax.fori_loop(0, first, lambda t, s: s + counts[t], jnp.int32(0))
        for u in range(per):
            count = counts[first + u]
            base = jnp.minimum(start, slots - window)
            fetch = pltpu.make_async_copy(
                adj_ref.at[pl.ds(base, window)], held.at[i * per + u], sems.at[i * per + u]
            )
            fetch.start()
            plans.append((start, start - base, count, fetch))
            start = start + count
    copied = pltpu.make_async_copy(features_ref, copied_ref, sems.at[len(plans)])
    copied.start()

    for i, out_ref in enumerate(outs):
        out_ref[...] = jnp.zeros_like(out_ref)
    for n, (start, shift, count, fetch) in enumerate(plans):
        out_ref = outs[n // per]
        rows = pl.ds((n % per) * tile, tile)
        fetch.wait()

        def place(j):
            c = cols[start + j]
            out_ref[rows, pl.ds(pl.multiple_of(c * tile, tile), tile)] = held[n, shift + j]
            return lax.shift_left(jnp.int32(1), c)

        def four(i, state):
            seen, twice = state
            for v in range(4):
                bit = place(4 * i + v)
                twice = twice | (seen & bit)
                seen = seen | bit
            return seen, twice

        def one(j, state):
            seen, twice = state
            bit = place(j)
            return seen | bit, twice | (seen & bit)

        groups = lax.div(count, 4)
        state = lax.fori_loop(0, groups, four, (jnp.int32(0), jnp.int32(0)))
        seen, twice = lax.fori_loop(4 * groups, count, one, state)
        repeated = (twice != 0) if width // tile <= 32 else (count > 0)

        @pl.when(repeated)
        def _():
            total[...] = jnp.zeros_like(total)

            def add(j, carry):
                here = pl.ds(pl.multiple_of(cols[start + j] * tile, tile), tile)
                total[:, here] += held[n, shift + j].astype(jnp.float32)
                return carry

            lax.fori_loop(0, count, add, 0)
            out_ref[rows, :] = total[...].astype(out_ref.dtype)

    copied.wait()


def dense_rows(where, steps, counts, cols, adj, features, rows, col_tiles):
    slots, tile, _ = adj.shape
    window = min(col_tiles, slots)
    width = col_tiles * tile
    tiles = rows // tile * len(steps)
    return pl.pallas_call(
        functools.partial(dense_kernel, steps=steps, window=window),
        out_shape=[pltpu.VMEM((rows, width), adj.dtype) for _ in steps]
        + [pltpu.VMEM(features.shape, features.dtype)],
        in_specs=[SCALARS] * 3 + [pl.BlockSpec(memory_space=pltpu.HBM)] * 2,
        out_specs=[WHOLE] * (len(steps) + 1),
        scratch_shapes=[
            pltpu.VMEM((tiles, window, tile, tile), adj.dtype),
            pltpu.VMEM((tile, width), jnp.float32),
            pltpu.SemaphoreType.DMA((tiles + 1,)),
        ],
        compiler_params=params(26),
        cost_estimate=cost(0, 5 * len(steps) * rows * width),
        name="dense_rows",
    )(where, *[pltpu.with_memory_space_constraint(x, pltpu.HBM) for x in (counts, cols, adj, features)])


def forward_kernel(where, a_ref, *refs, steps, before):
    shards, out_ref = refs[: len(steps)], refs[-1]
    depth = shards[0].shape[0]
    value = refs[len(steps)][...] if before else None
    for step, shard in zip(steps, shards):
        cols = pl.ds(pl.multiple_of((where[0] ^ step) * depth, depth), depth)
        part = jnp.dot(a_ref[:, cols], shard[...], preferred_element_type=jnp.float32)
        value = part if value is None else value + part
    out_ref[...] = value.astype(out_ref.dtype)


def forward(where, dense, shards, steps, before, kind):
    rows, width = dense.shape[0], shards[0].shape[1]
    operands = [near(x) for x in [dense, *[shards[s] for s in steps], *before]]
    return pl.pallas_call(
        functools.partial(forward_kernel, steps=steps, before=bool(before)),
        out_shape=pltpu.VMEM((rows, width), kind),
        in_specs=[SCALARS] + [WHOLE] * len(operands),
        out_specs=WHOLE,
        compiler_params=params(10),
        cost_estimate=cost(2 * dense.size * width, dense.size * 2),
        name="forward_rows",
    )(where, *operands)


def middle_kernel(*refs, scale, came):
    parts = refs[: came + 1]
    weight_ref, up_ref, hidden_ref, grad_ref, wgrad_ref = refs[came + 1 :]
    agg = parts[0][...].astype(jnp.float32)
    for part in parts[1:]:
        agg = agg + part[...].astype(jnp.float32)
    agg = agg.astype(jnp.bfloat16)
    weight = weight_ref[...]
    pre = jnp.dot(agg, weight, preferred_element_type=jnp.float32)
    sig = jax.nn.sigmoid(pre)
    hidden_ref[...] = (pre * sig).astype(jnp.bfloat16)
    pre_grad = (up_ref[...].astype(jnp.float32) * sig * (1.0 + pre * (1.0 - sig))).astype(jnp.bfloat16)
    grad_ref[...] = lax.dot_general(
        weight, pre_grad, (((1,), (1,)), ((), ())), preferred_element_type=jnp.float32
    ).astype(jnp.bfloat16)
    wgrad_ref[...] = scale * lax.dot_general(
        agg, pre_grad, (((0,), (0,)), ((), ())), preferred_element_type=jnp.float32
    )


def middle(parts, weight, upstream, scale):
    rows, width = upstream.shape
    return pl.pallas_call(
        functools.partial(middle_kernel, scale=scale, came=len(parts) - 1),
        out_shape=(
            jax.ShapeDtypeStruct((rows, width), jnp.bfloat16),
            jax.ShapeDtypeStruct((width, rows), jnp.bfloat16),
            jax.ShapeDtypeStruct((width, width), jnp.float32),
        ),
        compiler_params=params(16),
        cost_estimate=cost(6 * rows * width * width, 10 * rows * width, rows * width),
        name="middle",
    )(*parts, weight, upstream)


def backward_kernel(where, *refs, count, groups, before):
    dense, pieces = refs[:count], refs[count : 2 * count]
    outs = refs[-len(groups) :]
    depth = outs[0].shape[2]

    for out_ref, steps in zip(outs, groups):
        for j, step in enumerate(steps):
            cols = pl.ds(pl.multiple_of((where[0] ^ step) * depth, depth), depth)
            value = refs[2 * count][step] if before else None
            for a_ref, piece in zip(dense, pieces):
                part = jnp.dot(piece[...], a_ref[:, cols], preferred_element_type=jnp.float32)
                value = part if value is None else value + part
            out_ref[j] = value.astype(out_ref.dtype)


def backward(where, dense, pieces, groups, depth, before, kind, after=()):
    count = len(pieces)
    width, _ = pieces[0].shape
    operands = [near(x) for x in [*dense, *pieces] + ([] if before is None else [before])]
    return pl.pallas_call(
        functools.partial(backward_kernel, count=count, groups=groups, before=before is not None),
        out_shape=[pltpu.VMEM((len(steps), width, depth), kind) for steps in groups],
        in_specs=[SCALARS] + [WHOLE] * len(operands) + [UNREAD] * len(after),
        out_specs=[WHOLE] * len(groups),
        compiler_params=params(10),
        cost_estimate=cost(0, 0),
        name="backward_cols",
    )(where, *operands, *after)


def meet_kernel(where, kept_ref, came_ref, own_ref, first_ref, second_ref):
    core = where[0] & 1
    own_ref[...] = kept_ref[0] + came_ref[0].astype(jnp.float32)
    first_ref[...] = (kept_ref[1 + core] + came_ref[1 + core].astype(jnp.float32)).astype(first_ref.dtype)
    second_ref[...] = kept_ref[2 - core] + came_ref[2 - core].astype(jnp.float32)


def meet(where, kept, came):
    shape = kept.shape[1:]
    kinds = [jnp.float32, came.dtype, jnp.float32]
    return pl.pallas_call(
        meet_kernel,
        out_shape=[pltpu.VMEM(shape, kind) for kind in kinds],
        in_specs=[SCALARS, WHOLE, WHOLE],
        out_specs=[WHOLE] * len(kinds),
        compiler_params=params(10),
        cost_estimate=cost(0, 0),
        name="meet",
    )(where, near(kept), near(came))


def finish_kernel(*refs):
    parts, out_ref = refs[:-1], refs[-1]
    value = parts[0][...].astype(jnp.float32)
    for part in parts[1:]:
        value = value + part[...].astype(jnp.float32)
    out_ref[...] = value.astype(out_ref.dtype).T


def finish(parts):
    width, rows = parts[0].shape
    return pl.pallas_call(
        finish_kernel,
        out_shape=jax.ShapeDtypeStruct((rows, width), jnp.bfloat16),
        compiler_params=params(12),
        cost_estimate=cost(len(parts) * rows * width, 4 * len(parts) * rows * width),
        name="finish",
    )(*parts)


def gate(values, after):
    count = len(values)
    return pl.pallas_call(
        lambda *refs: None,
        out_shape=[pltpu.VMEM(x.shape, x.dtype) for x in values],
        in_specs=[WHOLE] * count + [UNREAD] * len(after),
        out_specs=[WHOLE] * count,
        input_output_aliases={i: i for i in range(count)},
        compiler_params=params(4),
        cost_estimate=cost(0, 0),
        name="gate",
    )(*map(near, values), *after)


def total_kernel(*refs, count):
    parts, out_ref = refs[:count], refs[-1]
    rows = out_ref.shape[0]
    value = None
    for part in parts:
        for i in range(part.shape[0] // rows):
            term = part[pl.ds(i * rows, rows), :].astype(jnp.float32)
            value = term if value is None else value + term
    out_ref[...] = value.astype(out_ref.dtype)


def total(parts, rows, kind, after=()):
    return pl.pallas_call(
        functools.partial(total_kernel, count=len(parts)),
        out_shape=jax.ShapeDtypeStruct((rows, parts[0].shape[1]), kind),
        in_specs=[WHOLE] * len(parts) + [UNREAD] * len(after),
        compiler_params=params(10),
        cost_estimate=cost(0, 0),
        name="total",
    )(*parts, *after)


def half_kernel(where, values_ref, out_ref):
    rows = out_ref.shape[0]
    value = None
    for i in range(values_ref.shape[0] // (2 * rows)):
        at = pl.ds(pl.multiple_of((2 * i + (where[0] & 1)) * rows, rows), rows)
        term = values_ref[at, :].astype(jnp.float32)
        value = term if value is None else value + term
    out_ref[...] = value.astype(out_ref.dtype)


def half_total(where, values, rows):
    return pl.pallas_call(
        half_kernel,
        out_shape=jax.ShapeDtypeStruct((rows, values.shape[1]), values.dtype),
        in_specs=[SCALARS, WHOLE],
        compiler_params=params(10),
        cost_estimate=cost(0, 0),
        name="half_total",
    )(where, values)


def join_kernel(where, own_ref, *refs):
    others, out_ref = refs[:-1], refs[-1]
    rows = own_ref.shape[0]
    core = where[0] & 1
    out_ref[pl.ds(pl.multiple_of(core * rows, rows), rows), :] = own_ref[...]
    part = rows // len(others)
    for i, other_ref in enumerate(others):
        out_ref[pl.ds(pl.multiple_of((1 - core) * rows + i * part, part), part), :] = other_ref[...]


def join(where, own, *others):
    rows, width = own.shape
    return pl.pallas_call(
        join_kernel,
        out_shape=jax.ShapeDtypeStruct((2 * rows, width), own.dtype),
        in_specs=[SCALARS] + [WHOLE] * (1 + len(others)),
        compiler_params=params(10),
        cost_estimate=cost(0, 0),
        name="join",
    )(where, own, *others)


def swap(value, axis, size, step):
    return lax.ppermute(value, axis, [(i, i ^ step) for i in range(size)])


def shards(adj_tiles, tile_counts, tile_cols, features, weight, upstream):
    n_row, n_col = lax.axis_size("row"), lax.axis_size("col")
    assert n_row & (n_row - 1) == 0 and n_col & (n_col - 1) == 0 and n_row > 1
    adj, counts, cols = adj_tiles[0, 0], tile_counts[0, 0], tile_cols[0, 0]
    rows, depth = upstream.shape[0], features.shape[0]
    col_tiles = depth * n_row // adj.shape[1]
    chips = n_row // 2
    where = jnp.stack([lax.axis_index("row"), lax.axis_index("col")]).astype(jnp.int32)
    line = n_col == 4
    steps = [*range(n_col - 1, 0, -1), 0]

    *blocks, near_features = dense_rows(where, steps, counts, cols, adj, features, rows, col_tiles)
    dense = dict(zip(steps, blocks))

    far = n_col - 1
    every = list(range(n_row))
    away = gate([swap(features, "row", n_row, 2 * c) for c in range(chips - 1, 0, -1)], blocks)[::-1]
    parts = {0: near_features, 1: swap(features, "row", n_row, 1)}
    for c, shard in enumerate(away, 1):
        parts.update({2 * c: shard, 2 * c + 1: swap(shard, "row", n_row, 1)})

    half = forward(where, dense[far], parts, every[::2], [], jnp.float32)
    first = forward(where, dense[far], parts, every[1::2], [half], jnp.bfloat16)
    shares = {far: first}
    for s in steps[1:-1]:
        shares[s] = forward(where, dense[s], parts, every, [], jnp.bfloat16)
    if line:
        relayed = lax.ppermute(shares[3], "col", [(0, 1), (3, 2)])
        came = [lax.ppermute(shares[3], "col", [(1, 2), (2, 1)])]
        joined = (shares[2].astype(jnp.float32) + relayed.astype(jnp.float32)).astype(jnp.bfloat16)
        came += [swap(joined, "col", n_col, 2), swap(shares[1], "col", n_col, 1)]
    else:
        came = [swap(share, "col", n_col, s) for s, share in shares.items()]
    mine = forward(where, dense[0], parts, every, [], jnp.float32)
    scale = 1.0 / math.sqrt(rows * n_row * n_col)
    hidden, piece, part = middle([mine, *came], weight, upstream, scale)

    cores = [[i for i in range(n_row) if i % 2 == core] for core in range(2)]
    part = (part + swap(part, "row", n_row, 1)).astype(jnp.bfloat16)
    gathered = lax.all_gather(part, "row", axis_index_groups=cores, tiled=True)
    part = half_total(where, gathered, part.shape[0] // 2)
    if line:
        pieces = {s: swap(piece, "col", n_col, s) for s in (1, 2)}
        pieces[0], pieces[2], part = gate([piece, pieces[2], part], [])
        beside = lax.ppermute(pieces[0], "col", [(1, 2), (2, 1)])
        pieces[3] = beside + lax.ppermute(pieces[2], "col", [(1, 0), (2, 3)])
    else:
        pieces = {s: swap(piece, "col", n_col, s) for s in steps[:-1]}
        pieces[0] = piece

    sums, latest = None, n_col - 1
    for group in [list(range(n_col - 1))]:
        sums = backward(where, [dense[s] for s in group], [pieces[s] for s in group], [every], depth, sums, jnp.float32)[0]
    for s in range(n_col.bit_length() - 2):
        part = total([part, swap(part, "col", n_col, 1 << s)], part.shape[0], jnp.bfloat16)
    last = functools.partial(backward, where, [dense[latest]], [pieces[latest]])
    groups = [every[-2:], every[:-2]]
    sent = last([group[1::2] for group in groups], depth, sums, jnp.bfloat16, [part])
    kept = last([group[::2] for group in groups], depth, sums, jnp.float32)
    came = [swap(block, "row", n_row, 1) for block in sent]
    corner = kept[0][0] + came[0][0].astype(jnp.float32)
    after = []
    if chips == 4:
        own, first, second = meet(where, kept[1], came[1])
        there = [(i, i ^ (2 if i % 2 == 0 else 4)) for i in range(n_row)]
        across = [(i, i ^ (4 if i % 2 == 0 else 2)) for i in range(n_row)]
        corner = lax.ppermute(corner.astype(jnp.bfloat16), "row", there)
        second = (second + corner.astype(jnp.float32)).astype(jnp.bfloat16)
        after = [second]
        first = gate([first], [])[0]
        parts = [lax.ppermute(first, "row", there), lax.ppermute(second, "row", across)]
    else:
        own, *summed = [kept[1][c] + came[1][c].astype(jnp.float32) for c in range(chips - 1)]
        summed.append(corner)
        parts = [swap(summed[c - 1].astype(jnp.bfloat16), "row", n_row, 2 * c) for c in range(1, chips)]

    feature_grad = finish([own, *parts])
    part = total([part, swap(part, "col", n_col, n_col // 2)], part.shape[0], jnp.float32, after)
    top, low = part[: part.shape[0] // 2], part[part.shape[0] // 2 :]
    top_came = swap(top, "row", n_row, 1)
    low_came = swap(gate([low], [top_came])[0], "row", n_row, 1)
    weight_grad = join(where, part, top_came, low_came)
    return hidden, weight_grad, feature_grad


def solution(mesh):
    placed = (
        P("row", "col", None, None, None),
        P("row", "col", None),
        P("row", "col", None),
        P(("col", "row"), None),
        P(),
        P(("row", "col"), None),
    )
    return jax.shard_map(
        shards,
        mesh=mesh,
        in_specs=placed,
        out_specs=(P(("row", "col"), None), P(), P(("col", "row"), None)),
        check_vma=False,
    )
```

```python
import functools
import math

import jax
import jax.numpy as jnp
from jax import lax
from jax.experimental import pallas as pl
from jax.experimental.pallas import tpu as pltpu
from jax.sharding import PartitionSpec as P


MIB = 1024 * 1024
SCALARS = pl.BlockSpec(memory_space=pltpu.SMEM)
WHOLE = pl.BlockSpec(memory_space=pltpu.VMEM)
UNREAD = pl.BlockSpec(memory_space=pl.ANY)


def params(mib):
    return pltpu.CompilerParams(vmem_limit_bytes=mib * MIB)


def cost(flops, moved, exps=0):
    return pl.CostEstimate(flops=flops, bytes_accessed=moved, transcendentals=exps)


def near(value):
    return pltpu.with_memory_space_constraint(value, pltpu.VMEM)


def dense_kernel(where, counts, cols, adj_ref, features_ref, *refs, steps, window):
    outs, (copied_ref, held, total, sems) = refs[: len(steps)], refs[len(steps) :]
    slots, tile, _ = adj_ref.shape
    per = outs[0].shape[0] // tile
    width = outs[0].shape[1]

    plans = []
    for i, step in enumerate(steps):
        first = (where[1] ^ step) * per
        start = lax.fori_loop(0, first, lambda t, s: s + counts[t], jnp.int32(0))
        for u in range(per):
            count = counts[first + u]
            base = jnp.minimum(start, slots - window)
            fetch = pltpu.make_async_copy(
                adj_ref.at[pl.ds(base, window)], held.at[i * per + u], sems.at[i * per + u]
            )
            fetch.start()
            plans.append((start, start - base, count, fetch))
            start = start + count
    copied = pltpu.make_async_copy(features_ref, copied_ref, sems.at[len(plans)])
    copied.start()

    for i, out_ref in enumerate(outs):
        out_ref[...] = jnp.zeros_like(out_ref)
    for n, (start, shift, count, fetch) in enumerate(plans):
        out_ref = outs[n // per]
        rows = pl.ds((n % per) * tile, tile)
        fetch.wait()

        def place(j):
            c = cols[start + j]
            out_ref[rows, pl.ds(pl.multiple_of(c * tile, tile), tile)] = held[n, shift + j]
            return lax.shift_left(jnp.int32(1), c)

        def four(i, state):
            seen, twice = state
            for v in range(4):
                bit = place(4 * i + v)
                twice = twice | (seen & bit)
                seen = seen | bit
            return seen, twice

        def one(j, state):
            seen, twice = state
            bit = place(j)
            return seen | bit, twice | (seen & bit)

        groups = lax.div(count, 4)
        state = lax.fori_loop(0, groups, four, (jnp.int32(0), jnp.int32(0)))
        seen, twice = lax.fori_loop(4 * groups, count, one, state)
        repeated = (twice != 0) if width // tile <= 32 else (count > 0)

        @pl.when(repeated)
        def _():
            total[...] = jnp.zeros_like(total)

            def add(j, carry):
                here = pl.ds(pl.multiple_of(cols[start + j] * tile, tile), tile)
                total[:, here] += held[n, shift + j].astype(jnp.float32)
                return carry

            lax.fori_loop(0, count, add, 0)
            out_ref[rows, :] = total[...].astype(out_ref.dtype)

    copied.wait()


def dense_rows(where, steps, counts, cols, adj, features, rows, col_tiles):
    slots, tile, _ = adj.shape
    window = min(col_tiles, slots)
    width = col_tiles * tile
    tiles = rows // tile * len(steps)
    return pl.pallas_call(
        functools.partial(dense_kernel, steps=steps, window=window),
        out_shape=[pltpu.VMEM((rows, width), adj.dtype) for _ in steps]
        + [pltpu.VMEM(features.shape, features.dtype)],
        in_specs=[SCALARS] * 3 + [pl.BlockSpec(memory_space=pltpu.HBM)] * 2,
        out_specs=[WHOLE] * (len(steps) + 1),
        scratch_shapes=[
            pltpu.VMEM((tiles, window, tile, tile), adj.dtype),
            pltpu.VMEM((tile, width), jnp.float32),
            pltpu.SemaphoreType.DMA((tiles + 1,)),
        ],
        compiler_params=params(26),
        cost_estimate=cost(0, 5 * len(steps) * rows * width),
        name="dense_rows",
    )(where, *[pltpu.with_memory_space_constraint(x, pltpu.HBM) for x in (counts, cols, adj, features)])


def forward_kernel(where, a_ref, *refs, steps, before):
    shards, out_ref = refs[: len(steps)], refs[-1]
    depth = shards[0].shape[0]
    value = refs[len(steps)][...] if before else None
    for step, shard in zip(steps, shards):
        cols = pl.ds(pl.multiple_of((where[0] ^ step) * depth, depth), depth)
        part = jnp.dot(a_ref[:, cols], shard[...], preferred_element_type=jnp.float32)
        value = part if value is None else value + part
    out_ref[...] = value.astype(out_ref.dtype)


def forward(where, dense, shards, steps, before, kind):
    rows, width = dense.shape[0], shards[0].shape[1]
    operands = [near(x) for x in [dense, *[shards[s] for s in steps], *before]]
    return pl.pallas_call(
        functools.partial(forward_kernel, steps=steps, before=bool(before)),
        out_shape=pltpu.VMEM((rows, width), kind),
        in_specs=[SCALARS] + [WHOLE] * len(operands),
        out_specs=WHOLE,
        compiler_params=params(10),
        cost_estimate=cost(2 * dense.size * width, dense.size * 2),
        name="forward_rows",
    )(where, *operands)


def middle_kernel(*refs, scale, came):
    parts = refs[: came + 1]
    weight_ref, up_ref, hidden_ref, grad_ref, wgrad_ref = refs[came + 1 :]
    agg = parts[0][...].astype(jnp.float32)
    for part in parts[1:]:
        agg = agg + part[...].astype(jnp.float32)
    agg = agg.astype(jnp.bfloat16)
    weight = weight_ref[...]
    pre = jnp.dot(agg, weight, preferred_element_type=jnp.float32)
    sig = jax.nn.sigmoid(pre)
    hidden_ref[...] = (pre * sig).astype(jnp.bfloat16)
    pre_grad = (up_ref[...].astype(jnp.float32) * sig * (1.0 + pre * (1.0 - sig))).astype(jnp.bfloat16)
    grad_ref[...] = lax.dot_general(
        weight, pre_grad, (((1,), (1,)), ((), ())), preferred_element_type=jnp.float32
    ).astype(jnp.bfloat16)
    wgrad_ref[...] = scale * lax.dot_general(
        agg, pre_grad, (((0,), (0,)), ((), ())), preferred_element_type=jnp.float32
    )


def middle(parts, weight, upstream, scale):
    rows, width = upstream.shape
    return pl.pallas_call(
        functools.partial(middle_kernel, scale=scale, came=len(parts) - 1),
        out_shape=(
            jax.ShapeDtypeStruct((rows, width), jnp.bfloat16),
            jax.ShapeDtypeStruct((width, rows), jnp.bfloat16),
            jax.ShapeDtypeStruct((width, width), jnp.float32),
        ),
        compiler_params=params(16),
        cost_estimate=cost(6 * rows * width * width, 10 * rows * width, rows * width),
        name="middle",
    )(*parts, weight, upstream)


def backward_kernel(where, *refs, count, groups, before):
    dense, pieces = refs[:count], refs[count : 2 * count]
    outs = refs[-len(groups) :]
    depth = outs[0].shape[2]

    for out_ref, steps in zip(outs, groups):
        for j, step in enumerate(steps):
            cols = pl.ds(pl.multiple_of((where[0] ^ step) * depth, depth), depth)
            value = refs[2 * count][step] if before else None
            for a_ref, piece in zip(dense, pieces):
                part = jnp.dot(piece[...], a_ref[:, cols], preferred_element_type=jnp.float32)
                value = part if value is None else value + part
            out_ref[j] = value.astype(out_ref.dtype)


def backward(where, dense, pieces, groups, depth, before, kind, after=()):
    count = len(pieces)
    width, _ = pieces[0].shape
    operands = [near(x) for x in [*dense, *pieces] + ([] if before is None else [before])]
    return pl.pallas_call(
        functools.partial(backward_kernel, count=count, groups=groups, before=before is not None),
        out_shape=[pltpu.VMEM((len(steps), width, depth), kind) for steps in groups],
        in_specs=[SCALARS] + [WHOLE] * len(operands) + [UNREAD] * len(after),
        out_specs=[WHOLE] * len(groups),
        compiler_params=params(10),
        cost_estimate=cost(0, 0),
        name="backward_cols",
    )(where, *operands, *after)


def meet_kernel(where, kept_ref, came_ref, own_ref, first_ref, second_ref):
    core = where[0] & 1
    own_ref[...] = kept_ref[0] + came_ref[0].astype(jnp.float32)
    first_ref[...] = (kept_ref[1 + core] + came_ref[1 + core].astype(jnp.float32)).astype(first_ref.dtype)
    second_ref[...] = kept_ref[2 - core] + came_ref[2 - core].astype(jnp.float32)


def meet(where, kept, came):
    shape = kept.shape[1:]
    kinds = [jnp.float32, came.dtype, jnp.float32]
    return pl.pallas_call(
        meet_kernel,
        out_shape=[pltpu.VMEM(shape, kind) for kind in kinds],
        in_specs=[SCALARS, WHOLE, WHOLE],
        out_specs=[WHOLE] * len(kinds),
        compiler_params=params(10),
        cost_estimate=cost(0, 0),
        name="meet",
    )(where, near(kept), near(came))


def finish_kernel(*refs):
    parts, out_ref = refs[:-1], refs[-1]
    value = parts[0][...].astype(jnp.float32)
    for part in parts[1:]:
        value = value + part[...].astype(jnp.float32)
    out_ref[...] = value.astype(out_ref.dtype).T


def finish(parts):
    width, rows = parts[0].shape
    return pl.pallas_call(
        finish_kernel,
        out_shape=jax.ShapeDtypeStruct((rows, width), jnp.bfloat16),
        compiler_params=params(12),
        cost_estimate=cost(len(parts) * rows * width, 4 * len(parts) * rows * width),
        name="finish",
    )(*parts)


def gate(values, after):
    count = len(values)
    return pl.pallas_call(
        lambda *refs: None,
        out_shape=[pltpu.VMEM(x.shape, x.dtype) for x in values],
        in_specs=[WHOLE] * count + [UNREAD] * len(after),
        out_specs=[WHOLE] * count,
        input_output_aliases={i: i for i in range(count)},
        compiler_params=params(4),
        cost_estimate=cost(0, 0),
        name="gate",
    )(*map(near, values), *after)


def total_kernel(*refs, count):
    parts, out_ref = refs[:count], refs[-1]
    rows = out_ref.shape[0]
    value = None
    for part in parts:
        for i in range(part.shape[0] // rows):
            term = part[pl.ds(i * rows, rows), :].astype(jnp.float32)
            value = term if value is None else value + term
    out_ref[...] = value.astype(out_ref.dtype)


def total(parts, rows, kind, after=()):
    return pl.pallas_call(
        functools.partial(total_kernel, count=len(parts)),
        out_shape=jax.ShapeDtypeStruct((rows, parts[0].shape[1]), kind),
        in_specs=[WHOLE] * len(parts) + [UNREAD] * len(after),
        compiler_params=params(10),
        cost_estimate=cost(0, 0),
        name="total",
    )(*parts, *after)


def half_kernel(where, values_ref, out_ref):
    rows = out_ref.shape[0]
    value = None
    for i in range(values_ref.shape[0] // (2 * rows)):
        at = pl.ds(pl.multiple_of((2 * i + (where[0] & 1)) * rows, rows), rows)
        term = values_ref[at, :].astype(jnp.float32)
        value = term if value is None else value + term
    out_ref[...] = value.astype(out_ref.dtype)


def half_total(where, values, rows):
    return pl.pallas_call(
        half_kernel,
        out_shape=jax.ShapeDtypeStruct((rows, values.shape[1]), values.dtype),
        in_specs=[SCALARS, WHOLE],
        compiler_params=params(10),
        cost_estimate=cost(0, 0),
        name="half_total",
    )(where, values)


def join_kernel(where, own_ref, *refs):
    others, out_ref = refs[:-1], refs[-1]
    rows = own_ref.shape[0]
    core = where[0] & 1
    out_ref[pl.ds(pl.multiple_of(core * rows, rows), rows), :] = own_ref[...]
    part = rows // len(others)
    for i, other_ref in enumerate(others):
        out_ref[pl.ds(pl.multiple_of((1 - core) * rows + i * part, part), part), :] = other_ref[...]


def join(where, own, *others):
    rows, width = own.shape
    return pl.pallas_call(
        join_kernel,
        out_shape=jax.ShapeDtypeStruct((2 * rows, width), own.dtype),
        in_specs=[SCALARS] + [WHOLE] * (1 + len(others)),
        compiler_params=params(10),
        cost_estimate=cost(0, 0),
        name="join",
    )(where, own, *others)


def swap(value, axis, size, step):
    return lax.ppermute(value, axis, [(i, i ^ step) for i in range(size)])


def shards(adj_tiles, tile_counts, tile_cols, features, weight, upstream):
    n_row, n_col = lax.axis_size("row"), lax.axis_size("col")
    assert n_row & (n_row - 1) == 0 and n_col & (n_col - 1) == 0 and n_row > 1
    adj, counts, cols = adj_tiles[0, 0], tile_counts[0, 0], tile_cols[0, 0]
    rows, depth = upstream.shape[0], features.shape[0]
    col_tiles = depth * n_row // adj.shape[1]
    chips = n_row // 2
    where = jnp.stack([lax.axis_index("row"), lax.axis_index("col")]).astype(jnp.int32)
    line = n_col == 4
    steps = [*range(n_col - 1, 0, -1), 0]

    *blocks, near_features = dense_rows(where, steps, counts, cols, adj, features, rows, col_tiles)
    dense = dict(zip(steps, blocks))

    far = n_col - 1
    every = list(range(n_row))
    away = gate([swap(features, "row", n_row, 2 * c) for c in range(chips - 1, 0, -1)], blocks)[::-1]
    parts = {0: near_features, 1: swap(features, "row", n_row, 1)}
    for c, shard in enumerate(away, 1):
        parts.update({2 * c: shard, 2 * c + 1: swap(shard, "row", n_row, 1)})

    half = forward(where, dense[far], parts, every[::2], [], jnp.float32)
    first = forward(where, dense[far], parts, every[1::2], [half], jnp.bfloat16)
    shares = {far: first}
    for s in steps[1:-1]:
        shares[s] = forward(where, dense[s], parts, every, [], jnp.bfloat16)
    if line:
        relayed = lax.ppermute(shares[3], "col", [(0, 1), (3, 2)])
        came = [lax.ppermute(shares[3], "col", [(1, 2), (2, 1)])]
        joined = (shares[2].astype(jnp.float32) + relayed.astype(jnp.float32)).astype(jnp.bfloat16)
        came += [lax.ppermute(shares[2], "col", [(0, 2), (3, 1)]), lax.ppermute(joined, "col", [(1, 3), (2, 0)])]
        came.append(swap(shares[1], "col", n_col, 1))
    else:
        came = [swap(share, "col", n_col, s) for s, share in shares.items()]
    mine = forward(where, dense[0], parts, every, [], jnp.float32)
    scale = 1.0 / math.sqrt(rows * n_row * n_col)
    hidden, piece, part = middle([mine, *came], weight, upstream, scale)

    cores = [[i for i in range(n_row) if i % 2 == core] for core in range(2)]
    part = (part + swap(part, "row", n_row, 1)).astype(jnp.bfloat16)
    gathered = lax.all_gather(part, "row", axis_index_groups=cores, tiled=True)
    part = half_total(where, gathered, part.shape[0] // 2)
    if line:
        pieces = {s: swap(piece, "col", n_col, s) for s in (1, 2)}
        pieces[0], pieces[2], part = gate([piece, pieces[2], part], [])
        beside = lax.ppermute(pieces[0], "col", [(1, 2), (2, 1)])
        pieces[3] = beside + lax.ppermute(pieces[2], "col", [(1, 0), (2, 3)])
    else:
        pieces = {s: swap(piece, "col", n_col, s) for s in steps[:-1]}
        pieces[0] = piece

    sums, latest = None, n_col - 1
    for group in [list(range(n_col - 1))]:
        sums = backward(where, [dense[s] for s in group], [pieces[s] for s in group], [every], depth, sums, jnp.float32)[0]
    for s in range(n_col.bit_length() - 2):
        part = total([part, swap(part, "col", n_col, 1 << s)], part.shape[0], jnp.bfloat16)
    last = functools.partial(backward, where, [dense[latest]], [pieces[latest]])
    groups = [every[-2:], every[:-2]]
    sent = last([group[1::2] for group in groups], depth, sums, jnp.bfloat16, [part])
    kept = last([group[::2] for group in groups], depth, sums, jnp.float32)
    came = [swap(block, "row", n_row, 1) for block in sent]
    corner = kept[0][0] + came[0][0].astype(jnp.float32)
    after = []
    if chips == 4:
        own, first, second = meet(where, kept[1], came[1])
        there = [(i, i ^ (2 if i % 2 == 0 else 4)) for i in range(n_row)]
        across = [(i, i ^ (4 if i % 2 == 0 else 2)) for i in range(n_row)]
        corner = lax.ppermute(corner.astype(jnp.bfloat16), "row", there)
        second = (second + corner.astype(jnp.float32)).astype(jnp.bfloat16)
        after = [second]
        first = gate([first], [])[0]
        parts = [lax.ppermute(first, "row", there), lax.ppermute(second, "row", across)]
    else:
        own, *summed = [kept[1][c] + came[1][c].astype(jnp.float32) for c in range(chips - 1)]
        summed.append(corner)
        parts = [swap(summed[c - 1].astype(jnp.bfloat16), "row", n_row, 2 * c) for c in range(1, chips)]

    feature_grad = finish([own, *parts])
    part = total([part, swap(part, "col", n_col, n_col // 2)], part.shape[0], jnp.float32, after)
    top, low = part[: part.shape[0] // 2], part[part.shape[0] // 2 :]
    top_came = swap(top, "row", n_row, 1)
    low_came = swap(gate([low], [top_came])[0], "row", n_row, 1)
    weight_grad = join(where, part, top_came, low_came)
    return hidden, weight_grad, feature_grad


def solution(mesh):
    placed = (
        P("row", "col", None, None, None),
        P("row", "col", None),
        P("row", "col", None),
        P(("col", "row"), None),
        P(),
        P(("row", "col"), None),
    )
    return jax.shard_map(
        shards,
        mesh=mesh,
        in_specs=placed,
        out_specs=(P(("row", "col"), None), P(), P(("col", "row"), None)),
        check_vma=False,
    )
```

```python
import functools
import math

import jax
import jax.numpy as jnp
from jax import lax
from jax.experimental import pallas as pl
from jax.experimental.pallas import tpu as pltpu
from jax.sharding import PartitionSpec as P


MIB = 1024 * 1024
SCALARS = pl.BlockSpec(memory_space=pltpu.SMEM)
WHOLE = pl.BlockSpec(memory_space=pltpu.VMEM)
UNREAD = pl.BlockSpec(memory_space=pl.ANY)


def params(mib):
    return pltpu.CompilerParams(vmem_limit_bytes=mib * MIB)


def cost(flops, moved, exps=0):
    return pl.CostEstimate(flops=flops, bytes_accessed=moved, transcendentals=exps)


def near(value):
    return pltpu.with_memory_space_constraint(value, pltpu.VMEM)


def dense_kernel(where, counts, cols, adj_ref, features_ref, *refs, steps, window):
    outs, (copied_ref, held, total, sems) = refs[: len(steps)], refs[len(steps) :]
    slots, tile, _ = adj_ref.shape
    per = outs[0].shape[0] // tile
    width = outs[0].shape[1]

    plans = []
    for i, step in enumerate(steps):
        first = (where[1] ^ step) * per
        start = lax.fori_loop(0, first, lambda t, s: s + counts[t], jnp.int32(0))
        for u in range(per):
            count = counts[first + u]
            base = jnp.minimum(start, slots - window)
            fetch = pltpu.make_async_copy(
                adj_ref.at[pl.ds(base, window)], held.at[i * per + u], sems.at[i * per + u]
            )
            fetch.start()
            plans.append((start, start - base, count, fetch))
            start = start + count
    copied = pltpu.make_async_copy(features_ref, copied_ref, sems.at[len(plans)])
    copied.start()

    for i, out_ref in enumerate(outs):
        out_ref[...] = jnp.zeros_like(out_ref)
    for n, (start, shift, count, fetch) in enumerate(plans):
        out_ref = outs[n // per]
        rows = pl.ds((n % per) * tile, tile)
        fetch.wait()

        def place(j):
            c = cols[start + j]
            out_ref[rows, pl.ds(pl.multiple_of(c * tile, tile), tile)] = held[n, shift + j]
            return lax.shift_left(jnp.int32(1), c)

        def four(i, state):
            seen, twice = state
            for v in range(4):
                bit = place(4 * i + v)
                twice = twice | (seen & bit)
                seen = seen | bit
            return seen, twice

        def one(j, state):
            seen, twice = state
            bit = place(j)
            return seen | bit, twice | (seen & bit)

        groups = lax.div(count, 4)
        state = lax.fori_loop(0, groups, four, (jnp.int32(0), jnp.int32(0)))
        seen, twice = lax.fori_loop(4 * groups, count, one, state)
        repeated = (twice != 0) if width // tile <= 32 else (count > 0)

        @pl.when(repeated)
        def _():
            total[...] = jnp.zeros_like(total)

            def add(j, carry):
                here = pl.ds(pl.multiple_of(cols[start + j] * tile, tile), tile)
                total[:, here] += held[n, shift + j].astype(jnp.float32)
                return carry

            lax.fori_loop(0, count, add, 0)
            out_ref[rows, :] = total[...].astype(out_ref.dtype)

    copied.wait()


def dense_rows(where, steps, counts, cols, adj, features, rows, col_tiles):
    slots, tile, _ = adj.shape
    window = min(col_tiles, slots)
    width = col_tiles * tile
    tiles = rows // tile * len(steps)
    return pl.pallas_call(
        functools.partial(dense_kernel, steps=steps, window=window),
        out_shape=[pltpu.VMEM((rows, width), adj.dtype) for _ in steps]
        + [pltpu.VMEM(features.shape, features.dtype)],
        in_specs=[SCALARS] * 3 + [pl.BlockSpec(memory_space=pltpu.HBM)] * 2,
        out_specs=[WHOLE] * (len(steps) + 1),
        scratch_shapes=[
            pltpu.VMEM((tiles, window, tile, tile), adj.dtype),
            pltpu.VMEM((tile, width), jnp.float32),
            pltpu.SemaphoreType.DMA((tiles + 1,)),
        ],
        compiler_params=params(26),
        cost_estimate=cost(0, 5 * len(steps) * rows * width),
        name="dense_rows",
    )(where, *[pltpu.with_memory_space_constraint(x, pltpu.HBM) for x in (counts, cols, adj, features)])


def forward_kernel(where, a_ref, *refs, steps, before):
    shards, out_ref = refs[: len(steps)], refs[-1]
    depth = shards[0].shape[0]
    value = refs[len(steps)][...] if before else None
    for step, shard in zip(steps, shards):
        cols = pl.ds(pl.multiple_of((where[0] ^ step) * depth, depth), depth)
        part = jnp.dot(a_ref[:, cols], shard[...], preferred_element_type=jnp.float32)
        value = part if value is None else value + part
    out_ref[...] = value.astype(out_ref.dtype)


def forward(where, dense, shards, steps, before, kind):
    rows, width = dense.shape[0], shards[0].shape[1]
    operands = [near(x) for x in [dense, *[shards[s] for s in steps], *before]]
    return pl.pallas_call(
        functools.partial(forward_kernel, steps=steps, before=bool(before)),
        out_shape=pltpu.VMEM((rows, width), kind),
        in_specs=[SCALARS] + [WHOLE] * len(operands),
        out_specs=WHOLE,
        compiler_params=params(10),
        cost_estimate=cost(2 * dense.size * width, dense.size * 2),
        name="forward_rows",
    )(where, *operands)


def middle_kernel(*refs, scale, came):
    parts = refs[: came + 1]
    weight_ref, up_ref, hidden_ref, grad_ref, wgrad_ref = refs[came + 1 :]
    agg = parts[0][...].astype(jnp.float32)
    for part in parts[1:]:
        agg = agg + part[...].astype(jnp.float32)
    agg = agg.astype(jnp.bfloat16)
    weight = weight_ref[...]
    pre = jnp.dot(agg, weight, preferred_element_type=jnp.float32)
    sig = jax.nn.sigmoid(pre)
    hidden_ref[...] = (pre * sig).astype(jnp.bfloat16)
    pre_grad = (up_ref[...].astype(jnp.float32) * sig * (1.0 + pre * (1.0 - sig))).astype(jnp.bfloat16)
    grad_ref[...] = lax.dot_general(
        weight, pre_grad, (((1,), (1,)), ((), ())), preferred_element_type=jnp.float32
    ).astype(jnp.bfloat16)
    wgrad_ref[...] = scale * lax.dot_general(
        agg, pre_grad, (((0,), (0,)), ((), ())), preferred_element_type=jnp.float32
    )


def middle(parts, weight, upstream, scale):
    rows, width = upstream.shape
    return pl.pallas_call(
        functools.partial(middle_kernel, scale=scale, came=len(parts) - 1),
        out_shape=(
            pltpu.VMEM((rows, width), jnp.bfloat16),
            pltpu.VMEM((width, rows), jnp.bfloat16),
            pltpu.VMEM((width, width), jnp.float32),
        ),
        compiler_params=params(16),
        cost_estimate=cost(6 * rows * width * width, 10 * rows * width, rows * width),
        name="middle",
    )(*parts, weight, upstream)


def backward_kernel(where, *refs, count, groups, before):
    dense, pieces = refs[:count], refs[count : 2 * count]
    outs = refs[-len(groups) :]
    depth = outs[0].shape[2]

    for out_ref, steps in zip(outs, groups):
        for j, step in enumerate(steps):
            cols = pl.ds(pl.multiple_of((where[0] ^ step) * depth, depth), depth)
            value = refs[2 * count][step] if before else None
            for a_ref, piece in zip(dense, pieces):
                part = jnp.dot(piece[...], a_ref[:, cols], preferred_element_type=jnp.float32)
                value = part if value is None else value + part
            out_ref[j] = value.astype(out_ref.dtype)


def backward(where, dense, pieces, groups, depth, before, kind, after=()):
    count = len(pieces)
    width, _ = pieces[0].shape
    operands = [near(x) for x in [*dense, *pieces] + ([] if before is None else [before])]
    return pl.pallas_call(
        functools.partial(backward_kernel, count=count, groups=groups, before=before is not None),
        out_shape=[pltpu.VMEM((len(steps), width, depth), kind) for steps in groups],
        in_specs=[SCALARS] + [WHOLE] * len(operands) + [UNREAD] * len(after),
        out_specs=[WHOLE] * len(groups),
        compiler_params=params(10),
        cost_estimate=cost(0, 0),
        name="backward_cols",
    )(where, *operands, *after)


def meet_kernel(where, kept_ref, came_ref, own_ref, first_ref, second_ref):
    core = where[0] & 1
    own_ref[...] = kept_ref[0] + came_ref[0].astype(jnp.float32)
    first_ref[...] = (kept_ref[1 + core] + came_ref[1 + core].astype(jnp.float32)).astype(first_ref.dtype)
    second_ref[...] = kept_ref[2 - core] + came_ref[2 - core].astype(jnp.float32)


def meet(where, kept, came):
    shape = kept.shape[1:]
    kinds = [jnp.float32, came.dtype, jnp.float32]
    return pl.pallas_call(
        meet_kernel,
        out_shape=[pltpu.VMEM(shape, kind) for kind in kinds],
        in_specs=[SCALARS, WHOLE, WHOLE],
        out_specs=[WHOLE] * len(kinds),
        compiler_params=params(10),
        cost_estimate=cost(0, 0),
        name="meet",
    )(where, near(kept), near(came))


def finish_kernel(*refs):
    parts, out_ref = refs[:-1], refs[-1]
    value = parts[0][...].astype(jnp.float32)
    for part in parts[1:]:
        value = value + part[...].astype(jnp.float32)
    out_ref[...] = value.astype(out_ref.dtype).T


def finish(parts):
    width, rows = parts[0].shape
    return pl.pallas_call(
        finish_kernel,
        out_shape=jax.ShapeDtypeStruct((rows, width), jnp.bfloat16),
        compiler_params=params(12),
        cost_estimate=cost(len(parts) * rows * width, 4 * len(parts) * rows * width),
        name="finish",
    )(*parts)


def gate(values, after):
    count = len(values)
    return pl.pallas_call(
        lambda *refs: None,
        out_shape=[pltpu.VMEM(x.shape, x.dtype) for x in values],
        in_specs=[WHOLE] * count + [UNREAD] * len(after),
        out_specs=[WHOLE] * count,
        input_output_aliases={i: i for i in range(count)},
        compiler_params=params(4),
        cost_estimate=cost(0, 0),
        name="gate",
    )(*map(near, values), *after)


def total_kernel(*refs, count):
    parts, out_ref = refs[:count], refs[-1]
    rows = out_ref.shape[0]
    value = None
    for part in parts:
        for i in range(part.shape[0] // rows):
            term = part[pl.ds(i * rows, rows), :].astype(jnp.float32)
            value = term if value is None else value + term
    out_ref[...] = value.astype(out_ref.dtype)


def total(parts, rows, kind, after=()):
    return pl.pallas_call(
        functools.partial(total_kernel, count=len(parts)),
        out_shape=jax.ShapeDtypeStruct((rows, parts[0].shape[1]), kind),
        in_specs=[WHOLE] * len(parts) + [UNREAD] * len(after),
        compiler_params=params(10),
        cost_estimate=cost(0, 0),
        name="total",
    )(*parts, *after)


def half_kernel(where, values_ref, out_ref):
    rows = out_ref.shape[0]
    value = None
    for i in range(values_ref.shape[0] // (2 * rows)):
        at = pl.ds(pl.multiple_of((2 * i + (where[0] & 1)) * rows, rows), rows)
        term = values_ref[at, :].astype(jnp.float32)
        value = term if value is None else value + term
    out_ref[...] = value.astype(out_ref.dtype)


def half_total(where, values, rows):
    return pl.pallas_call(
        half_kernel,
        out_shape=jax.ShapeDtypeStruct((rows, values.shape[1]), values.dtype),
        in_specs=[SCALARS, WHOLE],
        compiler_params=params(10),
        cost_estimate=cost(0, 0),
        name="half_total",
    )(where, values)


def join_kernel(where, own_ref, *refs):
    others, out_ref = refs[:-1], refs[-1]
    rows = own_ref.shape[0]
    core = where[0] & 1
    out_ref[pl.ds(pl.multiple_of(core * rows, rows), rows), :] = own_ref[...]
    part = rows // len(others)
    for i, other_ref in enumerate(others):
        out_ref[pl.ds(pl.multiple_of((1 - core) * rows + i * part, part), part), :] = other_ref[...]


def join(where, own, *others):
    rows, width = own.shape
    return pl.pallas_call(
        join_kernel,
        out_shape=jax.ShapeDtypeStruct((2 * rows, width), own.dtype),
        in_specs=[SCALARS] + [WHOLE] * (1 + len(others)),
        compiler_params=params(10),
        cost_estimate=cost(0, 0),
        name="join",
    )(where, own, *others)


def swap(value, axis, size, step):
    return lax.ppermute(value, axis, [(i, i ^ step) for i in range(size)])


def shards(adj_tiles, tile_counts, tile_cols, features, weight, upstream):
    n_row, n_col = lax.axis_size("row"), lax.axis_size("col")
    assert n_row & (n_row - 1) == 0 and n_col & (n_col - 1) == 0 and n_row > 1
    adj, counts, cols = adj_tiles[0, 0], tile_counts[0, 0], tile_cols[0, 0]
    rows, depth = upstream.shape[0], features.shape[0]
    col_tiles = depth * n_row // adj.shape[1]
    chips = n_row // 2
    where = jnp.stack([lax.axis_index("row"), lax.axis_index("col")]).astype(jnp.int32)
    line = n_col == 4
    steps = [*range(n_col - 1, 0, -1), 0]

    *blocks, near_features = dense_rows(where, steps, counts, cols, adj, features, rows, col_tiles)
    dense = dict(zip(steps, blocks))

    far = n_col - 1
    every = list(range(n_row))
    away = gate([swap(features, "row", n_row, 2 * c) for c in range(chips - 1, 0, -1)], blocks)[::-1]
    parts = {0: near_features, 1: swap(features, "row", n_row, 1)}
    for c, shard in enumerate(away, 1):
        parts.update({2 * c: shard, 2 * c + 1: swap(shard, "row", n_row, 1)})

    half = forward(where, dense[far], parts, every[::2], [], jnp.float32)
    first = forward(where, dense[far], parts, every[1::2], [half], jnp.bfloat16)
    shares = {far: first}
    for s in steps[1:-1]:
        shares[s] = forward(where, dense[s], parts, every, [], jnp.bfloat16)
    if line:
        relayed = lax.ppermute(shares[3], "col", [(0, 1), (3, 2)])
        came = [lax.ppermute(shares[3], "col", [(1, 2), (2, 1)])]
        joined = (shares[2].astype(jnp.float32) + relayed.astype(jnp.float32)).astype(jnp.bfloat16)
        came += [swap(joined, "col", n_col, 2), swap(shares[1], "col", n_col, 1)]
    else:
        came = [swap(share, "col", n_col, s) for s, share in shares.items()]
    mine = forward(where, dense[0], parts, every, [], jnp.float32)
    scale = 1.0 / math.sqrt(rows * n_row * n_col)
    hidden, piece, part = middle([mine, *came], weight, upstream, scale)

    cores = [[i for i in range(n_row) if i % 2 == core] for core in range(2)]
    part = (part + swap(part, "row", n_row, 1)).astype(jnp.bfloat16)
    gathered = lax.all_gather(part, "row", axis_index_groups=cores, tiled=True)
    part = half_total(where, gathered, part.shape[0] // 2)
    if line:
        pieces = {s: swap(piece, "col", n_col, s) for s in (1, 2)}
        pieces[0], pieces[2], part = gate([piece, pieces[2], part], [])
        beside = lax.ppermute(pieces[0], "col", [(1, 2), (2, 1)])
        pieces[3] = beside + lax.ppermute(pieces[2], "col", [(1, 0), (2, 3)])
    else:
        pieces = {s: swap(piece, "col", n_col, s) for s in steps[:-1]}
        pieces[0] = piece

    sums, latest = None, n_col - 1
    for group in [list(range(n_col - 1))]:
        sums = backward(where, [dense[s] for s in group], [pieces[s] for s in group], [every], depth, sums, jnp.float32)[0]
    for s in range(n_col.bit_length() - 2):
        part = total([part, swap(part, "col", n_col, 1 << s)], part.shape[0], jnp.bfloat16)
    last = functools.partial(backward, where, [dense[latest]], [pieces[latest]])
    groups = [every[-2:], every[:-2]]
    sent = last([group[1::2] for group in groups], depth, sums, jnp.bfloat16, [part])
    kept = last([group[::2] for group in groups], depth, sums, jnp.float32)
    came = [swap(block, "row", n_row, 1) for block in sent]
    corner = kept[0][0] + came[0][0].astype(jnp.float32)
    after = []
    if chips == 4:
        own, first, second = meet(where, kept[1], came[1])
        there = [(i, i ^ (2 if i % 2 == 0 else 4)) for i in range(n_row)]
        across = [(i, i ^ (4 if i % 2 == 0 else 2)) for i in range(n_row)]
        corner = lax.ppermute(corner.astype(jnp.bfloat16), "row", there)
        second = (second + corner.astype(jnp.float32)).astype(jnp.bfloat16)
        after = [second]
        first = gate([first], [])[0]
        parts = [lax.ppermute(first, "row", there), lax.ppermute(second, "row", across)]
    else:
        own, *summed = [kept[1][c] + came[1][c].astype(jnp.float32) for c in range(chips - 1)]
        summed.append(corner)
        parts = [swap(summed[c - 1].astype(jnp.bfloat16), "row", n_row, 2 * c) for c in range(1, chips)]

    feature_grad = finish([own, *parts])
    part = total([part, swap(part, "col", n_col, n_col // 2)], part.shape[0], jnp.float32, after)
    top, low = part[: part.shape[0] // 2], part[part.shape[0] // 2 :]
    top_came = swap(top, "row", n_row, 1)
    low_came = swap(gate([low], [top_came])[0], "row", n_row, 1)
    weight_grad = join(where, part, top_came, low_came)
    return hidden, weight_grad, feature_grad


def solution(mesh):
    placed = (
        P("row", "col", None, None, None),
        P("row", "col", None),
        P("row", "col", None),
        P(("col", "row"), None),
        P(),
        P(("row", "col"), None),
    )
    return jax.shard_map(
        shards,
        mesh=mesh,
        in_specs=placed,
        out_specs=(P(("row", "col"), None), P(), P(("col", "row"), None)),
        check_vma=False,
    )
```
